32 devices in a mesh: section: 2 (over core), fsdp: 4 (over y, x), replica: 4 (over z).
Axes of the slice: x: 2, y: 2, z: 4, core: 2. Of those that a mesh axis runs over, the one named last changes fastest.
Arguments:
- ends_in: bfloat16 [2, 320, 197, 384], P('section', ('fsdp', 'replica')), may hold values from -6 to 6
- live: int32 [2, 16], P(None, ('fsdp', 'replica')), may hold values from 9 to 10, as said below
- gain_attn: bfloat16 [2, 384], P('section', 'fsdp'), may hold values from 0.25 to 1.75
- w_qkv: bfloat16 [2, 384, 1152], P('section', 'fsdp'), may hold values from -0.4375 to 0.4375
- w_out: bfloat16 [2, 384, 384], P('section', 'fsdp'), may hold values from -0.875 to 0.875
- gain_mlp: bfloat16 [2, 384], P('section', 'fsdp'), may hold values from 0.25 to 1.75
- w_up: bfloat16 [2, 384, 1536], P('section', 'fsdp'), may hold values from -0.3125 to 0.3125
- w_down: bfloat16 [2, 1536, 384], P('section', 'fsdp'), may hold values from -0.21875 to 0.21875
Outputs:
- ends_out: bfloat16 [2, 320, 197, 384], P('section', ('fsdp', 'replica'))
- grad_gain_attn: float32 [2, 384], P('section', 'fsdp')
- grad_w_qkv: float32 [2, 384, 1152], P('section', 'fsdp')
- grad_w_out: float32 [2, 384, 384], P('section', 'fsdp')
- grad_gain_mlp: float32 [2, 384], P('section', 'fsdp')
- grad_w_up: float32 [2, 384, 1536], P('section', 'fsdp')
- grad_w_down: float32 [2, 1536, 384], P('section', 'fsdp')
The draws below stay inside these ranges and needn't reach their ends.
Inputs may be any that keep to these rules, and one draw needn't show every extreme that they name: live[m, d] is the number of live images among the 10 slots of device d in micro-batch m; they are its first slots, the rest are padding.
All inputs are finite; a program needn't handle non-finite values.
Results may differ from the reference program's by a relative error of at most 0.03.
The reference program's roundings to bfloat16 on the way count: a program that leaves them out, or rounds other values in their place, can miss the bound.
Values may be sent and summed in bfloat16 or wider, within the bound.
No kernel may reach another device: no remote copies, remote signals or barrier semaphores. Data moves between devices by JAX's collectives and lax.ppermute only.
A program may use at most 512 MiB of HBM per device.

```python
import jax
import jax.numpy as jnp
from jax import lax

D = 384
HEADS = 6
HEAD_DIM = 64
FF = 1536
SEQ = 197
MICRO = 2
IMG_DEV = 10
DATA_DEVS = 16
IMAGES = 320


def draw_live(key, part):
    key = jax.random.fold_in(key, 11)
    counts = jax.random.randint(key, (MICRO, DATA_DEVS), IMG_DEV - 1, IMG_DEV + 1, dtype=jnp.int32)
    counts = counts.at[0, 0].set(IMG_DEV - 1)
    counts = counts.at[MICRO - 1, DATA_DEVS - 1].set(IMG_DEV)
    return counts.astype(jnp.int32)


def block_levels(stream_key, extent, pieces, smallest, largest):
    def one(position, parts):
        steps = jax.random.uniform(jax.random.fold_in(jax.random.fold_in(stream_key, 6), position), (parts,), jnp.float32, smallest / len(pieces), largest / len(pieces))
        return jnp.repeat(jnp.exp(steps), extent[position] // parts).reshape((-1,) + (1,) * (len(extent) - position - 1))

    gain = one(*pieces[0])
    for cut in pieces[1:]:
        gain = gain * one(*cut)
    return gain


def centred(own_key, dims, scale, reach, pieces=(), kind=jnp.bfloat16):
    drawn = scale * jax.random.normal(own_key, dims, jnp.float32)
    if pieces:
        drawn = drawn * block_levels(own_key, dims, pieces, -0.22, 0.18)
    return jnp.clip(drawn, -reach, reach).astype(kind)


def setup_inputs(seed: int = 0) -> dict:
    streams_of = jax.random.split(jax.random.key(seed), 9)
    ends_in = centred(streams_of[0], (2, IMAGES, SEQ, D), 1.0, 6.0, ((0, 2), (1, 16)))
    live = draw_live(jax.random.fold_in(streams_of[8], 71), 0)
    gain_attn = jnp.clip(1.0 + 0.15 * jax.random.normal(streams_of[2], (2, D), jnp.float32), 0.25, 1.75).astype(jnp.bfloat16)
    w_qkv = centred(streams_of[3], (2, D, 3 * D), (D // 2) ** -0.5, 0.4375, ((0, 2), (1, 4)))
    w_out = centred(streams_of[4], (2, D, D), (D // 8) ** -0.5, 0.875, ((0, 2), (1, 4)))
    gain_mlp = jnp.clip(1.0 + 0.15 * jax.random.normal(streams_of[5], (2, D), jnp.float32), 0.25, 1.75).astype(jnp.bfloat16)
    w_up = centred(streams_of[6], (2, D, FF), D ** -0.5, 0.3125, ((0, 2), (1, 4)))
    w_down = centred(streams_of[7], (2, FF, D), (FF // 2) ** -0.5, 0.21875, ((0, 2), (1, 4)))
    return dict(ends_in=ends_in, live=live, gain_attn=gain_attn, w_qkv=w_qkv, w_out=w_out, gain_mlp=gain_mlp, w_up=w_up, w_down=w_down)


EPS = 1e-06
HIGH = lax.Precision.HIGHEST

@jax.custom_vjp
def low(v):
    return lax.optimization_barrier(v.astype(jnp.bfloat16)).astype(jnp.float32)

@jax.custom_vjp
def low_back(v):
    return v

def low_keep(v):
    return (low(v), None)

def low_pass(kept, grad):
    return (grad,)

def back_keep(v):
    return (v, None)

def back_low(kept, grad):
    return (low(grad),)
low.defvjp(low_keep, low_pass)
low_back.defvjp(back_keep, back_low)

def normalize(values, gain_vec):
    row_mean = lax.optimization_barrier(jnp.mean(values, axis=-1, keepdims=True))
    centered = values - row_mean
    variance = lax.optimization_barrier(jnp.mean(centered * centered, axis=-1, keepdims=True))
    return centered * lax.rsqrt(variance + EPS) * gain_vec

def apply_matrix(left_side, right_side):
    return jnp.einsum('bsk,kn->bsn', left_side, right_side, precision=HIGH)

def encoder(inputs, params):
    gain_one, qkv_matrix, out_matrix, gain_two, up_matrix, down_matrix = params
    image_count = inputs.shape[0]
    entry_one = low(normalize(inputs, gain_one))
    joint_qkv = low(low_back(apply_matrix(entry_one, qkv_matrix)))
    joint_qkv = joint_qkv.reshape(image_count, SEQ, 3, HEADS, HEAD_DIM)
    queries = joint_qkv[:, :, 0]
    key_rows = joint_qkv[:, :, 1]
    values = joint_qkv[:, :, 2]
    scores = low_back(jnp.einsum('bqhd,bkhd->bhqk', queries, key_rows, precision=HIGH) * HEAD_DIM ** (-0.5))
    attn_probs = low(jax.nn.softmax(scores, axis=-1))
    mixed_heads = jnp.einsum('bhqk,bkhd->bqhd', attn_probs, values, precision=HIGH)
    mixed_heads = low(low_back(mixed_heads.reshape(image_count, SEQ, D)))
    middle = inputs + low_back(apply_matrix(mixed_heads, out_matrix))
    entry_two = low(normalize(middle, gain_two))
    hidden = low_back(apply_matrix(entry_two, up_matrix))
    active = low(jax.nn.gelu(hidden, approximate=False))
    return middle + low_back(apply_matrix(active, down_matrix))

def reference(ends_in, live, gain_attn, w_qkv, w_out, gain_mlp, w_up, w_down):
    per_device = MICRO * IMG_DEV
    image_ids = jnp.arange(IMAGES, dtype=jnp.int32)
    slot_ids = image_ids % per_device
    owner_ids = image_ids // per_device
    live_mask = (slot_ids % IMG_DEV < live[slot_ids // IMG_DEV, owner_ids]).astype(jnp.float32)
    float_weights = tuple((member.astype(jnp.float32) for member in (gain_attn, w_qkv, w_out, gain_mlp, w_up, w_down)))
    layer_weights = tuple((tuple((member[layer_idx] for member in float_weights)) for layer_idx in range(2)))
    block_images = 16
    blocks = IMAGES // block_images
    inputs = ends_in[0].astype(jnp.float32).reshape(blocks, block_images, SEQ, D)
    cotangent = ends_in[1].astype(jnp.float32).reshape(blocks, block_images, SEQ, D)
    mask_blocks = live_mask.reshape(blocks, block_images)

    def one_block(running, block_item):
        block_in, block_cot, block_mask = block_item

        def forward(first_in, params):
            between = low(low_back(encoder(first_in, params[0])))
            return encoder(between, params[1]) * block_mask[:, None, None]
        outputs, pullback = jax.vjp(forward, block_in, layer_weights)
        grad_in, grad_params = pullback(block_cot)
        running = jax.tree.map(jnp.add, running, grad_params)
        return (running, (grad_in, outputs))
    zeros_tree = jax.tree.map(jnp.zeros_like, layer_weights)
    grad_sums, (grad_in, outputs) = lax.scan(one_block, zeros_tree, (inputs, cotangent, mask_blocks))
    ends_out = jnp.stack([grad_in.reshape(IMAGES, SEQ, D), outputs.reshape(IMAGES, SEQ, D)]).astype(jnp.bfloat16)
    stacked = tuple((jnp.stack([grad_sums[0][member_idx], grad_sums[1][member_idx]]) for member_idx in range(6)))
    return (ends_out, stacked[0], stacked[1], stacked[2], stacked[3], stacked[4], stacked[5])
```

```python
import functools

import jax
import jax.numpy as jnp
from jax import lax
from jax.experimental import pallas as pl
from jax.experimental.pallas import tpu as pltpu
from jax.sharding import PartitionSpec as P

HEADS = 6
HEAD_DIM = 64
EPS = 1e-06
BF = jnp.bfloat16
F32 = jnp.float32
VMEM_LIMIT = 56 * 1024 * 1024
PER_STEP = 2
MOST_PIECES = 8


def dot_nn(a, b):
    return lax.dot_general(a, b, (((1,), (0,)), ((), ())), preferred_element_type=F32)


def dot_nt(a, b):
    return lax.dot_general(a, b, (((1,), (1,)), ((), ())), preferred_element_type=F32)


def norm_rows(values):
    centered = values - jnp.mean(values, axis=-1, keepdims=True)
    scale = lax.rsqrt(jnp.mean(centered * centered, axis=-1, keepdims=True) + EPS)
    return centered * scale, scale


def norm_rows_back(grad_normed, normed, scale):
    first = jnp.mean(grad_normed, axis=-1, keepdims=True)
    second = jnp.mean(grad_normed * normed, axis=-1, keepdims=True)
    return scale * (grad_normed - first - normed * second)


def gelu_both(v):
    cdf = 0.5 * (1.0 + lax.erf(v * 0.7071067811865476))
    density = jnp.exp(-0.5 * v * v) * 0.3989422804014327
    return v * cdf, cdf + v * density


def attn_fwd_kernel(length, x_ref, gain_ref, wqkv_ref, wout_ref,
                    qkv_ref, probs_ref, mixt_ref, mid_ref, entry_s, qkv_s, mixed_s):
    images, rows, width = x_ref.shape
    for g in range(images):
        normed, _ = norm_rows(x_ref[g].astype(F32))
        entry_s[g * rows:(g + 1) * rows, :] = (normed * gain_ref[...]).astype(BF)
    joint = dot_nn(entry_s[...], wqkv_ref[...]).astype(BF)
    qkv_s[...] = joint
    lane = lax.broadcasted_iota(jnp.int32, (rows, 2 * HEAD_DIM), 1)
    cut = (length // 8) * 8
    tail_row = lax.broadcasted_iota(jnp.int32, (rows - cut, rows), 0) + cut
    for g in range(images):
        qkv_ref[g] = qkv_s[g * rows:(g + 1) * rows, :]
        for pair in range(HEADS // 2):
            at = pair * 2 * HEAD_DIM
            q = qkv_s[g * rows:(g + 1) * rows, at:at + 2 * HEAD_DIM] * 0.125
            k = qkv_s[g * rows:(g + 1) * rows, width + at:width + at + 2 * HEAD_DIM]
            v = qkv_s[g * rows:(g + 1) * rows, 2 * width + at:2 * width + at + 2 * HEAD_DIM]
            v_t = v.T
            for side in range(2):
                own = (lane // HEAD_DIM) == side
                scores = dot_nt(k, jnp.where(own, q, jnp.zeros_like(q)))
                tail = jnp.where(tail_row < length, scores[cut:], -1e30)
                top = jnp.maximum(jnp.max(scores[:cut], axis=0, keepdims=True),
                                  jnp.max(tail, axis=0, keepdims=True))
                e_top = jnp.exp(scores[:cut] - top)
                e_tail = jnp.exp(tail - top)
                total = jnp.sum(e_top, axis=0, keepdims=True) + jnp.sum(e_tail, axis=0, keepdims=True)
                inv = 1.0 / total
                head = pair * 2 + side
                probs = jnp.concatenate([e_top * inv, e_tail * inv], axis=0).astype(BF)
                probs_ref[g, head] = probs
                mixed = dot_nn(v_t[side * HEAD_DIM:(side + 1) * HEAD_DIM], probs)
                mixt_ref[g, head * HEAD_DIM:(head + 1) * HEAD_DIM, :] = mixed.astype(BF)
        mixed_s[g * rows:(g + 1) * rows, :] = mixt_ref[g].T
    added = dot_nn(mixed_s[...], wout_ref[...])
    for g in range(images):
        mid_ref[g] = x_ref[g].astype(F32) + added[g * rows:(g + 1) * rows]


def mlp_fwd_kernel(mid_ref, gain_ref, wup_ref, wdown_ref, out_ref, act_ref, slope_ref, entry_s, act_s):
    images, rows, width = mid_ref.shape
    for g in range(images):
        normed, _ = norm_rows(mid_ref[g])
        entry_s[g * rows:(g + 1) * rows, :] = (normed * gain_ref[...]).astype(BF)
    hidden_width = wup_ref.shape[1]
    step = 256
    for at in range(0, hidden_width, step):
        hidden = dot_nn(entry_s[...], wup_ref[:, at:at + step])
        act, slope = gelu_both(hidden)
        act_s[:, at:at + step] = act.astype(BF)
        for g in range(images):
            slope_ref[g, :, at:at + step] = slope[g * rows:(g + 1) * rows].astype(BF)
    added = dot_nn(act_s[...], wdown_ref[...])
    for g in range(images):
        act_ref[g] = act_s[g * rows:(g + 1) * rows, :]
        out_ref[g] = (mid_ref[g] + added[g * rows:(g + 1) * rows]).astype(BF)


def mlp_bwd_kernel(cot_ref, mid_ref, act_ref, slope_ref, gain_ref, wup_ref, wdown_ref,
                   gmid_ref, gup_ref, gdown_ref, up_acc, down_acc, entry_t, cot_t, gh_s):
    images, rows, width = mid_ref.shape
    step_id = pl.program_id(0)

    @pl.when(step_id == 0)
    def _():
        up_acc[...] = jnp.zeros_like(up_acc)
        down_acc[...] = jnp.zeros_like(down_acc)

    hidden_width = wup_ref.shape[1]
    step = 256
    for g in range(images):
        cot = cot_ref[g]
        normed, scale = norm_rows(mid_ref[g])
        entry = (normed * gain_ref[...]).astype(BF)
        entry_t[...] = entry.T
        cot_t[...] = cot.T
        for at in range(0, hidden_width, step):
            grad_act = dot_nt(cot, wdown_ref[at:at + step, :])
            gh_s[:, at:at + step] = (grad_act * slope_ref[g, :, at:at + step].astype(F32)).astype(BF)
        up_acc[...] += dot_nn(entry_t[...], gh_s[...])
        down_acc[...] += dot_nn(cot_t[...], act_ref[g])
        grad_entry = dot_nt(gh_s[...], wup_ref[...])
        back = norm_rows_back(grad_entry * gain_ref[...], normed, scale)
        gmid_ref[g] = cot.astype(F32) + back

    @pl.when(step_id == pl.num_programs(0) - 1)
    def _():
        gup_ref[...] = up_acc[...].astype(BF)
        for at in range(0, hidden_width, 128):
            gdown_ref[at:at + 128, :] = down_acc[:, at:at + 128].T.astype(BF)


def attn_bwd_kernel(gmid_ref, x_ref, qkv_ref, probs_ref, mixt_ref, gain_ref, wqkv_ref, wout_ref,
                    gx_ref, gqkv_ref, gout_ref, qkv_acc, out_acc, joint_s, entry_t):
    images, rows, width = x_ref.shape
    step_id = pl.program_id(0)

    @pl.when(step_id == 0)
    def _():
        qkv_acc[...] = jnp.zeros_like(qkv_acc)
        out_acc[...] = jnp.zeros_like(out_acc)

    lane = lax.broadcasted_iota(jnp.int32, (rows, 2 * HEAD_DIM), 1)
    for g in range(images):
        normed, scale = norm_rows(x_ref[g].astype(F32))
        entry_t[...] = (normed * gain_ref[...]).astype(BF).T
        low = gmid_ref[g].astype(BF)
        out_acc[...] += dot_nn(mixt_ref[g], low)
        grad_mixed = dot_nt(low, wout_ref[...]).astype(BF)
        grad_mixed_t = dot_nt(wout_ref[...], low).astype(BF)
        for pair in range(HEADS // 2):
            at = pair * 2 * HEAD_DIM
            q = qkv_ref[g, :, at:at + 2 * HEAD_DIM] * 0.125
            k = qkv_ref[g, :, width + at:width + at + 2 * HEAD_DIM]
            v = qkv_ref[g, :, 2 * width + at:2 * width + at + 2 * HEAD_DIM]
            k_t = (k * 0.125).T
            gm = grad_mixed[:, at:at + 2 * HEAD_DIM]
            grad_k = None
            grad_v = None
            grad_q_t = []
            for side in range(2):
                head = pair * 2 + side
                lo = head * HEAD_DIM
                own = (lane // HEAD_DIM) == side
                gm_own = jnp.where(own, gm, jnp.zeros_like(gm))
                q_own = jnp.where(own, q, jnp.zeros_like(q))
                probs = probs_ref[g, head]
                delta = jnp.sum(grad_mixed_t[lo:lo + HEAD_DIM].astype(F32)
                                * mixt_ref[g, lo:lo + HEAD_DIM, :].astype(F32), axis=0, keepdims=True)
                grad_probs = dot_nt(v, gm_own)
                grad_scores = (probs.astype(F32) * (grad_probs - delta)).astype(BF)
                part_v = dot_nn(probs, gm_own)
                part_k = dot_nn(grad_scores, q_own)
                grad_v = part_v if grad_v is None else grad_v + part_v
                grad_k = part_k if grad_k is None else grad_k + part_k
                grad_q_t.append(dot_nn(k_t[side * HEAD_DIM:(side + 1) * HEAD_DIM], grad_scores))
            grad_q = jnp.concatenate(grad_q_t, axis=0).astype(BF).T
            joint_s[:, at:at + 2 * HEAD_DIM] = grad_q
            joint_s[:, width + at:width + at + 2 * HEAD_DIM] = grad_k.astype(BF)
            joint_s[:, 2 * width + at:2 * width + at + 2 * HEAD_DIM] = grad_v.astype(BF)
        qkv_acc[...] += dot_nn(entry_t[...], joint_s[...])
        grad_entry = dot_nt(joint_s[...], wqkv_ref[...])
        back = norm_rows_back(grad_entry * gain_ref[...], normed, scale)
        gx_ref[g] = (gmid_ref[g] + back).astype(BF)

    @pl.when(step_id == pl.num_programs(0) - 1)
    def _():
        gqkv_ref[...] = qkv_acc[...].astype(BF)
        gout_ref[...] = out_acc[...].astype(BF)


def per_image(shape, g):
    return pl.BlockSpec((g,) + shape[1:], lambda i: (i,) + (0,) * (len(shape) - 1))


def whole(shape):
    return pl.BlockSpec(shape, lambda i: (0,) * len(shape))


def call(body, name, streams, fixed, stream_outs, fixed_outs, scratch, flops):
    images = streams[0].shape[0]
    g = PER_STEP if images % PER_STEP == 0 else 1
    outs = [jax.ShapeDtypeStruct(s, d) for s, d in stream_outs + fixed_outs]
    moved = sum(a.size * a.dtype.itemsize for a in list(streams) + list(fixed) + outs)
    return pl.pallas_call(
        body,
        name=name,
        grid=(images // g,),
        in_specs=[per_image(a.shape, g) for a in streams] + [whole(a.shape) for a in fixed],
        out_specs=[per_image(s, g) for s, _ in stream_outs] + [whole(s) for s, _ in fixed_outs],
        out_shape=outs,
        scratch_shapes=scratch(g),
        compiler_params=pltpu.CompilerParams(vmem_limit_bytes=VMEM_LIMIT, dimension_semantics=("arbitrary",)),
        cost_estimate=pl.CostEstimate(flops=int(flops), bytes_accessed=int(moved), transcendentals=0),
    )(*streams, *fixed)


def attn_fwd(x, length, gain, wqkv, wout):
    n, rows, width = x.shape
    return call(
        functools.partial(attn_fwd_kernel, length), "attention_forward", [x], [gain, wqkv, wout],
        [((n, rows, 3 * width), BF), ((n, HEADS, rows, rows), BF), ((n, width, rows), BF), ((n, rows, width), F32)],
        [],
        lambda g: [pltpu.VMEM((g * rows, width), BF), pltpu.VMEM((g * rows, 3 * width), BF), pltpu.VMEM((g * rows, width), BF)],
        2 * n * rows * width * 4 * width + 4 * n * rows * rows * width)


def mlp_fwd(mid, gain, wup, wdown):
    n, rows, width = mid.shape
    ff = wup.shape[1]
    return call(
        mlp_fwd_kernel, "mlp_forward", [mid], [gain, wup, wdown],
        [((n, rows, width), BF), ((n, rows, ff), BF), ((n, rows, ff), BF)], [],
        lambda g: [pltpu.VMEM((g * rows, width), BF), pltpu.VMEM((g * rows, ff), BF)],
        4 * n * rows * width * ff)


def mlp_bwd(cot, mid, act, slope, gain, wup, wdown):
    n, rows, width = mid.shape
    ff = wup.shape[1]
    return call(
        mlp_bwd_kernel, "mlp_backward", [cot, mid, act, slope], [gain, wup, wdown],
        [((n, rows, width), F32)], [((width, ff), BF), ((ff, width), BF)],
        lambda g: [pltpu.VMEM((width, ff), F32), pltpu.VMEM((width, ff), F32), pltpu.VMEM((width, rows), BF),
                   pltpu.VMEM((width, rows), BF), pltpu.VMEM((rows, ff), BF)],
        8 * n * rows * width * ff)


def attn_bwd(gmid, x, qkv, probs, mixt, gain, wqkv, wout):
    n, rows, width = x.shape
    return call(
        attn_bwd_kernel, "attention_backward", [gmid, x, qkv, probs, mixt], [gain, wqkv, wout],
        [((n, rows, width), BF)], [((width, 3 * width), BF), ((width, width), BF)],
        lambda g: [pltpu.VMEM((width, 3 * width), F32), pltpu.VMEM((width, width), F32),
                   pltpu.VMEM((rows, 3 * width), BF), pltpu.VMEM((width, rows), BF)],
        4 * n * rows * width * 4 * width + 10 * n * rows * rows * width)


def swap_section(value):
    return lax.ppermute(value, "section", [(0, 1), (1, 0)])


def pick(stack, index):
    return lax.dynamic_index_in_dim(stack, index, 0, keepdims=False)


def after(value, *others):
    return lax.optimization_barrier((value,) + others)[0]


def spread(value, axis):
    size = lax.axis_size(axis)
    me = lax.axis_index(axis)
    if size & (size - 1) or size > MOST_PIECES:
        return lax.all_gather(value, axis)
    full = jnp.zeros((size,) + value.shape, value.dtype)
    full = lax.dynamic_update_index_in_dim(full, value, me, 0)
    for k in range(1, size):
        piece = lax.ppermute(value, axis, [(i, i ^ k) for i in range(size)])
        full = lax.dynamic_update_index_in_dim(full, piece, me ^ k, 0)
    return full


def scatter_sum(stack, axis, dim):
    size = lax.axis_size(axis)
    me = lax.axis_index(axis)
    if size & (size - 1) or size > MOST_PIECES:
        return lax.psum_scatter(stack, axis, scatter_dimension=dim)
    total = lax.dynamic_index_in_dim(stack, me, dim, keepdims=False).astype(F32)
    for k in range(1, size):
        sent = lax.dynamic_index_in_dim(stack, me ^ k, dim, keepdims=False)
        total = total + lax.ppermute(sent, axis, [(i, i ^ k) for i in range(size)]).astype(F32)
    return total.astype(BF)


def all_sum(value, axis):
    size = lax.axis_size(axis)
    if size & (size - 1) or size > MOST_PIECES:
        return lax.psum(value, axis)
    total = value.astype(F32)
    for k in range(1, size):
        total = total + lax.ppermute(value, axis, [(i, i ^ k) for i in range(size)]).astype(F32)
    return total.astype(BF)


def gather_group(half, me):
    mine = spread(half, "fsdp")
    other = swap_section(mine)
    both = jnp.zeros((2,) + mine.shape, mine.dtype)
    both = lax.dynamic_update_index_in_dim(both, mine, me, 0)
    both = lax.dynamic_update_index_in_dim(both, other, 1 - me, 0)
    both = both.transpose(0, 2, 1, 3, 4)
    return both.reshape(2 * half.shape[0], -1, half.shape[2])


def reduce_group(halves, me):
    other = swap_section(pick(halves, 1 - me))
    chip = (pick(halves, me).astype(F32) + other.astype(F32)).astype(BF)
    return all_sum(scatter_sum(chip, "fsdp", 1), "replica")


def local(ends_in, live, gain_attn, w_qkv, w_out, gain_mlp, w_up, w_down):
    me = lax.axis_index("section")
    first = me == 0
    shards = lax.axis_size("fsdp")
    slots, length, width = ends_in.shape[1:]
    share = slots // 2
    rows = -(-length // 16) * 16
    depth = w_qkv.shape[1]
    ratio = w_up.shape[2] // width

    def columns(matrix):
        return matrix[0].reshape(depth, -1, width).transpose(1, 0, 2)

    attn_own = jnp.concatenate([columns(w_qkv), columns(w_out)]).reshape(2, 2, depth, width)
    mlp_own = jnp.stack([columns(w_up), w_down[0].reshape(ratio, depth, width)])
    gains_own = jnp.stack([gain_attn[0], gain_mlp[0]])

    def by_layer(own):
        kept, came = pick(own, me), swap_section(pick(own, 1 - me))
        return jnp.where(first, kept, came), jnp.where(first, came, kept)

    attn_halves = by_layer(attn_own)
    mlp_halves = by_layer(mlp_own)
    gains_mine = spread(gains_own, "fsdp").transpose(1, 0, 2).reshape(2, 1, width).astype(F32)
    gains_other = swap_section(gains_mine.astype(BF)).astype(F32)
    gains = (jnp.where(first, gains_mine, gains_other), jnp.where(first, gains_other, gains_mine))

    images = ends_in[0].reshape(2, share, length, width)
    kept = pick(images, me)
    came = swap_section(pick(images, 1 - me))
    slot_ids = jnp.arange(slots, dtype=jnp.int32)
    per_micro = slots // live.shape[0]
    mask = (slot_ids % per_micro < live[:, 0][slot_ids // per_micro]).reshape(2, share)
    mask = pick(mask, me)[:, None, None]
    pad = ((0, 0), (0, rows - length), (0, 0))
    x0 = jnp.pad(jnp.where(first, kept, came), pad)
    cot1 = jnp.pad(jnp.where(mask, jnp.where(first, came, kept), 0), pad)

    def attn_weights(layer):
        blocks = gather_group(attn_halves[layer], me)
        return blocks[:3].transpose(1, 0, 2).reshape(width, 3 * width), blocks[3]

    def mlp_weights(layer):
        blocks = gather_group(mlp_halves[layer], me)
        up = blocks[:ratio].transpose(1, 0, 2).reshape(width, ratio * width)
        down = blocks[ratio:].reshape(ratio, shards, depth, width).transpose(1, 0, 2, 3)
        return up, down.reshape(ratio * width, width)

    weights = [attn_weights(l) + mlp_weights(l) for l in range(2)]

    def forward(x, layer):
        wqkv, wout, wup, wdown = weights[layer]
        qkv, probs, mixt, mid = attn_fwd(x, length, gains[layer][0], wqkv, wout)
        out, act, slope = mlp_fwd(mid, gains[layer][1], wup, wdown)
        return out, (x, qkv, probs, mixt, mid, act, slope)

    def backward(cot, kept, layer):
        wqkv, wout, wup, wdown = weights[layer]
        x, qkv, probs, mixt, mid, act, slope = kept
        gmid, gup, gdown = mlp_bwd(cot, mid, act, slope, gains[layer][1], wup, wdown)
        gup = gup.reshape(shards, depth, ratio, width).transpose(2, 0, 1, 3)
        gdown = gdown.reshape(shards, ratio, depth, width).transpose(1, 0, 2, 3)
        mlp_sum = reduce_group(jnp.stack([gup, gdown]), me)
        gx, gqkv, gout = attn_bwd(gmid, x, qkv, probs, mixt, gains[layer][0], wqkv, wout)
        gqkv = gqkv.reshape(shards, depth, 3, width).transpose(2, 0, 1, 3)
        gout = gout.reshape(1, shards, depth, width)
        attn_sum = reduce_group(jnp.concatenate([gqkv, gout]).reshape(2, 2, shards, depth, width), me)
        return gx, attn_sum, mlp_sum

    x1, kept0 = forward(x0, 0)
    out, kept1 = forward(x1, 1)
    cot0, attn_sum1, mlp_sum1 = backward(cot1, kept1, 1)
    gx, attn_sum0, mlp_sum0 = backward(cot0, kept0, 0)

    def own_layer(sum0, sum1):
        mine = jnp.where(first, sum0, sum1)
        other = swap_section(jnp.where(first, sum1, sum0))
        return jnp.concatenate([jnp.where(first, mine, other), jnp.where(first, other, mine)]).astype(F32)

    mlp_grad = own_layer(mlp_sum0, mlp_sum1)
    attn_grad = own_layer(attn_sum0, attn_sum1)

    def rows_of(blocks):
        return blocks.transpose(1, 0, 2).reshape(1, depth, -1)

    grad_qkv, grad_out = rows_of(attn_grad[:3]), attn_grad[3:]
    grad_up, grad_down = rows_of(mlp_grad[:ratio]), mlp_grad[ratio:].reshape(1, ratio * depth, width)
    grad_gain_attn = jnp.sum(grad_qkv * w_qkv.astype(F32), axis=-1) / gain_attn.astype(F32)
    grad_gain_mlp = jnp.sum(grad_up * w_up.astype(F32), axis=-1) / gain_mlp.astype(F32)

    gx = gx[:, :length]
    out = jnp.where(mask, out[:, :length], 0)
    came = swap_section(jnp.where(first, out, gx))
    ends_out = jnp.zeros(images.shape, BF)
    ends_out = lax.dynamic_update_index_in_dim(ends_out, jnp.where(first, gx, out), me, 0)
    ends_out = lax.dynamic_update_index_in_dim(ends_out, came, 1 - me, 0)
    return (ends_out.reshape(ends_in.shape), grad_gain_attn, grad_qkv, grad_out, grad_gain_mlp, grad_up, grad_down)


def solution(mesh):
    in_specs = (
        P("section", ("fsdp", "replica"), None, None),
        P(None, ("fsdp", "replica")),
        P("section", "fsdp"),
        P("section", "fsdp", None),
        P("section", "fsdp", None),
        P("section", "fsdp"),
        P("section", "fsdp", None),
        P("section", "fsdp", None),
    )
    out_specs = (
        P("section", ("fsdp", "replica"), None, None),
        P("section", "fsdp"),
        P("section", "fsdp", None),
        P("section", "fsdp", None),
        P("section", "fsdp"),
        P("section", "fsdp", None),
        P("section", "fsdp", None),
    )
    return jax.shard_map(local, mesh=mesh, in_specs=in_specs, out_specs=out_specs, check_vma=False)
```

```python
import functools

import jax
import jax.numpy as jnp
from jax import lax
from jax.experimental import pallas as pl
from jax.experimental.pallas import tpu as pltpu
from jax.sharding import PartitionSpec as P

HEADS = 6
HEAD_DIM = 64
PAIR = 2 * HEAD_DIM
EPS = 1e-06
BF = jnp.bfloat16
F32 = jnp.float32
VMEM_LIMIT = 56 * 1024 * 1024
PER_STEP = 2
MOST_PIECES = 8


def dot_nn(a, b):
    return lax.dot_general(a, b, (((1,), (0,)), ((), ())), preferred_element_type=F32)


def dot_nt(a, b):
    return lax.dot_general(a, b, (((1,), (1,)), ((), ())), preferred_element_type=F32)


def norm_rows(values):
    centered = values - jnp.mean(values, axis=-1, keepdims=True)
    scale = lax.rsqrt(jnp.mean(centered * centered, axis=-1, keepdims=True) + EPS)
    return centered * scale, scale


def norm_rows_back(grad_normed, normed, scale):
    first = jnp.mean(grad_normed, axis=-1, keepdims=True)
    second = jnp.mean(grad_normed * normed, axis=-1, keepdims=True)
    return scale * (grad_normed - first - normed * second)


def gelu_both(v):
    cdf = 0.5 * (1.0 + lax.erf(v * 0.7071067811865476))
    density = jnp.exp(-0.5 * v * v) * 0.3989422804014327
    return v * cdf, cdf + v * density


def place_attn(ids_ref, pieces, weight_ref):
    count = len(pieces) // 2
    width = weight_ref.shape[0]
    depth = width // count
    for section in range(2):
        @pl.when(ids_ref[0] == section)
        def _():
            for k in range(count):
                at = pl.ds(pl.multiple_of((ids_ref[1] ^ k) * depth, depth), depth)
                for half, piece in ((section, pieces[k]), (1 - section, pieces[count + k])):
                    for b in range(2):
                        lanes = (2 * half + b) * width
                        weight_ref[at, lanes:lanes + width] = piece[b * depth:(b + 1) * depth, :]


def place_mlp(ids_ref, pieces, up_ref, down_ref):
    count = len(pieces) // 2
    width, hidden = up_ref.shape
    depth = width // count
    tall = hidden // count
    for section in range(2):
        @pl.when(ids_ref[0] == section)
        def _():
            for k in range(count):
                shard = ids_ref[1] ^ k
                at = pl.ds(pl.multiple_of(shard * depth, depth), depth)
                for half, piece in ((section, pieces[k]), (1 - section, pieces[count + k])):
                    if half == 0:
                        for b in range(hidden // width):
                            up_ref[at, b * width:(b + 1) * width] = piece[b * depth:(b + 1) * depth, :]
                    else:
                        down_ref[pl.ds(pl.multiple_of(shard * tall, tall), tall), :] = piece[...]


def attn_fwd_kernel(length, count, entering, ids_ref, *refs):
    if entering:
        own_ref, came_ref = refs[:2]
        pieces, refs = refs[2:2 + 2 * count], refs[2 + 2 * count:]
        qkv_ref, probs_ref, mixt_ref, mid_ref, weight_ref, x_ref, entry_s, qkv_s, mixed_s, pad_s = refs
    else:
        x_ref = refs[0]
        pieces, refs = refs[1:1 + 2 * count], refs[1 + 2 * count:]
        qkv_ref, probs_ref, mixt_ref, mid_ref, weight_ref, entry_s, qkv_s, mixed_s = refs
    images, rows, width = x_ref.shape

    @pl.when(pl.program_id(0) == 0)
    def _():
        place_attn(ids_ref, pieces, weight_ref)
        if entering:
            pad_s[...] = jnp.zeros_like(pad_s)

    for g in range(images):
        if entering:
            pad_s[g, :length, :] = jnp.where(ids_ref[0] == 0, own_ref[g].astype(F32), came_ref[g].astype(F32))
            values = pad_s[g]
            x_ref[g] = values.astype(BF)
        else:
            values = x_ref[g].astype(F32)
        normed, _ = norm_rows(values)
        entry_s[g * rows:(g + 1) * rows, :] = normed.astype(BF)
    qkv_s[...] = dot_nn(entry_s[...], weight_ref[:, :3 * width]).astype(BF)
    lane = lax.broadcasted_iota(jnp.int32, (rows, PAIR), 1)
    cut = (length // 8) * 8
    tail_row = lax.broadcasted_iota(jnp.int32, (rows - cut, rows), 0) + cut
    for g in range(images):
        qkv_ref[g] = qkv_s[g * rows:(g + 1) * rows, :]
        for pair in range(HEADS // 2):
            at = pair * PAIR
            q = qkv_s[g * rows:(g + 1) * rows, at:at + PAIR] * 0.125
            k = qkv_s[g * rows:(g + 1) * rows, width + at:width + at + PAIR]
            v = qkv_s[g * rows:(g + 1) * rows, 2 * width + at:2 * width + at + PAIR]
            v_t = v.T
            for side in range(2):
                own = (lane // HEAD_DIM) == side
                scores = dot_nt(k, jnp.where(own, q, jnp.zeros_like(q)))
                tail = jnp.where(tail_row < length, scores[cut:], -1e30)
                top = jnp.maximum(jnp.max(scores[:cut], axis=0, keepdims=True),
                                  jnp.max(tail, axis=0, keepdims=True))
                e_top = jnp.exp(scores[:cut] - top)
                e_tail = jnp.exp(tail - top)
                total = jnp.sum(e_top, axis=0, keepdims=True) + jnp.sum(e_tail, axis=0, keepdims=True)
                inv = 1.0 / total
                head = pair * 2 + side
                probs = jnp.concatenate([e_top * inv, e_tail * inv], axis=0).astype(BF)
                probs_ref[g, head] = probs
                mixed = dot_nn(v_t[side * HEAD_DIM:(side + 1) * HEAD_DIM], probs)
                mixt_ref[g, head * HEAD_DIM:(head + 1) * HEAD_DIM, :] = mixed.astype(BF)
        mixed_s[g * rows:(g + 1) * rows, :] = mixt_ref[g].T
    added = dot_nn(mixed_s[...], weight_ref[:, 3 * width:])
    for g in range(images):
        mid_ref[g] = x_ref[g].astype(F32) + added[g * rows:(g + 1) * rows]


def mlp_fwd_kernel(length, count, leaving, ids_ref, mid_ref, *refs):
    pieces, refs = refs[:2 * count], refs[2 * count:]
    out_ref, act_ref, slope_ref, up_ref, down_ref, entry_s, act_s = refs
    images, rows, width = mid_ref.shape
    hidden_width = up_ref.shape[1]

    @pl.when(pl.program_id(0) == 0)
    def _():
        place_mlp(ids_ref, pieces, up_ref, down_ref)

    for g in range(images):
        normed, _ = norm_rows(mid_ref[g])
        entry_s[g * rows:(g + 1) * rows, :] = normed.astype(BF)
    step = 256
    for at in range(0, hidden_width, step):
        hidden = dot_nn(entry_s[...], up_ref[:, at:at + step])
        act, slope = gelu_both(hidden)
        act_s[:, at:at + step] = act.astype(BF)
        for g in range(images):
            slope_ref[g, :, at:at + step] = slope[g * rows:(g + 1) * rows].astype(BF)
    added = dot_nn(act_s[...], down_ref[...])
    for g in range(images):
        act_ref[g] = act_s[g * rows:(g + 1) * rows, :]
        out = mid_ref[g] + added[g * rows:(g + 1) * rows]
        if leaving:
            live = pl.program_id(0) * images + g < ids_ref[2]
            out_ref[g] = jnp.where(live, out[:length], 0.0).astype(BF)
        else:
            out_ref[g] = out.astype(BF)


def mlp_bwd_kernel(length, count, entering, ids_ref, *refs):
    if entering:
        own_ref, came_ref, *refs = refs
        *refs, pad_s = refs
    else:
        cot_ref, *refs = refs
    mid_ref, act_ref, slope_ref, up_ref, down_ref, gmid_ref, keep_ref, send_ref, *refs = refs
    up_acc, down_acc, entry_t, cot_t, gh_s = refs
    images, rows, width = mid_ref.shape
    step_id = pl.program_id(0)

    @pl.when(step_id == 0)
    def _():
        up_acc[...] = jnp.zeros_like(up_acc)
        down_acc[...] = jnp.zeros_like(down_acc)
        if entering:
            pad_s[...] = jnp.zeros_like(pad_s)

    hidden_width = up_ref.shape[1]
    step = 256
    for g in range(images):
        if entering:
            live = step_id * images + g < ids_ref[2]
            came = jnp.where(ids_ref[0] == 0, came_ref[g].astype(F32), own_ref[g].astype(F32))
            pad_s[:length, :] = jnp.where(live, came, 0.0)
            cot = pad_s[...].astype(BF)
        else:
            cot = cot_ref[g]
        normed, scale = norm_rows(mid_ref[g])
        entry_t[...] = normed.astype(BF).T
        cot_t[...] = cot.T
        for at in range(0, hidden_width, step):
            grad_act = dot_nt(cot, down_ref[at:at + step, :])
            gh_s[:, at:at + step] = (grad_act * slope_ref[g, :, at:at + step].astype(F32)).astype(BF)
        up_acc[...] += dot_nn(entry_t[...], gh_s[...])
        down_acc[...] += dot_nn(cot_t[...], act_ref[g])
        grad_entry = dot_nt(gh_s[...], up_ref[...])
        gmid_ref[g] = cot.astype(F32) + norm_rows_back(grad_entry, normed, scale)

    @pl.when(step_id == pl.num_programs(0) - 1)
    def _():
        depth = width // count
        tall = hidden_width // count
        for section in range(2):
            @pl.when(ids_ref[0] == section)
            def _():
                for k in range(count):
                    shard = ids_ref[1] ^ k
                    at = pl.ds(pl.multiple_of(shard * depth, depth), depth)
                    up_out, down_out = (keep_ref, send_ref) if section == 0 else (send_ref, keep_ref)
                    for b in range(hidden_width // width):
                        up_out[k, b * depth:(b + 1) * depth, :] = up_acc[at, b * width:(b + 1) * width].astype(BF)
                    for j in range(0, tall, 128):
                        lanes = pl.ds(pl.multiple_of(shard * tall + j, 128), 128)
                        down_out[k, j:j + 128, :] = down_acc[:, lanes].T.astype(BF)


def attn_bwd_kernel(length, count, leaving, ids_ref, gmid_ref, x_ref, qkv_ref, probs_ref, mixt_ref, weight_ref,
                    gx_ref, keep_ref, send_ref, acc, joint_s, entry_t):
    images, rows, width = x_ref.shape
    step_id = pl.program_id(0)

    @pl.when(step_id == 0)
    def _():
        acc[...] = jnp.zeros_like(acc)

    lane = lax.broadcasted_iota(jnp.int32, (rows, PAIR), 1)
    for g in range(images):
        normed, scale = norm_rows(x_ref[g].astype(F32))
        entry_t[...] = normed.astype(BF).T
        low = gmid_ref[g].astype(BF)
        acc[:, 3 * width:] += dot_nn(mixt_ref[g], low)
        grad_mixed = dot_nt(low, weight_ref[:, 3 * width:]).astype(BF)
        grad_mixed_t = dot_nt(weight_ref[:, 3 * width:], low).astype(BF)
        for pair in range(HEADS // 2):
            at = pair * PAIR
            q = qkv_ref[g, :, at:at + PAIR] * 0.125
            k = qkv_ref[g, :, width + at:width + at + PAIR]
            v = qkv_ref[g, :, 2 * width + at:2 * width + at + PAIR]
            k_t = (k * 0.125).T
            gm = grad_mixed[:, at:at + PAIR]
            grad_k = None
            grad_v = None
            grad_q_t = []
            for side in range(2):
                head = pair * 2 + side
                lo = head * HEAD_DIM
                own = (lane // HEAD_DIM) == side
                gm_own = jnp.where(own, gm, jnp.zeros_like(gm))
                q_own = jnp.where(own, q, jnp.zeros_like(q))
                probs = probs_ref[g, head]
                delta = jnp.sum(grad_mixed_t[lo:lo + HEAD_DIM].astype(F32)
                                * mixt_ref[g, lo:lo + HEAD_DIM, :].astype(F32), axis=0, keepdims=True)
                grad_probs = dot_nt(v, gm_own)
                grad_scores = (probs.astype(F32) * (grad_probs - delta)).astype(BF)
                part_v = dot_nn(probs, gm_own)
                part_k = dot_nn(grad_scores, q_own)
                grad_v = part_v if grad_v is None else grad_v + part_v
                grad_k = part_k if grad_k is None else grad_k + part_k
                grad_q_t.append(dot_nn(k_t[side * HEAD_DIM:(side + 1) * HEAD_DIM], grad_scores))
            joint_s[:, at:at + PAIR] = jnp.concatenate(grad_q_t, axis=0).astype(BF).T
            joint_s[:, width + at:width + at + PAIR] = grad_k.astype(BF)
            joint_s[:, 2 * width + at:2 * width + at + PAIR] = grad_v.astype(BF)
        acc[:, :3 * width] += dot_nn(entry_t[...], joint_s[...])
        grad_entry = dot_nt(joint_s[...], weight_ref[:, :3 * width])
        grad_x = gmid_ref[g] + norm_rows_back(grad_entry, normed, scale)
        gx_ref[g] = (grad_x[:length] if leaving else grad_x).astype(BF)

    @pl.when(step_id == pl.num_programs(0) - 1)
    def _():
        depth = width // count
        for section in range(2):
            @pl.when(ids_ref[0] == section)
            def _():
                for k in range(count):
                    at = pl.ds(pl.multiple_of((ids_ref[1] ^ k) * depth, depth), depth)
                    for half, out_ref in ((section, keep_ref), (1 - section, send_ref)):
                        for b in range(2):
                            lanes = (2 * half + b) * width
                            out_ref[k, b * depth:(b + 1) * depth, :] = acc[at, lanes:lanes + width].astype(BF)


def call(body, name, ids, images, entering, streams, fixed, stream_outs, fixed_outs, scratch, flops):
    g = PER_STEP if images % PER_STEP == 0 else 1

    def entering_spec(shape):
        return pl.BlockSpec((g,) + shape[1:], lambda i, ids: (ids[0] * (images // g) + i,) + (0,) * (len(shape) - 1))

    def per_image(shape):
        return pl.BlockSpec((g,) + shape[1:], lambda i, ids: (i,) + (0,) * (len(shape) - 1))

    def whole(shape):
        return pl.BlockSpec(shape, lambda i, ids: (0,) * len(shape))

    outs = [jax.ShapeDtypeStruct(s, d) for s, d in stream_outs + fixed_outs]
    moved = sum(a.size * a.dtype.itemsize for a in list(streams) + list(fixed) + outs)
    return pl.pallas_call(
        body,
        name=name,
        grid_spec=pltpu.PrefetchScalarGridSpec(
            num_scalar_prefetch=1,
            grid=(images // g,),
            in_specs=[entering_spec(a.shape) for a in entering] + [per_image(a.shape) for a in streams]
            + [whole(a.shape) for a in fixed],
            out_specs=[per_image(s) for s, _ in stream_outs] + [whole(s) for s, _ in fixed_outs],
            scratch_shapes=scratch(g),
        ),
        out_shape=outs,
        compiler_params=pltpu.CompilerParams(vmem_limit_bytes=VMEM_LIMIT, dimension_semantics=("arbitrary",)),
        cost_estimate=pl.CostEstimate(flops=int(flops), bytes_accessed=int(moved), transcendentals=0),
    )(ids, *entering, *streams, *fixed)


def attn_fwd(ids, x, pieces, dims, entering):
    n, rows, length, width, ff = dims
    count = len(pieces) // 2
    outs = [((n, rows, 3 * width), BF), ((n, HEADS, rows, rows), BF), ((n, width, rows), BF), ((n, rows, width), F32)]
    fixed_outs = [((width, 4 * width), BF)]
    body = functools.partial(attn_fwd_kernel, length, count, entering)

    def scratch(g):
        refs = [pltpu.VMEM((g * rows, width), BF), pltpu.VMEM((g * rows, 3 * width), BF), pltpu.VMEM((g * rows, width), BF)]
        return refs + ([pltpu.VMEM((g, rows, width), F32)] if entering else [])

    flops = 2 * n * rows * width * 4 * width + 4 * n * rows * rows * width
    if entering:
        def reordered(ids_ref, *refs):
            ins, rest = refs[:2 + 2 * count], refs[2 + 2 * count:]
            qkv, probs, mixt, mid, xp, weight, *scr = rest
            body(ids_ref, *ins, qkv, probs, mixt, mid, weight, xp, *scr)
        return call(reordered, "attention_forward", ids, n, x, [], pieces, outs + [((n, rows, width), BF)], fixed_outs,
                    scratch, flops)
    qkv, probs, mixt, mid, weight = call(body, "attention_forward", ids, n, [], [x], pieces, outs, fixed_outs, scratch, flops)
    return qkv, probs, mixt, mid, x, weight


def mlp_fwd(ids, mid, pieces, dims, leaving):
    n, rows, length, width, ff = dims
    count = len(pieces) // 2
    return call(
        functools.partial(mlp_fwd_kernel, length, count, leaving), "mlp_forward", ids, n, [], [mid], pieces,
        [((n, length if leaving else rows, width), BF), ((n, rows, ff), BF), ((n, rows, ff), BF)],
        [((width, ff), BF), ((ff, width), BF)],
        lambda g: [pltpu.VMEM((g * rows, width), BF), pltpu.VMEM((g * rows, ff), BF)],
        4 * n * rows * width * ff)


def mlp_bwd(ids, cot, mid, act, slope, up, down, dims, count, entering):
    n, rows, length, width, ff = dims
    scratch = [pltpu.VMEM((width, ff), F32), pltpu.VMEM((width, ff), F32), pltpu.VMEM((width, rows), BF),
               pltpu.VMEM((width, rows), BF), pltpu.VMEM((rows, ff), BF)]
    if entering:
        scratch.append(pltpu.VMEM((rows, width), F32))
    half = (count, ff // count, width)
    return call(
        functools.partial(mlp_bwd_kernel, length, count, entering), "mlp_backward", ids, n,
        cot if entering else [], ([] if entering else [cot]) + [mid, act, slope], [up, down],
        [((n, rows, width), F32)], [(half, BF), (half, BF)], lambda g: scratch, 8 * n * rows * width * ff)


def attn_bwd(ids, gmid, x, qkv, probs, mixt, weight, dims, count, leaving):
    n, rows, length, width, ff = dims
    half = (count, 2 * width // count, width)
    return call(
        functools.partial(attn_bwd_kernel, length, count, leaving), "attention_backward", ids, n, [],
        [gmid, x, qkv, probs, mixt], [weight],
        [((n, length if leaving else rows, width), BF)], [(half, BF), (half, BF)],
        lambda g: [pltpu.VMEM((width, 4 * width), F32), pltpu.VMEM((rows, 3 * width), BF), pltpu.VMEM((width, rows), BF)],
        4 * n * rows * width * 4 * width + 10 * n * rows * rows * width)


def swap_section(value):
    return lax.ppermute(value, "section", [(0, 1), (1, 0)])


def pick(stack, index):
    return lax.dynamic_index_in_dim(stack, index, 0, keepdims=False)


def tie(*values):
    return lax.optimization_barrier(values)


def exchange(values, axis):
    size = lax.axis_size(axis)
    return [lax.ppermute(v, axis, [(i, i ^ (k + 1)) for i in range(size)]) for k, v in enumerate(values)]


def direct(size):
    return size & (size - 1) == 0 and size <= MOST_PIECES


def total(first, others):
    result = first.astype(F32)
    for other in others:
        result = result + other.astype(F32)
    return result.astype(BF)


def local(ends_in, live, gain_attn, w_qkv, w_out, gain_mlp, w_up, w_down):
    me = lax.axis_index("section")
    mine_at = lax.axis_index("fsdp")
    first = me == 0
    shards = lax.axis_size("fsdp")
    replicas = lax.axis_size("replica")
    slots, length, width = ends_in.shape[1:]
    share = slots // 2
    rows = -(-length // 16) * 16
    depth = w_qkv.shape[1]
    ff = w_up.shape[2]
    ratio = ff // width
    dims = (share, rows, length, width, ff)
    packed = direct(shards) and depth % 16 == 0
    count = shards if packed else 1

    live_here = pick(live[:, 0], me)
    ids = jnp.stack([me, mine_at if packed else jnp.zeros_like(mine_at), live_here]).astype(jnp.int32)

    def columns(matrix):
        return matrix.reshape(depth, -1, width).transpose(1, 0, 2).reshape(-1, width)

    qkv_scaled = (w_qkv[0].astype(F32) * gain_attn[0].astype(F32)[:, None]).astype(BF)
    up_scaled = (w_up[0].astype(F32) * gain_mlp[0].astype(F32)[:, None]).astype(BF)
    attn_own = jnp.concatenate([columns(qkv_scaled), w_out[0]]).reshape(2, 2 * depth, width)
    mlp_own = jnp.stack([columns(up_scaled), w_down[0]])

    def by_layer(own):
        kept, came = pick(own, me), swap_section(pick(own, 1 - me))
        return jnp.where(first, kept, came), jnp.where(first, came, kept)

    def spread(half, mlp):
        if packed:
            return [half] + exchange([half] * (shards - 1), "fsdp")
        full = lax.all_gather(half, "fsdp")
        blocks = full.reshape(shards, -1, depth, width).transpose(1, 0, 2, 3).reshape(-1, width)
        if mlp:
            blocks = jnp.where(first, blocks, full.reshape(-1, width))
        return [blocks]

    attn0, attn1 = by_layer(attn_own)
    attn0 = spread(attn0, False)
    mlp0, mlp1 = by_layer(mlp_own)
    came_images = swap_section(ends_in[0])
    images = [ends_in[0], came_images]
    attn0 = attn0 + [swap_section(p) for p in attn0]

    *tied, attn1, mlp0 = tie(*attn0, attn1, mlp0)
    attn0 = tied
    mlp0 = spread(mlp0, True)
    attn1 = spread(attn1, False)
    qkv0, probs0, mixt0, mid0, x0, weight0 = attn_fwd(ids, images, attn0, dims, True)

    np_ = len(mlp0)
    mid0, mlp1, *tied = tie(mid0, mlp1, *mlp0, *attn1)
    mlp0, attn1 = tied[:np_], tied[np_:]
    mlp0 = mlp0 + [swap_section(p) for p in mlp0]
    mlp1 = spread(mlp1, True)
    attn1 = attn1 + [swap_section(p) for p in attn1]
    x1, act0, slope0, up0, down0 = mlp_fwd(ids, mid0, mlp0, dims, False)

    x1, *tied = tie(x1, *attn1, *mlp1)
    attn1, mlp1 = tied[:2 * np_], tied[2 * np_:]
    mlp1 = mlp1 + [swap_section(p) for p in mlp1]
    qkv1, probs1, mixt1, mid1, x1, weight1 = attn_fwd(ids, x1, attn1, dims, False)
    mid1, *mlp1 = tie(mid1, *mlp1)
    out, act1, slope1, up1, down1 = mlp_fwd(ids, mid1, mlp1, dims, True)

    def scatter(half, came, mlp):
        if packed:
            parts = [total(half[k], [came[k]]) for k in range(count)]
            return [parts[0]] + exchange(parts[1:], "fsdp")
        chip = total(half, [came])
        blocks = chip.reshape(-1, shards, depth, width).transpose(1, 0, 2, 3).reshape(shards, -1, width)
        if mlp:
            blocks = jnp.where(first, blocks, chip.reshape(shards, -1, width))
        return [lax.psum_scatter(blocks, "fsdp", scatter_dimension=0)]

    def gather_sums(part):
        if direct(replicas):
            return [part] + exchange([part] * (replicas - 1), "replica")
        return [lax.psum(part, "replica")]

    def added(parts):
        return total(parts[0], parts[1:])

    gmid1, keep_m1, send_m1 = mlp_bwd(ids, images, mid1, act1, slope1, up1, down1, dims, count, True)
    came_m1 = swap_section(send_m1)
    came_out = swap_section(out)
    cot0, keep_a1, send_a1 = attn_bwd(ids, gmid1, x1, qkv1, probs1, mixt1, weight1, dims, count, False)

    cot0, came_m1, keep_m1, came_out = tie(cot0, came_m1, keep_m1, came_out)
    parts_m1 = scatter(keep_m1, came_m1, True)
    came_a1 = swap_section(send_a1)
    gmid0, keep_m0, send_m0 = mlp_bwd(ids, cot0, mid0, act0, slope0, up0, down0, dims, count, False)

    n1 = len(parts_m1)
    gmid0, came_a1, keep_a1, *parts_m1 = tie(gmid0, came_a1, keep_a1, *parts_m1)
    sums_m1 = gather_sums(added(parts_m1))
    parts_a1 = scatter(keep_a1, came_a1, False)
    came_m0 = swap_section(send_m0)
    gx, keep_a0, send_a0 = attn_bwd(ids, gmid0, x0, qkv0, probs0, mixt0, weight0, dims, count, True)

    nr = len(sums_m1)
    send_a0, gx, came_m0, keep_m0, *tied = tie(send_a0, gx, came_m0, keep_m0, *sums_m1, *parts_a1)
    sums_m1, parts_a1 = tied[:nr], tied[nr:]
    came_a0 = swap_section(send_a0)
    came_gx = swap_section(gx)
    parts_m0 = scatter(keep_m0, came_m0, True)
    sums_a1 = gather_sums(added(parts_a1))
    parts_a0 = scatter(keep_a0, came_a0, False)
    sums_m0 = gather_sums(added(parts_m0))
    sums_a0 = gather_sums(added(parts_a0))

    def own_layer(parts0, parts1):
        sum0, sum1 = added(parts0), added(parts1)
        mine = jnp.where(first, sum0, sum1)
        other = swap_section(jnp.where(first, sum1, sum0))
        return jnp.concatenate([jnp.where(first, mine, other), jnp.where(first, other, mine)]).astype(F32)

    mlp_grad = own_layer(sums_m0, sums_m1)
    attn_grad = own_layer(sums_a0, sums_a1)

    def rows_of(blocks):
        return blocks.reshape(-1, depth, width).transpose(1, 0, 2).reshape(depth, -1)

    def unscaled(grad, gain, weight):
        return (gain[0].astype(F32)[:, None] * grad)[None], jnp.sum(grad * weight[0].astype(F32), axis=-1)[None]

    grad_qkv, grad_gain_attn = unscaled(rows_of(attn_grad[:3 * depth]), gain_attn, w_qkv)
    grad_up, grad_gain_mlp = unscaled(rows_of(mlp_grad[:ff // width * depth]), gain_mlp, w_up)
    grad_out = attn_grad[3 * depth:][None]
    grad_down = mlp_grad[ratio * depth:][None]

    own = jnp.where(first, gx, out)
    came = jnp.where(first, came_gx, came_out)
    ends_out = jnp.where(first, jnp.concatenate([own, came]), jnp.concatenate([came, own]))
    return (ends_out[None], grad_gain_attn, grad_qkv, grad_out, grad_gain_mlp, grad_up, grad_down)


def solution(mesh):
    in_specs = (
        P("section", ("fsdp", "replica"), None, None),
        P(None, ("fsdp", "replica")),
        P("section", "fsdp"),
        P("section", "fsdp", None),
        P("section", "fsdp", None),
        P("section", "fsdp"),
        P("section", "fsdp", None),
        P("section", "fsdp", None),
    )
    out_specs = (
        P("section", ("fsdp", "replica"), None, None),
        P("section", "fsdp"),
        P("section", "fsdp", None),
        P("section", "fsdp", None),
        P("section", "fsdp"),
        P("section", "fsdp", None),
        P("section", "fsdp", None),
    )
    return jax.shard_map(local, mesh=mesh, in_specs=in_specs, out_specs=out_specs, check_vma=False)
```

```python
import functools

import jax
import jax.numpy as jnp
from jax import lax
from jax.experimental import pallas as pl
from jax.experimental.pallas import tpu as pltpu
from jax.sharding import PartitionSpec as P

HEADS = 6
HEAD_DIM = 64
PAIR = 2 * HEAD_DIM
EPS = 1e-06
BF = jnp.bfloat16
F32 = jnp.float32
VMEM_LIMIT = 56 * 1024 * 1024
PER_STEP = 2
GAIN_ROWS = 16
MOST_PIECES = 8


def dot_nn(a, b):
    return lax.dot_general(a, b, (((1,), (0,)), ((), ())), preferred_element_type=F32)


def dot_nt(a, b):
    return lax.dot_general(a, b, (((1,), (1,)), ((), ())), preferred_element_type=F32)


def dot_tn(a, b):
    return lax.dot_general(a, b, (((0,), (0,)), ((), ())), preferred_element_type=F32)


def norm_rows(values):
    centered = values - jnp.mean(values, axis=-1, keepdims=True)
    scale = lax.rsqrt(jnp.mean(centered * centered, axis=-1, keepdims=True) + EPS)
    return centered * scale, scale


def norm_rows_back(grad_normed, normed, scale):
    first = jnp.mean(grad_normed, axis=-1, keepdims=True)
    second = jnp.mean(grad_normed * normed, axis=-1, keepdims=True)
    return scale * (grad_normed - first - normed * second)


def gelu_both(v):
    cdf = 0.5 * (1.0 + lax.erf(v * 0.7071067811865476))
    density = jnp.exp(-0.5 * v * v) * 0.3989422804014327
    return v * cdf, cdf + v * density


def gain_of(weight_ref, width):
    return weight_ref[width:width + GAIN_ROWS, :width].astype(F32)[:1]


def place_gain(pieces, weight_ref, width):
    rows = sum(piece[-GAIN_ROWS:, :].astype(F32) for piece in pieces)
    weight_ref[width:width + GAIN_ROWS, :width] = rows.astype(BF)


def place_attn(ids_ref, pieces, weight_ref):
    count = len(pieces) // 2
    width = weight_ref.shape[1] // 4
    place_gain(pieces[:count], weight_ref, width)
    depth = width // count
    for section in range(2):
        @pl.when(ids_ref[0] == section)
        def _():
            for k in range(count):
                at = pl.ds(pl.multiple_of((ids_ref[1] ^ k) * depth, depth), depth)
                for half, piece in ((section, pieces[k]), (1 - section, pieces[count + k])):
                    for b in range(2):
                        lanes = (2 * half + b) * width
                        weight_ref[at, lanes:lanes + width] = piece[b * depth:(b + 1) * depth, :]


def place_mlp(ids_ref, pieces, up_ref, down_ref):
    count = len(pieces) // 2
    hidden, width = down_ref.shape
    place_gain(pieces[:count], up_ref, width)
    depth = width // count
    tall = hidden // count
    for section in range(2):
        @pl.when(ids_ref[0] == section)
        def _():
            for k in range(count):
                shard = ids_ref[1] ^ k
                at = pl.ds(pl.multiple_of(shard * depth, depth), depth)
                for half, piece in ((section, pieces[k]), (1 - section, pieces[count + k])):
                    if half == 0:
                        for b in range(hidden // width):
                            up_ref[at, b * width:(b + 1) * width] = piece[b * depth:(b + 1) * depth, :]
                    else:
                        down_ref[pl.ds(pl.multiple_of(shard * tall, tall), tall), :] = piece[:tall, :]


def attn_fwd_kernel(length, count, entering, ids_ref, *refs):
    if entering:
        own_ref, came_ref = refs[:2]
        pieces, refs = refs[2:2 + 2 * count], refs[2 + 2 * count:]
        qkv_ref, probs_ref, mixed_ref, mid_ref, weight_ref, x_ref, entry_s, qkv_s, scores_s, pad_s = refs
    else:
        x_ref = refs[0]
        pieces, refs = refs[1:1 + 2 * count], refs[1 + 2 * count:]
        qkv_ref, probs_ref, mixed_ref, mid_ref, weight_ref, entry_s, qkv_s, scores_s = refs
    images, rows, width = x_ref.shape

    @pl.when(pl.program_id(0) == 0)
    def _():
        place_attn(ids_ref, pieces, weight_ref)
        if entering:
            pad_s[...] = jnp.zeros_like(pad_s)

    gain = gain_of(weight_ref, width)
    for g in range(images):
        if entering:
            pad_s[g, :length, :] = jnp.where(ids_ref[0] == 0, own_ref[g].astype(F32), came_ref[g].astype(F32))
            values = pad_s[g]
            x_ref[g] = values.astype(BF)
        else:
            values = x_ref[g].astype(F32)
        normed, _ = norm_rows(values)
        entry_s[g * rows:(g + 1) * rows, :] = (normed * gain).astype(BF)
    qkv_s[...] = dot_nn(entry_s[...], weight_ref[:width, :3 * width]).astype(BF)
    lane = lax.broadcasted_iota(jnp.int32, (rows, PAIR), 1)
    cut = (length // 8) * 8

    def fill_scores(g):
        own_rows = slice(g * rows, (g + 1) * rows)
        for head in range(HEADS):
            at = head // 2 * PAIR
            q = qkv_s[own_rows, at:at + PAIR] * 0.125
            q = jnp.where((lane // HEAD_DIM) == head % 2, q, jnp.zeros_like(q))
            scores_s[g * HEADS + head, :, :rows] = dot_nt(qkv_s[own_rows, width + at:width + at + PAIR], q)

    def fill_probs(g):
        for head in range(HEADS):
            for lo in range(0, rows, 128):
                hi = min(lo + 128, rows)
                scores = scores_s[g * HEADS + head, :, lo:hi]
                tail_row = lax.broadcasted_iota(jnp.int32, (rows - cut, hi - lo), 0) + cut
                scores = jnp.concatenate([scores[:cut], jnp.where(tail_row < length, scores[cut:], -1e30)], axis=0)
                parts = jnp.exp(scores - jnp.max(scores, axis=0, keepdims=True))
                inv = 1.0 / jnp.sum(parts, axis=0, keepdims=True)
                probs_ref[g, head, :, lo:hi] = (parts * inv).astype(BF)

    def fill_mixed(g):
        own_rows = slice(g * rows, (g + 1) * rows)
        for pair in range(HEADS // 2):
            at = pair * PAIR
            v_t = qkv_s[own_rows, 2 * width + at:2 * width + at + PAIR].T
            mixed = [dot_nn(v_t[side * HEAD_DIM:(side + 1) * HEAD_DIM], probs_ref[g, pair * 2 + side]) for side in range(2)]
            mixed_ref[g, :, at:at + PAIR] = jnp.concatenate(mixed, axis=0).astype(BF).T

    fill_scores(0)
    for g in range(images):
        qkv_ref[g] = qkv_s[g * rows:(g + 1) * rows, :]
        if g + 1 < images:
            fill_scores(g + 1)
        fill_probs(g)
        fill_mixed(g)
    added = dot_nn(mixed_ref[...].reshape(images * rows, width), weight_ref[:width, 3 * width:])
    for g in range(images):
        mid_ref[g] = x_ref[g].astype(F32) + added[g * rows:(g + 1) * rows]


def mlp_fwd_kernel(length, count, leaving, ids_ref, mid_ref, *refs):
    pieces, refs = refs[:2 * count], refs[2 * count:]
    out_ref, act_ref, slope_ref, up_ref, down_ref, entry_s, act_s = refs
    images, rows, width = mid_ref.shape
    hidden_width = up_ref.shape[1]

    @pl.when(pl.program_id(0) == 0)
    def _():
        place_mlp(ids_ref, pieces, up_ref, down_ref)

    gain = gain_of(up_ref, width)
    for g in range(images):
        normed, _ = norm_rows(mid_ref[g])
        entry_s[g * rows:(g + 1) * rows, :] = (normed * gain).astype(BF)
    step = 256
    for at in range(0, hidden_width, step):
        hidden = dot_nn(entry_s[...], up_ref[:width, at:at + step])
        act, slope = gelu_both(hidden)
        act_s[:, at:at + step] = act.astype(BF)
        for g in range(images):
            slope_ref[g, :, at:at + step] = slope[g * rows:(g + 1) * rows].astype(BF)
    added = dot_nn(act_s[...], down_ref[...])
    for g in range(images):
        act_ref[g] = act_s[g * rows:(g + 1) * rows, :]
        out = mid_ref[g] + added[g * rows:(g + 1) * rows]
        if leaving:
            live = pl.program_id(0) * images + g < ids_ref[2]
            out_ref[g] = jnp.where(live, out[:length], 0.0).astype(BF)
        else:
            out_ref[g] = out.astype(BF)


def mlp_bwd_kernel(length, count, entering, entry_ready, ids_ref, *refs):
    if entering:
        own_ref, came_ref, *refs = refs
        *refs, pad_s = refs
    else:
        cot_ref, *refs = refs
    mid_ref, act_ref, slope_ref, up_ref, down_ref, gmid_ref, keep_ref, send_ref, *refs = refs
    up_acc, down_acc, entry_s, cot_s, gh_s = refs
    images, rows, width = mid_ref.shape
    step_id = pl.program_id(0)

    @pl.when(step_id == 0)
    def _():
        up_acc[...] = jnp.zeros_like(up_acc)
        down_acc[...] = jnp.zeros_like(down_acc)
        if entering:
            pad_s[...] = jnp.zeros_like(pad_s)

    hidden_width = up_ref.shape[1]
    step = 512
    gain = gain_of(up_ref, width)
    for g in range(images):
        if entering:
            live = step_id * images + g < ids_ref[2]
            came = jnp.where(ids_ref[0] == 0, came_ref[g].astype(F32), own_ref[g].astype(F32))
            pad_s[:length, :] = jnp.where(live, came, 0.0)
            cot_s[g * rows:(g + 1) * rows, :] = pad_s[...].astype(BF)
        else:
            cot_s[g * rows:(g + 1) * rows, :] = cot_ref[g]
        if not entry_ready:
            normed, _ = norm_rows(mid_ref[g])
            entry_s[g * rows:(g + 1) * rows, :] = (normed * gain).astype(BF)
    for at in range(0, hidden_width, step):
        tile = slice(at, at + step)
        grad_act = dot_nt(cot_s[...], down_ref[tile, :])
        slope = slope_ref[:, :, tile].reshape(images * rows, step)
        gh_s[:, tile] = (grad_act * slope.astype(F32)).astype(BF)
    down_acc[...] += dot_tn(cot_s[...], act_ref[...].reshape(images * rows, hidden_width))
    up_acc[...] += dot_tn(entry_s[...], gh_s[...])
    grad_entry = dot_nt(gh_s[...], up_ref[:width, :])
    for g in range(images):
        normed, scale = norm_rows(mid_ref[g])
        back = norm_rows_back(grad_entry[g * rows:(g + 1) * rows] * gain, normed, scale)
        gmid_ref[g] = cot_s[g * rows:(g + 1) * rows, :].astype(F32) + back

    @pl.when(step_id == pl.num_programs(0) - 1)
    def _():
        depth = width // count
        tall = hidden_width // count
        for section in range(2):
            @pl.when(ids_ref[0] == section)
            def _():
                for k in range(count):
                    shard = ids_ref[1] ^ k
                    at = pl.ds(pl.multiple_of(shard * depth, depth), depth)
                    up_out, down_out = (keep_ref, send_ref) if section == 0 else (send_ref, keep_ref)
                    for b in range(hidden_width // width):
                        up_out[k, b * depth:(b + 1) * depth, :] = up_acc[at, b * width:(b + 1) * width].astype(BF)
                    for j in range(0, tall, 128):
                        lanes = pl.ds(pl.multiple_of(shard * tall + j, 128), 128)
                        down_out[k, j:j + 128, :] = down_acc[:, lanes].T.astype(BF)


def attn_bwd_kernel(length, count, leaving, carried, final, ids_ref, gmid_ref, x_ref, qkv_ref, probs_ref, mixed_ref,
                    weight_ref, *refs):
    if carried:
        begun_ref, *refs = refs
    if final:
        gx_ref, keep_ref, send_ref, acc, *refs = refs
    else:
        gx_ref, acc, *refs = refs
    joint_s, entry_s, low_s, grad_mixed_s = refs
    images, rows, width = x_ref.shape
    step_id = pl.program_id(0)

    @pl.when(step_id == 0)
    def _():
        acc[...] = begun_ref[...] if carried else jnp.zeros_like(acc)

    lane = lax.broadcasted_iota(jnp.int32, (rows, PAIR), 1)
    gain = gain_of(weight_ref, width)
    head_of = (lax.broadcasted_iota(jnp.int32, (8, width), 1) // HEAD_DIM
               == lax.broadcasted_iota(jnp.int32, (8, width), 0)).astype(BF)
    for g in range(images):
        low_s[g * rows:(g + 1) * rows, :] = gmid_ref[g].astype(BF)
        normed, _ = norm_rows(x_ref[g].astype(F32))
        entry_s[g * rows:(g + 1) * rows, :] = (normed * gain).astype(BF)
    acc[:, 3 * width:] += dot_tn(mixed_ref[...].reshape(images * rows, width), low_s[...])
    grad_mixed_s[...] = dot_nt(low_s[...], weight_ref[:width, 3 * width:]).astype(BF)
    for g in range(images):
        own_rows = slice(g * rows, (g + 1) * rows)
        product = (grad_mixed_s[own_rows, :].astype(F32) * mixed_ref[g].astype(F32)).astype(BF)
        deltas = dot_nt(head_of, product)
        for pair in range(HEADS // 2):
            at = pair * PAIR
            q = qkv_ref[g, :, at:at + PAIR] * 0.125
            k = qkv_ref[g, :, width + at:width + at + PAIR]
            v = qkv_ref[g, :, 2 * width + at:2 * width + at + PAIR]
            k_t = (k * 0.125).T
            gm = grad_mixed_s[own_rows, at:at + PAIR]
            grad_k = None
            grad_v = None
            grad_q_t = []
            for side in range(2):
                head = pair * 2 + side
                own = (lane // HEAD_DIM) == side
                gm_own = jnp.where(own, gm, jnp.zeros_like(gm))
                q_own = jnp.where(own, q, jnp.zeros_like(q))
                probs = probs_ref[g, head]
                grad_probs = dot_nt(v, gm_own)
                grad_scores = (probs.astype(F32) * (grad_probs - deltas[head:head + 1])).astype(BF)
                part_v = dot_nn(probs, gm_own)
                part_k = dot_nn(grad_scores, q_own)
                grad_v = part_v if grad_v is None else grad_v + part_v
                grad_k = part_k if grad_k is None else grad_k + part_k
                grad_q_t.append(dot_nn(k_t[side * HEAD_DIM:(side + 1) * HEAD_DIM], grad_scores))
            joint_s[own_rows, at:at + PAIR] = jnp.concatenate(grad_q_t, axis=0).astype(BF).T
            joint_s[own_rows, width + at:width + at + PAIR] = grad_k.astype(BF)
            joint_s[own_rows, 2 * width + at:2 * width + at + PAIR] = grad_v.astype(BF)
    acc[:, :3 * width] += dot_tn(entry_s[...], joint_s[...])
    grad_entry = dot_nt(joint_s[...], weight_ref[:width, :3 * width])
    for g in range(images):
        normed, scale = norm_rows(x_ref[g].astype(F32))
        grad_x = gmid_ref[g] + norm_rows_back(grad_entry[g * rows:(g + 1) * rows] * gain, normed, scale)
        gx_ref[g] = (grad_x[:length] if leaving else grad_x).astype(BF)

    if not final:
        return

    @pl.when(step_id == pl.num_programs(0) - 1)
    def _():
        depth = width // count
        for section in range(2):
            @pl.when(ids_ref[0] == section)
            def _():
                for k in range(count):
                    at = pl.ds(pl.multiple_of((ids_ref[1] ^ k) * depth, depth), depth)
                    for half, out_ref in ((section, keep_ref), (1 - section, send_ref)):
                        for b in range(2):
                            lanes = (2 * half + b) * width
                            out_ref[k, b * depth:(b + 1) * depth, :] = acc[at, lanes:lanes + width].astype(BF)


def call(body, name, ids, images, entering, streams, fixed, stream_outs, fixed_outs, scratch, flops, start=0):
    g = PER_STEP if images % PER_STEP == 0 else 1

    def entering_spec(shape):
        return pl.BlockSpec((g,) + shape[1:], lambda i, ids: (ids[0] * (images // g) + i,) + (0,) * (len(shape) - 1))

    def per_image(shape, at=0):
        return pl.BlockSpec((g,) + shape[1:], lambda i, ids: (i + at // g,) + (0,) * (len(shape) - 1))

    def whole(shape):
        return pl.BlockSpec(shape, lambda i, ids: (0,) * len(shape))

    outs = [jax.ShapeDtypeStruct(s, d) for s, d in stream_outs + fixed_outs]
    moved = sum(a.size * a.dtype.itemsize for a in list(streams) + list(fixed) + outs)
    return pl.pallas_call(
        body,
        name=name,
        grid_spec=pltpu.PrefetchScalarGridSpec(
            num_scalar_prefetch=1,
            grid=(images // g,),
            in_specs=[entering_spec(a.shape) for a in entering] + [per_image(a.shape, start) for a in streams]
            + [whole(a.shape) for a in fixed],
            out_specs=[per_image(s) for s, _ in stream_outs] + [whole(s) for s, _ in fixed_outs],
            scratch_shapes=scratch(g),
        ),
        out_shape=outs,
        compiler_params=pltpu.CompilerParams(vmem_limit_bytes=VMEM_LIMIT, dimension_semantics=("arbitrary",)),
        cost_estimate=pl.CostEstimate(flops=int(flops), bytes_accessed=int(moved), transcendentals=0),
    )(ids, *entering, *streams, *fixed)


def attn_fwd(ids, x, pieces, dims, entering):
    n, rows, length, width, ff = dims
    count = len(pieces) // 2
    outs = [((n, rows, 3 * width), BF), ((n, HEADS, rows, rows), BF), ((n, rows, width), BF), ((n, rows, width), F32)]
    fixed_outs = [((width + GAIN_ROWS, 4 * width), BF)]
    body = functools.partial(attn_fwd_kernel, length, count, entering)

    def scratch(g):
        refs = [pltpu.VMEM((g * rows, width), BF), pltpu.VMEM((g * rows, 3 * width), BF),
                pltpu.VMEM((g * HEADS, rows, -(-rows // 128) * 128), F32)]
        return refs + ([pltpu.VMEM((g, rows, width), F32)] if entering else [])

    flops = 2 * n * rows * width * 4 * width + 4 * n * rows * rows * width
    if entering:
        def reordered(ids_ref, *refs):
            ins, rest = refs[:2 + 2 * count], refs[2 + 2 * count:]
            qkv, probs, mixed, mid, xp, weight, *scr = rest
            body(ids_ref, *ins, qkv, probs, mixed, mid, weight, xp, *scr)
        return call(reordered, "attention_forward", ids, n, x, [], pieces, outs + [((n, rows, width), BF)], fixed_outs,
                    scratch, flops)
    qkv, probs, mixed, mid, weight = call(body, "attention_forward", ids, n, [], [x], pieces, outs, fixed_outs, scratch, flops)
    return qkv, probs, mixed, mid, x, weight


def mlp_fwd(ids, mid, pieces, dims, leaving):
    n, rows, length, width, ff = dims
    count = len(pieces) // 2
    return call(
        functools.partial(mlp_fwd_kernel, length, count, leaving), "mlp_forward", ids, n, [], [mid], pieces,
        [((n, length if leaving else rows, width), BF), ((n, rows, ff), BF), ((n, rows, ff), BF)],
        [((width + GAIN_ROWS, ff), BF), ((ff, width), BF)],
        lambda g: [pltpu.VMEM((g * rows, width), BF), pltpu.VMEM((g * rows, ff), BF)],
        4 * n * rows * width * ff)


def mlp_bwd(ids, cot, mid, act, slope, up, down, dims, count, entering):
    n, rows, length, width, ff = dims

    def scratch(g):
        refs = [pltpu.VMEM((width, ff), F32), pltpu.VMEM((width, ff), F32), pltpu.VMEM((g * rows, width), BF),
                pltpu.VMEM((g * rows, width), BF), pltpu.VMEM((g * rows, ff), BF)]
        return refs + ([pltpu.VMEM((rows, width), F32)] if entering else [])

    half = (count, ff // count, width)
    return call(
        functools.partial(mlp_bwd_kernel, length, count, entering, False), "mlp_backward", ids, n,
        cot if entering else [], ([] if entering else [cot]) + [mid, act, slope], [up, down],
        [((n, rows, width), F32)], [(half, BF), (half, BF)], scratch, 8 * n * rows * width * ff)


def attn_bwd(ids, streams, weight, dims, count, leaving, span, begun=None, final=True):
    n, rows, length, width, ff = dims
    low, high = span
    half = (count, 2 * width // count, width)
    acc = ((width, 4 * width), F32)
    return call(
        functools.partial(attn_bwd_kernel, length, count, leaving, begun is not None, final), "attention_backward",
        ids, high - low, [], streams, [weight] + ([] if begun is None else [begun]),
        [((high - low, length if leaving else rows, width), BF)], [(half, BF), (half, BF)] if final else [acc],
        lambda g: ([pltpu.VMEM(*acc)] if final else []) + [pltpu.VMEM((g * rows, 3 * width), BF)]
        + [pltpu.VMEM((g * rows, width), BF)] * 3,
        (high - low) * (4 * rows * width * 4 * width + 10 * rows * rows * width), start=low)


def middle_kernel(length, count, ids_ref, own_ref, came_ref, x_ref, *refs):
    attn, mlp, refs = refs[:2 * count], refs[2 * count:4 * count], refs[4 * count:]
    qkv_ref, probs_ref, mixed_ref, out_ref, gmid_ref, weight_ref, keep_ref, send_ref, *refs = refs
    entry_s, qkv_s, scores_s, mid_s, act_s, slope_s, up_s, down_s, up_acc, down_acc, cot_s, gh_s, pad_s = refs
    attn_fwd_kernel(length, count, False, ids_ref, x_ref, *attn, qkv_ref, probs_ref, mixed_ref, mid_s, weight_ref,
                    entry_s, qkv_s, scores_s)
    mlp_fwd_kernel(length, count, True, ids_ref, mid_s, *mlp, out_ref, act_s, slope_s, up_s, down_s, entry_s, gh_s)
    mlp_bwd_kernel(length, count, True, True, ids_ref, own_ref, came_ref, mid_s, act_s, slope_s, up_s, down_s, gmid_ref,
                   keep_ref, send_ref, up_acc, down_acc, entry_s, cot_s, gh_s, pad_s)


def middle(ids, cots, x, attn, mlp, dims):
    n, rows, length, width, ff = dims
    count = len(attn) // 2
    half = (count, ff // count, width)

    def scratch(g):
        tokens = g * rows
        return [pltpu.VMEM((tokens, width), BF), pltpu.VMEM((tokens, 3 * width), BF),
                pltpu.VMEM((g * HEADS, rows, -(-rows // 128) * 128), F32), pltpu.VMEM((g, rows, width), F32),
                pltpu.VMEM((g, rows, ff), BF), pltpu.VMEM((g, rows, ff), BF), pltpu.VMEM((width + GAIN_ROWS, ff), BF),
                pltpu.VMEM((ff, width), BF), pltpu.VMEM((width, ff), F32), pltpu.VMEM((width, ff), F32),
                pltpu.VMEM((tokens, width), BF), pltpu.VMEM((tokens, ff), BF), pltpu.VMEM((rows, width), F32)]

    return call(
        functools.partial(middle_kernel, length, count), "middle", ids, n, cots, [x], attn + mlp,
        [((n, rows, 3 * width), BF), ((n, HEADS, rows, rows), BF), ((n, rows, width), BF), ((n, length, width), BF),
         ((n, rows, width), F32)],
        [((width + GAIN_ROWS, 4 * width), BF), (half, BF), (half, BF)], scratch,
        n * rows * width * (8 * width + 12 * ff + 4 * rows))


def swap_section(value):
    return lax.ppermute(value, "section", [(0, 1), (1, 0)])


def pick(stack, index):
    return lax.dynamic_index_in_dim(stack, index, 0, keepdims=False)


def tie(*values):
    return lax.optimization_barrier(values)


def exchange(values, axis):
    size = lax.axis_size(axis)
    return [lax.ppermute(v, axis, [(i, i ^ (k + 1)) for i in range(size)]) for k, v in enumerate(values)]


def direct(size):
    return size & (size - 1) == 0 and size <= MOST_PIECES


def total(first, others):
    result = first.astype(F32)
    for other in others:
        result = result + other.astype(F32)
    return result.astype(BF)


def local(ends_in, live, gain_attn, w_qkv, w_out, gain_mlp, w_up, w_down):
    me = lax.axis_index("section")
    mine_at = lax.axis_index("fsdp")
    first = me == 0
    shards = lax.axis_size("fsdp")
    replicas = lax.axis_size("replica")
    slots, length, width = ends_in.shape[1:]
    share = slots // 2
    rows = -(-length // 16) * 16
    depth = w_qkv.shape[1]
    ff = w_up.shape[2]
    ratio = ff // width
    dims = (share, rows, length, width, ff)
    packed = direct(shards) and depth % 16 == 0
    count = shards if packed else 1

    live_here = pick(live[:, 0], me)
    ids = jnp.stack([me, mine_at if packed else jnp.zeros_like(mine_at), live_here]).astype(jnp.int32)

    def columns(matrix):
        return matrix.reshape(depth, -1, width).transpose(1, 0, 2).reshape(-1, width)

    def halves(gain, first_half, second_half):
        row = lax.dynamic_update_slice(jnp.zeros((GAIN_ROWS, width), BF), gain, (0, mine_at * depth))
        return jnp.stack([jnp.concatenate([first_half, row]), jnp.concatenate([second_half, row])])

    qkv_own = columns(w_qkv[0])
    attn_own = halves(gain_attn, qkv_own[:2 * depth], jnp.concatenate([qkv_own[2 * depth:], w_out[0]]))
    mlp_own = halves(gain_mlp, columns(w_up[0]), w_down[0])

    def by_layer(own):
        kept, came = pick(own, me), swap_section(pick(own, 1 - me))
        return jnp.where(first, kept, came), jnp.where(first, came, kept)

    def spread(half, mlp):
        if packed:
            return [half] + exchange([half] * (shards - 1), "fsdp")
        full = lax.all_gather(half, "fsdp")
        gains = jnp.sum(full[:, -GAIN_ROWS:].astype(F32), axis=0).astype(BF)
        full = full[:, :-GAIN_ROWS]
        blocks = full.reshape(shards, -1, depth, width).transpose(1, 0, 2, 3).reshape(-1, width)
        if mlp:
            blocks = jnp.where(first, blocks, full.reshape(-1, width))
        return [jnp.concatenate([blocks, gains])]

    attn0, attn1 = by_layer(attn_own)
    attn0 = spread(attn0, False)
    mlp0, mlp1 = by_layer(mlp_own)
    came_images = swap_section(ends_in[0])
    images = [ends_in[0], came_images]
    attn0 = attn0 + [swap_section(p) for p in attn0]

    *tied, attn1, mlp0 = tie(*attn0, attn1, mlp0)
    attn0 = tied
    mlp0 = spread(mlp0, True)
    attn1 = spread(attn1, False)
    qkv0, probs0, mixed0, mid0, x0, weight0 = attn_fwd(ids, images, attn0, dims, True)

    np_ = len(mlp0)
    mid0, mlp1, *tied = tie(mid0, mlp1, *mlp0, *attn1)
    mlp0, attn1 = tied[:np_], tied[np_:]
    mlp0 = mlp0 + [swap_section(p) for p in mlp0]
    mlp1 = spread(mlp1, True)
    attn1 = attn1 + [swap_section(p) for p in attn1]
    x1, act0, slope0, up0, down0 = mlp_fwd(ids, mid0, mlp0, dims, False)

    x1, *tied = tie(x1, *attn1, *mlp1)
    attn1, mlp1 = tied[:2 * np_], tied[2 * np_:]
    mlp1 = mlp1 + [swap_section(p) for p in mlp1]
    qkv1, probs1, mixed1, out, gmid1, weight1, keep_m1, send_m1 = middle(ids, images, x1, attn1, mlp1, dims)

    def scatter(half, came, mlp):
        if packed:
            parts = [total(half[k], [came[k]]) for k in range(count)]
            return [parts[0]] + exchange(parts[1:], "fsdp")
        chip = total(half, [came])
        blocks = chip.reshape(-1, shards, depth, width).transpose(1, 0, 2, 3).reshape(shards, -1, width)
        if mlp:
            blocks = jnp.where(first, blocks, chip.reshape(shards, -1, width))
        return [lax.psum_scatter(blocks, "fsdp", scatter_dimension=0)]

    def added(parts):
        return total(parts[0], parts[1:])

    two_phase = direct(replicas) and depth % 16 == 0
    at_z = lax.axis_index("replica")

    def sum_quarters(part):
        if not two_phase:
            return [lax.psum(part, "replica")]
        quarters = part.reshape(replicas, -1, width)
        return [pick(quarters, at_z)] + exchange([pick(quarters, at_z ^ k) for k in range(1, replicas)], "replica")

    def share_quarters(parts):
        if not two_phase:
            return parts
        mine = added(parts)
        return [mine] + exchange([mine] * (replicas - 1), "replica")

    def joined(pieces):
        if not two_phase:
            return pieces[0]
        full = jnp.zeros((replicas,) + pieces[0].shape, BF)
        for k, piece in enumerate(pieces):
            full = lax.dynamic_update_index_in_dim(full, piece, at_z ^ k, 0)
        return full.reshape(-1, width)

    def tied_lists(lists, *values):
        flat = tie(*values, *[member for group in lists for member in group])
        values, flat = flat[:len(values)], flat[len(values):]
        groups = []
        for group in lists:
            groups.append(list(flat[:len(group)]))
            flat = flat[len(group):]
        return groups, values

    came_m1 = swap_section(send_m1)
    came_out = swap_section(out)
    cot0, keep_a1, send_a1 = attn_bwd(ids, [gmid1, x1, qkv1, probs1, mixed1], weight1, dims, count, False, (0, share))

    cot0, came_m1, keep_m1, came_out = tie(cot0, came_m1, keep_m1, came_out)
    m1 = scatter(keep_m1, came_m1, True)
    came_a1 = swap_section(send_a1)
    gmid0, keep_m0, send_m0 = mlp_bwd(ids, cot0, mid0, act0, slope0, up0, down0, dims, count, False)

    (m1,), (gmid0, came_a1, keep_a1) = tied_lists([m1], gmid0, came_a1, keep_a1)
    m1 = sum_quarters(added(m1))
    a1 = scatter(keep_a1, came_a1, False)
    came_m0 = swap_section(send_m0)
    early = (share // 2 + 1) // PER_STEP * PER_STEP
    saved = [gmid0, x0, qkv0, probs0, mixed0]
    gx_early, begun = attn_bwd(ids, saved, weight0, dims, count, True, (0, early), final=False)

    (m1, a1), (begun, gx_early, came_m0, keep_m0) = tied_lists([m1, a1], begun, gx_early, came_m0, keep_m0)
    m0 = scatter(keep_m0, came_m0, True)
    m1 = share_quarters(m1)
    a1 = sum_quarters(added(a1))
    came_gx_early = swap_section(gx_early)
    gx_late, keep_a0, send_a0 = attn_bwd(ids, saved, weight0, dims, count, True, (early, share), begun)

    (m1, a1, m0), (send_a0, keep_a0, gx_late, came_gx_early) = tied_lists([m1, a1, m0], send_a0, keep_a0, gx_late, came_gx_early)
    came_a0 = swap_section(send_a0)
    m0 = sum_quarters(added(m0))
    a1 = share_quarters(a1)
    a0 = scatter(keep_a0, came_a0, False)
    (m0, a0), (a1[0],) = tied_lists([m0, a0], a1[0])
    a0 = sum_quarters(added(a0))
    m0 = share_quarters(m0)
    came_gx_late = swap_section(gx_late)
    (m0, a0), _ = tied_lists([m0, a0])
    a0 = share_quarters(a0)
    gx = jnp.concatenate([gx_early, gx_late])
    came_gx = jnp.concatenate([came_gx_early, came_gx_late])

    def own_layer(parts0, parts1):
        sum0, sum1 = joined(parts0), joined(parts1)
        mine = jnp.where(first, sum0, sum1)
        other = swap_section(jnp.where(first, sum1, sum0))
        return jnp.concatenate([jnp.where(first, mine, other), jnp.where(first, other, mine)]).astype(F32)

    mlp_grad = own_layer(m0, m1)
    attn_grad = own_layer(a0, a1)

    def rows_of(blocks):
        return blocks.reshape(-1, depth, width).transpose(1, 0, 2).reshape(depth, -1)

    grad_qkv, grad_out = rows_of(attn_grad[:3 * depth])[None], attn_grad[3 * depth:][None]
    grad_up, grad_down = rows_of(mlp_grad[:ratio * depth])[None], mlp_grad[ratio * depth:][None]
    grad_gain_attn = jnp.sum(grad_qkv * w_qkv.astype(F32), axis=-1) / gain_attn.astype(F32)
    grad_gain_mlp = jnp.sum(grad_up * w_up.astype(F32), axis=-1) / gain_mlp.astype(F32)

    own = jnp.where(first, gx, out)
    came = jnp.where(first, came_gx, came_out)
    ends_out = jnp.where(first, jnp.concatenate([own, came]), jnp.concatenate([came, own]))
    return (ends_out[None], grad_gain_attn, grad_qkv, grad_out, grad_gain_mlp, grad_up, grad_down)


def solution(mesh):
    in_specs = (
        P("section", ("fsdp", "replica"), None, None),
        P(None, ("fsdp", "replica")),
        P("section", "fsdp"),
        P("section", "fsdp", None),
        P("section", "fsdp", None),
        P("section", "fsdp"),
        P("section", "fsdp", None),
        P("section", "fsdp", None),
    )
    out_specs = (
        P("section", ("fsdp", "replica"), None, None),
        P("section", "fsdp"),
        P("section", "fsdp", None),
        P("section", "fsdp", None),
        P("section", "fsdp"),
        P("section", "fsdp", None),
        P("section", "fsdp", None),
    )
    return jax.shard_map(local, mesh=mesh, in_specs=in_specs, out_specs=out_specs, check_vma=False)
```

```python
import functools

import jax
import jax.numpy as jnp
from jax import lax
from jax.experimental import pallas as pl
from jax.experimental.pallas import tpu as pltpu
from jax.sharding import PartitionSpec as P

HEADS = 6
HEAD_DIM = 64
PAIR = 2 * HEAD_DIM
EPS = 1e-06
BF = jnp.bfloat16
F32 = jnp.float32
VMEM_LIMIT = 56 * 1024 * 1024
PER_STEP = 2
MIDDLE_STEP = 2
GAIN_ROWS = 16
MOST_PIECES = 8


def dot_nn(a, b):
    return lax.dot_general(a, b, (((1,), (0,)), ((), ())), preferred_element_type=F32)


def dot_nt(a, b):
    return lax.dot_general(a, b, (((1,), (1,)), ((), ())), preferred_element_type=F32)


def dot_tn(a, b):
    return lax.dot_general(a, b, (((0,), (0,)), ((), ())), preferred_element_type=F32)


def norm_rows(values):
    centered = values - jnp.mean(values, axis=-1, keepdims=True)
    scale = lax.rsqrt(jnp.mean(centered * centered, axis=-1, keepdims=True) + EPS)
    return centered * scale, scale


def norm_rows_back(grad_normed, normed, scale):
    first = jnp.mean(grad_normed, axis=-1, keepdims=True)
    second = jnp.mean(grad_normed * normed, axis=-1, keepdims=True)
    return scale * (grad_normed - first - normed * second)


def gelu_both(v):
    cdf = 0.5 * (1.0 + lax.erf(v * 0.7071067811865476))
    density = jnp.exp(-0.5 * v * v) * 0.3989422804014327
    return v * cdf, cdf + v * density


def gain_of(weight_ref, width):
    return weight_ref[width:width + GAIN_ROWS, :width].astype(F32)[:1]


def place_gain(pieces, weight_ref, width):
    last = pieces[0].shape[0] - GAIN_ROWS
    rows = sum(piece[last:last + GAIN_ROWS, :].astype(F32) for piece in pieces)
    weight_ref[width:width + GAIN_ROWS, :width] = rows.astype(BF)


def place_attn(ids_ref, pieces, weight_ref):
    count = len(pieces) // 2
    width = weight_ref.shape[1] // 4
    place_gain(pieces[:count], weight_ref, width)
    depth = width // count
    for section in range(2):
        @pl.when(ids_ref[0] == section)
        def _():
            for k in range(count):
                at = pl.ds(pl.multiple_of((ids_ref[1] ^ k) * depth, depth), depth)
                for half, piece in ((section, pieces[k]), (1 - section, pieces[count + k])):
                    for b in range(2):
                        lanes = (2 * half + b) * width
                        weight_ref[at, lanes:lanes + width] = piece[b * depth:(b + 1) * depth, :]


def place_mlp(ids_ref, pieces, up_ref, down_ref):
    count = len(pieces) // 2
    hidden, width = down_ref.shape
    place_gain(pieces[:count], up_ref, width)
    depth = width // count
    tall = hidden // count
    for section in range(2):
        @pl.when(ids_ref[0] == section)
        def _():
            for k in range(count):
                shard = ids_ref[1] ^ k
                at = pl.ds(pl.multiple_of(shard * depth, depth), depth)
                for half, piece in ((section, pieces[k]), (1 - section, pieces[count + k])):
                    if half == 0:
                        for b in range(hidden // width):
                            up_ref[at, b * width:(b + 1) * width] = piece[b * depth:(b + 1) * depth, :]
                    else:
                        down_ref[pl.ds(pl.multiple_of(shard * tall, tall), tall), :] = piece[:tall, :]


def attn_fwd_kernel(length, count, entering, ids_ref, *refs):
    if entering:
        own_ref, came_ref = refs[:2]
        pieces, refs = refs[2:2 + 2 * count], refs[2 + 2 * count:]
        qkv_ref, probs_ref, mixed_ref, mid_ref, weight_ref, x_ref, entry_s, qkv_s, scores_s, pad_s = refs
    else:
        x_ref = refs[0]
        pieces, refs = refs[1:1 + 2 * count], refs[1 + 2 * count:]
        qkv_ref, probs_ref, mixed_ref, mid_ref, weight_ref, entry_s, qkv_s, scores_s = refs
    images, rows, width = x_ref.shape

    @pl.when(pl.program_id(0) == 0)
    def _():
        place_attn(ids_ref, pieces, weight_ref)
        if entering:
            pad_s[...] = jnp.zeros_like(pad_s)

    gain = gain_of(weight_ref, width)
    for g in range(images):
        if entering:
            pad_s[g, :length, :] = jnp.where(ids_ref[0] == 0, own_ref[g].astype(F32), came_ref[g].astype(F32))
            values = pad_s[g]
            x_ref[g] = values.astype(BF)
        else:
            values = x_ref[g].astype(F32)
        normed, _ = norm_rows(values)
        entry_s[g * rows:(g + 1) * rows, :] = (normed * gain).astype(BF)
    qkv_s[...] = dot_nn(entry_s[...], weight_ref[:width, :3 * width]).astype(BF)
    lane = lax.broadcasted_iota(jnp.int32, (rows, PAIR), 1)
    cut = (length // 8) * 8

    def fill_scores(g):
        own_rows = slice(g * rows, (g + 1) * rows)
        for head in range(HEADS):
            at = head // 2 * PAIR
            q = qkv_s[own_rows, at:at + PAIR] * 0.125
            q = jnp.where((lane // HEAD_DIM) == head % 2, q, jnp.zeros_like(q))
            scores_s[g * HEADS + head, :, :rows] = dot_nt(qkv_s[own_rows, width + at:width + at + PAIR], q)

    def fill_probs(g):
        for head in range(HEADS):
            for lo in range(0, rows, 128):
                hi = min(lo + 128, rows)
                scores = scores_s[g * HEADS + head, :, lo:hi]
                tail_row = lax.broadcasted_iota(jnp.int32, (rows - cut, hi - lo), 0) + cut
                scores = jnp.concatenate([scores[:cut], jnp.where(tail_row < length, scores[cut:], -1e30)], axis=0)
                parts = jnp.exp(scores - jnp.max(scores, axis=0, keepdims=True))
                inv = 1.0 / jnp.sum(parts, axis=0, keepdims=True)
                probs_ref[g, head, :, lo:hi] = (parts * inv).astype(BF)

    def fill_mixed(g):
        own_rows = slice(g * rows, (g + 1) * rows)
        for pair in range(HEADS // 2):
            at = pair * PAIR
            v_t = qkv_s[own_rows, 2 * width + at:2 * width + at + PAIR].T
            mixed = [dot_nn(v_t[side * HEAD_DIM:(side + 1) * HEAD_DIM], probs_ref[g, pair * 2 + side]) for side in range(2)]
            mixed_ref[g, :, at:at + PAIR] = jnp.concatenate(mixed, axis=0).astype(BF).T

    fill_scores(0)
    for g in range(images):
        qkv_ref[g] = qkv_s[g * rows:(g + 1) * rows, :]
        if g + 1 < images:
            fill_scores(g + 1)
        fill_probs(g)
        fill_mixed(g)
    added = dot_nn(mixed_ref[...].reshape(images * rows, width), weight_ref[:width, 3 * width:])
    for g in range(images):
        mid_ref[g] = x_ref[g].astype(F32) + added[g * rows:(g + 1) * rows]


def rows_at(pieces, low, high):
    return [piece.at[low:high, :] for piece in pieces]


def mlp_fwd_kernel(length, count, leaving, ids_ref, mid_ref, *refs):
    pieces, refs = refs[:2 * count], refs[2 * count:]
    pieces = rows_at(pieces, 0, refs[4].shape[0] // count + GAIN_ROWS)
    out_ref, act_ref, slope_ref, up_ref, down_ref, entry_s, act_s = refs
    images, rows, width = mid_ref.shape
    hidden_width = up_ref.shape[1]

    @pl.when(pl.program_id(0) == 0)
    def _():
        place_mlp(ids_ref, pieces, up_ref, down_ref)

    gain = gain_of(up_ref, width)
    for g in range(images):
        normed, _ = norm_rows(mid_ref[g])
        entry_s[g * rows:(g + 1) * rows, :] = (normed * gain).astype(BF)
    step = 256
    for at in range(0, hidden_width, step):
        hidden = dot_nn(entry_s[...], up_ref[:width, at:at + step])
        act, slope = gelu_both(hidden)
        act_s[:, at:at + step] = act.astype(BF)
        for g in range(images):
            slope_ref[g, :, at:at + step] = slope[g * rows:(g + 1) * rows].astype(BF)
    added = dot_nn(act_s[...], down_ref[...])
    for g in range(images):
        act_ref[g] = act_s[g * rows:(g + 1) * rows, :]
        out = mid_ref[g] + added[g * rows:(g + 1) * rows]
        if leaving:
            live = pl.program_id(0) * images + g < ids_ref[2]
            out_ref[g] = jnp.where(live, out[:length], 0.0).astype(BF)
        else:
            out_ref[g] = out.astype(BF)


def mlp_bwd_kernel(length, count, entering, entry_ready, ids_ref, *refs):
    if entering:
        own_ref, came_ref, *refs = refs
        *refs, pad_s = refs
    else:
        cot_ref, *refs = refs
    mid_ref, act_ref, slope_ref, up_ref, down_ref, gmid_ref, keep_ref, send_ref, *refs = refs
    up_acc, down_acc, entry_s, cot_s, gh_s = refs
    images, rows, width = mid_ref.shape
    step_id = pl.program_id(0)

    @pl.when(step_id == 0)
    def _():
        up_acc[...] = jnp.zeros_like(up_acc)
        down_acc[...] = jnp.zeros_like(down_acc)
        if entering:
            pad_s[...] = jnp.zeros_like(pad_s)

    hidden_width = up_ref.shape[1]
    step = 512
    gain = gain_of(up_ref, width)
    for g in range(images):
        if entering:
            live = step_id * images + g < ids_ref[2]
            came = jnp.where(ids_ref[0] == 0, came_ref[g].astype(F32), own_ref[g].astype(F32))
            pad_s[:length, :] = jnp.where(live, came, 0.0)
            cot_s[g * rows:(g + 1) * rows, :] = pad_s[...].astype(BF)
        else:
            cot_s[g * rows:(g + 1) * rows, :] = cot_ref[g]
        if not entry_ready:
            normed, _ = norm_rows(mid_ref[g])
            entry_s[g * rows:(g + 1) * rows, :] = (normed * gain).astype(BF)
    for at in range(0, hidden_width, step):
        tile = slice(at, at + step)
        grad_act = dot_nt(cot_s[...], down_ref[tile, :])
        slope = slope_ref[:, :, tile].reshape(images * rows, step)
        gh_s[:, tile] = (grad_act * slope.astype(F32)).astype(BF)
    down_acc[...] += dot_tn(cot_s[...], act_ref[...].reshape(images * rows, hidden_width))
    up_acc[...] += dot_tn(entry_s[...], gh_s[...])
    grad_entry = dot_nt(gh_s[...], up_ref[:width, :])
    for g in range(images):
        normed, scale = norm_rows(mid_ref[g])
        back = norm_rows_back(grad_entry[g * rows:(g + 1) * rows] * gain, normed, scale)
        gmid_ref[g] = cot_s[g * rows:(g + 1) * rows, :].astype(F32) + back

    @pl.when(step_id == pl.num_programs(0) - 1)
    def _():
        depth = width // count
        tall = hidden_width // count
        for section in range(2):
            @pl.when(ids_ref[0] == section)
            def _():
                for k in range(count):
                    shard = ids_ref[1] ^ k
                    at = pl.ds(pl.multiple_of(shard * depth, depth), depth)
                    up_out, down_out = (keep_ref, send_ref) if section == 0 else (send_ref, keep_ref)
                    for b in range(hidden_width // width):
                        up_out[k, b * depth:(b + 1) * depth, :] = up_acc[at, b * width:(b + 1) * width].astype(BF)
                    for j in range(0, tall, 128):
                        lanes = pl.ds(pl.multiple_of(shard * tall + j, 128), 128)
                        down_out[k, j:j + 128, :] = down_acc[:, lanes].T.astype(BF)


def attn_bwd_kernel(length, count, leaving, carried, final, ids_ref, gmid_ref, x_ref, qkv_ref, probs_ref, mixed_ref,
                    weight_ref, *refs, entry_ready=False):
    if carried:
        begun_ref, *refs = refs
    if final:
        gx_ref, keep_ref, send_ref, acc, *refs = refs
    else:
        gx_ref, acc, *refs = refs
    joint_s, entry_s, low_s, grad_mixed_s = refs
    images, rows, width = x_ref.shape
    step_id = pl.program_id(0)

    @pl.when(step_id == 0)
    def _():
        acc[...] = begun_ref[...] if carried else jnp.zeros_like(acc)

    lane = lax.broadcasted_iota(jnp.int32, (rows, PAIR), 1)
    gain = gain_of(weight_ref, width)
    head_of = (lax.broadcasted_iota(jnp.int32, (8, width), 1) // HEAD_DIM
               == lax.broadcasted_iota(jnp.int32, (8, width), 0)).astype(BF)
    for g in range(images):
        low_s[g * rows:(g + 1) * rows, :] = gmid_ref[g].astype(BF)
        if not entry_ready:
            normed, _ = norm_rows(x_ref[g].astype(F32))
            entry_s[g * rows:(g + 1) * rows, :] = (normed * gain).astype(BF)
    acc[:, 3 * width:] += dot_tn(mixed_ref[...].reshape(images * rows, width), low_s[...])
    grad_mixed_s[...] = dot_nt(low_s[...], weight_ref[:width, 3 * width:]).astype(BF)
    for g in range(images):
        own_rows = slice(g * rows, (g + 1) * rows)
        product = (grad_mixed_s[own_rows, :].astype(F32) * mixed_ref[g].astype(F32)).astype(BF)
        deltas = dot_nt(head_of, product)
        for pair in range(HEADS // 2):
            at = pair * PAIR
            q = qkv_ref[g, :, at:at + PAIR] * 0.125
            k = qkv_ref[g, :, width + at:width + at + PAIR]
            v = qkv_ref[g, :, 2 * width + at:2 * width + at + PAIR]
            k_t = (k * 0.125).T
            gm = grad_mixed_s[own_rows, at:at + PAIR]
            grad_k = None
            grad_v = None
            grad_q_t = []
            for side in range(2):
                head = pair * 2 + side
                own = (lane // HEAD_DIM) == side
                gm_own = jnp.where(own, gm, jnp.zeros_like(gm))
                q_own = jnp.where(own, q, jnp.zeros_like(q))
                probs = probs_ref[g, head]
                grad_probs = dot_nt(v, gm_own)
                grad_scores = (probs.astype(F32) * (grad_probs - deltas[head:head + 1])).astype(BF)
                part_v = dot_nn(probs, gm_own)
                part_k = dot_nn(grad_scores, q_own)
                grad_v = part_v if grad_v is None else grad_v + part_v
                grad_k = part_k if grad_k is None else grad_k + part_k
                grad_q_t.append(dot_nn(k_t[side * HEAD_DIM:(side + 1) * HEAD_DIM], grad_scores))
            joint_s[own_rows, at:at + PAIR] = jnp.concatenate(grad_q_t, axis=0).astype(BF).T
            joint_s[own_rows, width + at:width + at + PAIR] = grad_k.astype(BF)
            joint_s[own_rows, 2 * width + at:2 * width + at + PAIR] = grad_v.astype(BF)
    acc[:, :3 * width] += dot_tn(entry_s[...], joint_s[...])
    grad_entry = dot_nt(joint_s[...], weight_ref[:width, :3 * width])
    for g in range(images):
        normed, scale = norm_rows(x_ref[g].astype(F32))
        grad_x = gmid_ref[g] + norm_rows_back(grad_entry[g * rows:(g + 1) * rows] * gain, normed, scale)
        gx_ref[g] = (grad_x[:length] if leaving else grad_x).astype(BF)

    if not final:
        return

    @pl.when(step_id == pl.num_programs(0) - 1)
    def _():
        depth = width // count
        for section in range(2):
            @pl.when(ids_ref[0] == section)
            def _():
                for k in range(count):
                    at = pl.ds(pl.multiple_of((ids_ref[1] ^ k) * depth, depth), depth)
                    for half, out_ref in ((section, keep_ref), (1 - section, send_ref)):
                        for b in range(2):
                            lanes = (2 * half + b) * width
                            out_ref[k, b * depth:(b + 1) * depth, :] = acc[at, lanes:lanes + width].astype(BF)


def call(body, name, ids, images, entering, streams, fixed, stream_outs, fixed_outs, scratch, flops, start=0, g=PER_STEP):
    g = g if images % g == 0 else 1

    def entering_spec(shape):
        return pl.BlockSpec((g,) + shape[1:], lambda i, ids: (ids[0] * (images // g) + i,) + (0,) * (len(shape) - 1))

    def per_image(shape, at=0):
        return pl.BlockSpec((g,) + shape[1:], lambda i, ids: (i + at // g,) + (0,) * (len(shape) - 1))

    def whole(shape):
        return pl.BlockSpec(shape, lambda i, ids: (0,) * len(shape))

    outs = [jax.ShapeDtypeStruct(s, d) for s, d in stream_outs + fixed_outs]
    moved = sum(a.size * a.dtype.itemsize for a in list(streams) + list(fixed) + outs)
    return pl.pallas_call(
        body,
        name=name,
        grid_spec=pltpu.PrefetchScalarGridSpec(
            num_scalar_prefetch=1,
            grid=(images // g,),
            in_specs=[entering_spec(a.shape) for a in entering] + [per_image(a.shape, start) for a in streams]
            + [whole(a.shape) for a in fixed],
            out_specs=[per_image(s) for s, _ in stream_outs] + [whole(s) for s, _ in fixed_outs],
            scratch_shapes=scratch(g),
        ),
        out_shape=outs,
        compiler_params=pltpu.CompilerParams(vmem_limit_bytes=VMEM_LIMIT, dimension_semantics=("arbitrary",)),
        cost_estimate=pl.CostEstimate(flops=int(flops), bytes_accessed=int(moved), transcendentals=0),
    )(ids, *entering, *streams, *fixed)


def attn_fwd(ids, x, pieces, dims, entering):
    n, rows, length, width, ff = dims
    count = len(pieces) // 2
    outs = [((n, rows, 3 * width), BF), ((n, HEADS, rows, rows), BF), ((n, rows, width), BF), ((n, rows, width), F32)]
    fixed_outs = [((width + GAIN_ROWS, 4 * width), BF)]
    body = functools.partial(attn_fwd_kernel, length, count, entering)

    def scratch(g):
        refs = [pltpu.VMEM((g * rows, width), BF), pltpu.VMEM((g * rows, 3 * width), BF),
                pltpu.VMEM((g * HEADS, rows, -(-rows // 128) * 128), F32)]
        return refs + ([pltpu.VMEM((g, rows, width), F32)] if entering else [])

    flops = 2 * n * rows * width * 4 * width + 4 * n * rows * rows * width
    if entering:
        def reordered(ids_ref, *refs):
            ins, rest = refs[:2 + 2 * count], refs[2 + 2 * count:]
            qkv, probs, mixed, mid, xp, weight, *scr = rest
            body(ids_ref, *ins, qkv, probs, mixed, mid, weight, xp, *scr)
        return call(reordered, "attention_forward", ids, n, x, [], pieces, outs + [((n, rows, width), BF)], fixed_outs,
                    scratch, flops)
    qkv, probs, mixed, mid, weight = call(body, "attention_forward", ids, n, [], [x], pieces, outs, fixed_outs, scratch, flops)
    return qkv, probs, mixed, mid, x, weight


def mlp_fwd(ids, mid, pieces, dims, leaving):
    n, rows, length, width, ff = dims
    count = len(pieces) // 2
    return call(
        functools.partial(mlp_fwd_kernel, length, count, leaving), "mlp_forward", ids, n, [], [mid], pieces,
        [((n, length if leaving else rows, width), BF), ((n, rows, ff), BF), ((n, rows, ff), BF)],
        [((width + GAIN_ROWS, ff), BF), ((ff, width), BF)],
        lambda g: [pltpu.VMEM((g * rows, width), BF), pltpu.VMEM((g * rows, ff), BF)],
        4 * n * rows * width * ff)


def mlp_bwd(ids, cot, mid, act, slope, up, down, dims, count, entering):
    n, rows, length, width, ff = dims

    def scratch(g):
        refs = [pltpu.VMEM((width, ff), F32), pltpu.VMEM((width, ff), F32), pltpu.VMEM((g * rows, width), BF),
                pltpu.VMEM((g * rows, width), BF), pltpu.VMEM((g * rows, ff), BF)]
        return refs + ([pltpu.VMEM((rows, width), F32)] if entering else [])

    half = (count, ff // count, width)
    return call(
        functools.partial(mlp_bwd_kernel, length, count, entering, False), "mlp_backward", ids, n,
        cot if entering else [], ([] if entering else [cot]) + [mid, act, slope], [up, down],
        [((n, rows, width), F32)], [(half, BF), (half, BF)], scratch, 8 * n * rows * width * ff)


def attn_bwd(ids, streams, weight, dims, count, leaving, span, begun=None, final=True):
    n, rows, length, width, ff = dims
    low, high = span
    half = (count, 2 * width // count, width)
    acc = ((width, 4 * width), F32)
    return call(
        functools.partial(attn_bwd_kernel, length, count, leaving, begun is not None, final), "attention_backward",
        ids, high - low, [], streams, [weight] + ([] if begun is None else [begun]),
        [((high - low, length if leaving else rows, width), BF)], [(half, BF), (half, BF)] if final else [acc],
        lambda g: ([pltpu.VMEM(*acc)] if final else []) + [pltpu.VMEM((g * rows, 3 * width), BF)]
        + [pltpu.VMEM((g * rows, width), BF)] * 3,
        (high - low) * (4 * rows * width * 4 * width + 10 * rows * rows * width), start=low)


def middle_kernel(length, count, ids_ref, own_ref, came_ref, x_ref, *refs):
    attn, mlp, refs = refs[:2 * count], refs[2 * count:4 * count], refs[4 * count:]
    out_ref, cot_ref, keep_m_ref, send_m_ref, keep_a_ref, send_a_ref, *refs = refs
    entry_s, qkv_s, scores_s, mid_s, act_s, slope_s, up_s, down_s, up_acc, down_acc, cot_s, gh_s, pad_s, *refs = refs
    qkv3_s, probs_s, mixed_s, weight_s, gmid_s, acc, joint_s, grad_mixed_s, entry_a_s = refs
    skip = down_s.shape[0] // count + GAIN_ROWS
    attn = rows_at(attn, skip, attn[0].shape[0])
    attn_fwd_kernel(length, count, False, ids_ref, x_ref, *attn, qkv3_s, probs_s, mixed_s, mid_s, weight_s,
                    entry_a_s, qkv_s, scores_s)
    mlp_fwd_kernel(length, count, True, ids_ref, mid_s, *mlp, out_ref, act_s, slope_s, up_s, down_s, entry_s, gh_s)
    mlp_bwd_kernel(length, count, True, True, ids_ref, own_ref, came_ref, mid_s, act_s, slope_s, up_s, down_s, gmid_s,
                   keep_m_ref, send_m_ref, up_acc, down_acc, entry_s, cot_s, gh_s, pad_s)
    attn_bwd_kernel(length, count, False, False, True, ids_ref, gmid_s, x_ref, qkv3_s, probs_s, mixed_s, weight_s,
                    cot_ref, keep_a_ref, send_a_ref, acc, joint_s, entry_a_s, cot_s, grad_mixed_s, entry_ready=True)


def middle(ids, cots, x, attn, mlp, dims):
    n, rows, length, width, ff = dims
    count = len(attn) // 2
    half_m = (count, ff // count, width)
    half_a = (count, 2 * width // count, width)

    def scratch(g):
        tokens = g * rows
        return [pltpu.VMEM((tokens, width), BF), pltpu.VMEM((tokens, 3 * width), BF),
                pltpu.VMEM((g * HEADS, rows, -(-rows // 128) * 128), F32), pltpu.VMEM((g, rows, width), F32),
                pltpu.VMEM((g, rows, ff), BF), pltpu.VMEM((g, rows, ff), BF), pltpu.VMEM((width + GAIN_ROWS, ff), BF),
                pltpu.VMEM((ff, width), BF), pltpu.VMEM((width, ff), F32), pltpu.VMEM((width, ff), F32),
                pltpu.VMEM((tokens, width), BF), pltpu.VMEM((tokens, ff), BF), pltpu.VMEM((rows, width), F32),
                pltpu.VMEM((g, rows, 3 * width), BF), pltpu.VMEM((g, HEADS, rows, rows), BF),
                pltpu.VMEM((g, rows, width), BF), pltpu.VMEM((width + GAIN_ROWS, 4 * width), BF),
                pltpu.VMEM((g, rows, width), F32), pltpu.VMEM((width, 4 * width), F32),
                pltpu.VMEM((tokens, 3 * width), BF), pltpu.VMEM((tokens, width), BF), pltpu.VMEM((tokens, width), BF)]

    return call(
        functools.partial(middle_kernel, length, count), "middle", ids, n, cots, [x], attn + mlp,
        [((n, length, width), BF), ((n, rows, width), BF)], [(half_m, BF), (half_m, BF), (half_a, BF), (half_a, BF)], scratch,
        n * rows * width * (24 * width + 12 * ff + 14 * rows), g=MIDDLE_STEP)


def swap_section(value):
    return lax.ppermute(value, "section", [(0, 1), (1, 0)])


def pick(stack, index):
    return lax.dynamic_index_in_dim(stack, index, 0, keepdims=False)


def tie(*values):
    return lax.optimization_barrier(values)


def exchange(values, axis):
    size = lax.axis_size(axis)
    return [lax.ppermute(v, axis, [(i, i ^ (k + 1)) for i in range(size)]) for k, v in enumerate(values)]


def direct(size):
    return size & (size - 1) == 0 and size <= MOST_PIECES


def total(first, others):
    result = first.astype(F32)
    for other in others:
        result = result + other.astype(F32)
    return result.astype(BF)


def local(ends_in, live, gain_attn, w_qkv, w_out, gain_mlp, w_up, w_down):
    me = lax.axis_index("section")
    mine_at = lax.axis_index("fsdp")
    first = me == 0
    shards = lax.axis_size("fsdp")
    replicas = lax.axis_size("replica")
    slots, length, width = ends_in.shape[1:]
    share = slots // 2
    rows = -(-length // 16) * 16
    depth = w_qkv.shape[1]
    ff = w_up.shape[2]
    ratio = ff // width
    dims = (share, rows, length, width, ff)
    packed = direct(shards) and depth % 16 == 0
    count = shards if packed else 1

    live_here = pick(live[:, 0], me)
    ids = jnp.stack([me, mine_at if packed else jnp.zeros_like(mine_at), live_here]).astype(jnp.int32)

    def columns(matrix):
        return matrix.reshape(depth, -1, width).transpose(1, 0, 2).reshape(-1, width)

    def halves(gain, first_half, second_half):
        row = lax.dynamic_update_slice(jnp.zeros((GAIN_ROWS, width), BF), gain, (0, mine_at * depth))
        return jnp.stack([jnp.concatenate([first_half, row]), jnp.concatenate([second_half, row])])

    qkv_own = columns(w_qkv[0])
    attn_own = halves(gain_attn, qkv_own[:2 * depth], jnp.concatenate([qkv_own[2 * depth:], w_out[0]]))
    mlp_own = halves(gain_mlp, columns(w_up[0]), w_down[0])

    def by_layer(own):
        kept, came = pick(own, me), swap_section(pick(own, 1 - me))
        return jnp.where(first, kept, came), jnp.where(first, came, kept)

    def spread(half):
        return [half] + exchange([half] * (shards - 1), "fsdp")

    def whole(half, mlp):
        full = lax.all_gather(half, "fsdp")
        gains = jnp.sum(full[:, -GAIN_ROWS:].astype(F32), axis=0).astype(BF)
        full = full[:, :-GAIN_ROWS]
        blocks = full.reshape(shards, -1, depth, width).transpose(1, 0, 2, 3).reshape(-1, width)
        if mlp:
            blocks = jnp.where(first, blocks, full.reshape(-1, width))
        return jnp.concatenate([blocks, gains])

    attn0, attn1 = by_layer(attn_own)
    mlp0, mlp1 = by_layer(mlp_own)
    came_images = swap_section(ends_in[0])
    images = [ends_in[0], came_images]
    attn0 = spread(attn0) if packed else [whole(attn0, False)]
    attn0 = attn0 + [swap_section(p) for p in attn0]

    *tied, attn1, mlp0 = tie(*attn0, attn1, mlp0)
    attn0 = tied
    if packed:
        both = spread(jnp.concatenate([mlp0, attn1]))
    else:
        both = [jnp.concatenate([whole(mlp0, True), whole(attn1, False)])]
    qkv0, probs0, mixed0, mid0, x0, weight0 = attn_fwd(ids, images, attn0, dims, True)

    mid0, mlp1, *both = tie(mid0, mlp1, *both)
    both = both + [swap_section(p) for p in both]
    mlp1 = spread(mlp1) if packed else [whole(mlp1, True)]
    x1, act0, slope0, up0, down0 = mlp_fwd(ids, mid0, both, dims, False)

    x1, *mlp1 = tie(x1, *mlp1)
    mlp1 = mlp1 + [swap_section(p) for p in mlp1]
    out, cot0, keep_m1, send_m1, keep_a1, send_a1 = middle(ids, images, x1, both, mlp1, dims)

    def scatter(half, came, mlp):
        if packed:
            parts = [total(half[k], [came[k]]) for k in range(count)]
            return [parts[0]] + exchange(parts[1:], "fsdp")
        chip = total(half, [came])
        blocks = chip.reshape(-1, shards, depth, width).transpose(1, 0, 2, 3).reshape(shards, -1, width)
        if mlp:
            blocks = jnp.where(first, blocks, chip.reshape(shards, -1, width))
        return [lax.psum_scatter(blocks, "fsdp", scatter_dimension=0)]

    def added(parts):
        return total(parts[0], parts[1:])

    line = replicas == 4
    at_z = lax.axis_index("replica")

    def inwards(part):
        return [part, lax.ppermute(part, "replica", [(0, 1), (3, 2)])] if line else [lax.psum(part, "replica")]

    def across(part):
        return [part, lax.ppermute(part, "replica", [(1, 2), (2, 1)])] if line else [part]

    def outwards(part):
        return [part, lax.ppermute(part, "replica", [(1, 0), (2, 3)])] if line else [part]

    def settled(parts):
        return jnp.where((at_z == 0) | (at_z == 3), parts[1], parts[0]) if line else parts[0]

    def doubled(part, k):
        return [part, lax.ppermute(part, "replica", [(i, i ^ k) for i in range(replicas)])]

    def tied_lists(lists, *values):
        flat = tie(*values, *[member for group in lists for member in group])
        values, flat = flat[:len(values)], flat[len(values):]
        groups = []
        for group in lists:
            groups.append(list(flat[:len(group)]))
            flat = flat[len(group):]
        return groups, values

    came_m1 = swap_section(send_m1)
    came_out = swap_section(out)
    came_a1 = swap_section(send_a1)
    gmid0, keep_m0, send_m0 = mlp_bwd(ids, cot0, mid0, act0, slope0, up0, down0, dims, count, False)

    gmid0, came_a1, keep_a1, came_m1, keep_m1, came_out = tie(gmid0, came_a1, keep_a1, came_m1, keep_m1, came_out)
    if packed:
        l1 = scatter(jnp.concatenate([keep_m1, keep_a1], 1), jnp.concatenate([came_m1, came_a1], 1), True)
    else:
        l1 = [jnp.concatenate([scatter(keep_m1, came_m1, True)[0], scatter(keep_a1, came_a1, False)[0]])]
    came_m0 = swap_section(send_m0)
    early = (share // 2 + 1) // PER_STEP * PER_STEP
    saved = [gmid0, x0, qkv0, probs0, mixed0]
    gx_early, begun = attn_bwd(ids, saved, weight0, dims, count, True, (0, early), final=False)

    (l1,), (begun, gx_early, came_m0, keep_m0) = tied_lists([l1], begun, gx_early, came_m0, keep_m0)
    m0 = scatter(keep_m0, came_m0, True)
    l1 = inwards(added(l1))
    came_gx_early = swap_section(gx_early)
    gx_late, keep_a0, send_a0 = attn_bwd(ids, saved, weight0, dims, count, True, (early, share), begun)

    (l1, m0), (send_a0, keep_a0, gx_late, came_gx_early) = tied_lists([l1, m0], send_a0, keep_a0, gx_late, came_gx_early)
    came_a0 = swap_section(send_a0)
    came_a0, l1, m0 = tie(came_a0, added(l1), added(m0))
    a0 = scatter(keep_a0, came_a0, False)
    l1 = across(l1)
    m0 = inwards(m0)
    came_gx_late = swap_section(gx_late)
    (a0, l1, m0), (came_gx_late,) = tied_lists([a0, l1, m0], came_gx_late)
    a0 = doubled(added(a0), 1) if line else [lax.psum(added(a0), "replica")]
    l1 = outwards(added(l1))
    m0 = across(added(m0))
    (l1, m0, a0), _ = tied_lists([l1, m0, a0])
    a0 = doubled(added(a0), 3) if line else a0
    m0 = outwards(added(m0))
    l1 = settled(l1)
    m0 = settled(m0)
    m1, a1 = l1[:ff // width * depth], l1[ff // width * depth:]
    gx = jnp.concatenate([gx_early, gx_late])
    came_gx = jnp.concatenate([came_gx_early, came_gx_late])

    def own_layer(sum0, sum1):
        mine = jnp.where(first, sum0, sum1)
        other = swap_section(jnp.where(first, sum1, sum0))
        return jnp.concatenate([jnp.where(first, mine, other), jnp.where(first, other, mine)]).astype(F32)

    mlp_grad = own_layer(m0, m1)
    attn_grad = own_layer(added(a0), a1)

    def rows_of(blocks):
        return blocks.reshape(-1, depth, width).transpose(1, 0, 2).reshape(depth, -1)

    grad_qkv, grad_out = rows_of(attn_grad[:3 * depth])[None], attn_grad[3 * depth:][None]
    grad_up, grad_down = rows_of(mlp_grad[:ratio * depth])[None], mlp_grad[ratio * depth:][None]
    grad_gain_attn = jnp.sum(grad_qkv * w_qkv.astype(F32), axis=-1) / gain_attn.astype(F32)
    grad_gain_mlp = jnp.sum(grad_up * w_up.astype(F32), axis=-1) / gain_mlp.astype(F32)

    own = jnp.where(first, gx, out)
    came = jnp.where(first, came_gx, came_out)
    ends_out = jnp.where(first, jnp.concatenate([own, came]), jnp.concatenate([came, own]))
    return (ends_out[None], grad_gain_attn, grad_qkv, grad_out, grad_gain_mlp, grad_up, grad_down)


def solution(mesh):
    in_specs = (
        P("section", ("fsdp", "replica"), None, None),
        P(None, ("fsdp", "replica")),
        P("section", "fsdp"),
        P("section", "fsdp", None),
        P("section", "fsdp", None),
        P("section", "fsdp"),
        P("section", "fsdp", None),
        P("section", "fsdp", None),
    )
    out_specs = (
        P("section", ("fsdp", "replica"), None, None),
        P("section", "fsdp"),
        P("section", "fsdp", None),
        P("section", "fsdp", None),
        P("section", "fsdp"),
        P("section", "fsdp", None),
        P("section", "fsdp", None),
    )
    return jax.shard_map(local, mesh=mesh, in_specs=in_specs, out_specs=out_specs, check_vma=False)
```

```python
import functools

import jax
import jax.numpy as jnp
from jax import lax
from jax.experimental import pallas as pl
from jax.experimental.pallas import tpu as pltpu
from jax.sharding import PartitionSpec as P

HEADS = 6
HEAD_DIM = 64
PAIR = 2 * HEAD_DIM
EPS = 1e-06
BF = jnp.bfloat16
F32 = jnp.float32
VMEM_LIMIT = 56 * 1024 * 1024
PER_STEP = 2
MIDDLE_STEP = 2
GAIN_ROWS = 16
MOST_PIECES = 8


def dot_nn(a, b):
    return lax.dot_general(a, b, (((1,), (0,)), ((), ())), preferred_element_type=F32)


def dot_nt(a, b):
    return lax.dot_general(a, b, (((1,), (1,)), ((), ())), preferred_element_type=F32)


def dot_tn(a, b):
    return lax.dot_general(a, b, (((0,), (0,)), ((), ())), preferred_element_type=F32)


def norm_rows(values):
    centered = values - jnp.mean(values, axis=-1, keepdims=True)
    scale = lax.rsqrt(jnp.mean(centered * centered, axis=-1, keepdims=True) + EPS)
    return centered * scale, scale


def norm_rows_back(grad_normed, normed, scale):
    first = jnp.mean(grad_normed, axis=-1, keepdims=True)
    second = jnp.mean(grad_normed * normed, axis=-1, keepdims=True)
    return scale * (grad_normed - first - normed * second)


def gelu_both(v):
    cdf = 0.5 * (1.0 + lax.erf(v * 0.7071067811865476))
    density = jnp.exp(-0.5 * v * v) * 0.3989422804014327
    return v * cdf, cdf + v * density


def gain_of(weight_ref, width):
    return weight_ref[width:width + GAIN_ROWS, :width].astype(F32)[:1]


def place_gain(pieces, weight_ref, width):
    last = pieces[0].shape[0] - GAIN_ROWS
    rows = sum(piece[last:last + GAIN_ROWS, :].astype(F32) for piece in pieces)
    weight_ref[width:width + GAIN_ROWS, :width] = rows.astype(BF)


def place_attn(ids_ref, pieces, weight_ref):
    count = len(pieces) // 2
    width = weight_ref.shape[1] // 4
    place_gain(pieces[:count], weight_ref, width)
    depth = width // count
    for section in range(2):
        @pl.when(ids_ref[0] == section)
        def _():
            for k in range(count):
                at = pl.ds(pl.multiple_of((ids_ref[1] ^ k) * depth, depth), depth)
                for half, piece in ((section, pieces[k]), (1 - section, pieces[count + k])):
                    for b in range(2):
                        lanes = (2 * half + b) * width
                        weight_ref[at, lanes:lanes + width] = piece[b * depth:(b + 1) * depth, :]


def place_mlp(ids_ref, pieces, up_ref, down_ref):
    count = len(pieces) // 2
    hidden, width = down_ref.shape
    place_gain(pieces[:count], up_ref, width)
    depth = width // count
    tall = hidden // count
    for section in range(2):
        @pl.when(ids_ref[0] == section)
        def _():
            for k in range(count):
                shard = ids_ref[1] ^ k
                at = pl.ds(pl.multiple_of(shard * depth, depth), depth)
                for half, piece in ((section, pieces[k]), (1 - section, pieces[count + k])):
                    if half == 0:
                        for b in range(hidden // width):
                            up_ref[at, b * width:(b + 1) * width] = piece[b * depth:(b + 1) * depth, :]
                    else:
                        down_ref[pl.ds(pl.multiple_of(shard * tall, tall), tall), :] = piece[:tall, :]


def attn_fwd_kernel(length, count, entering, ids_ref, *refs):
    if entering:
        own_ref, came_ref = refs[:2]
        pieces, refs = refs[2:2 + 2 * count], refs[2 + 2 * count:]
        qkv_ref, probs_ref, mixed_ref, mid_ref, weight_ref, x_ref, entry_s, qkv_s, scores_s, pad_s = refs
    else:
        x_ref = refs[0]
        pieces, refs = refs[1:1 + 2 * count], refs[1 + 2 * count:]
        qkv_ref, probs_ref, mixed_ref, mid_ref, weight_ref, entry_s, qkv_s, scores_s = refs
    images, rows, width = x_ref.shape

    @pl.when(pl.program_id(0) == 0)
    def _():
        place_attn(ids_ref, pieces, weight_ref)
        if entering:
            pad_s[...] = jnp.zeros_like(pad_s)

    gain = gain_of(weight_ref, width)
    for g in range(images):
        if entering:
            pad_s[g, :length, :] = jnp.where(ids_ref[0] == 0, own_ref[g].astype(F32), came_ref[g].astype(F32))
            values = pad_s[g]
            x_ref[g] = values.astype(BF)
        else:
            values = x_ref[g].astype(F32)
        normed, _ = norm_rows(values)
        entry_s[g * rows:(g + 1) * rows, :] = (normed * gain).astype(BF)
    qkv_s[...] = dot_nn(entry_s[...], weight_ref[:width, :3 * width]).astype(BF)
    lane = lax.broadcasted_iota(jnp.int32, (rows, PAIR), 1)
    cut = (length // 8) * 8

    def fill_scores(g):
        own_rows = slice(g * rows, (g + 1) * rows)
        for head in range(HEADS):
            at = head // 2 * PAIR
            q = qkv_s[own_rows, at:at + PAIR] * 0.125
            q = jnp.where((lane // HEAD_DIM) == head % 2, q, jnp.zeros_like(q))
            scores_s[g % 2 * HEADS + head, :, :rows] = dot_nt(qkv_s[own_rows, width + at:width + at + PAIR], q)

    def fill_probs(g):
        for head in range(HEADS):
            for lo in range(0, rows, 128):
                hi = min(lo + 128, rows)
                scores = scores_s[g % 2 * HEADS + head, :, lo:hi]
                tail_row = lax.broadcasted_iota(jnp.int32, (rows - cut, hi - lo), 0) + cut
                scores = jnp.concatenate([scores[:cut], jnp.where(tail_row < length, scores[cut:], -1e30)], axis=0)
                parts = jnp.exp(scores - jnp.max(scores, axis=0, keepdims=True))
                inv = 1.0 / jnp.sum(parts, axis=0, keepdims=True)
                probs_ref[g, head, :, lo:hi] = (parts * inv).astype(BF)

    def fill_mixed(g):
        own_rows = slice(g * rows, (g + 1) * rows)
        for pair in range(HEADS // 2):
            at = pair * PAIR
            v_t = qkv_s[own_rows, 2 * width + at:2 * width + at + PAIR].T
            mixed = [dot_nn(v_t[side * HEAD_DIM:(side + 1) * HEAD_DIM], probs_ref[g, pair * 2 + side]) for side in range(2)]
            mixed_ref[g, :, at:at + PAIR] = jnp.concatenate(mixed, axis=0).astype(BF).T

    fill_scores(0)
    for g in range(images):
        qkv_ref[g] = qkv_s[g * rows:(g + 1) * rows, :]
        if g + 1 < images:
            fill_scores(g + 1)
        fill_probs(g)
        fill_mixed(g)
    added = dot_nn(mixed_ref[...].reshape(images * rows, width), weight_ref[:width, 3 * width:])
    for g in range(images):
        mid_ref[g] = x_ref[g].astype(F32) + added[g * rows:(g + 1) * rows]


def rows_at(pieces, low, high):
    return [piece.at[low:high, :] for piece in pieces]


def mlp_fwd_kernel(length, count, leaving, ids_ref, mid_ref, *refs):
    pieces, refs = refs[:2 * count], refs[2 * count:]
    pieces = rows_at(pieces, 0, refs[4].shape[0] // count + GAIN_ROWS)
    out_ref, act_ref, slope_ref, up_ref, down_ref, entry_s, act_s = refs
    images, rows, width = mid_ref.shape
    hidden_width = up_ref.shape[1]

    @pl.when(pl.program_id(0) == 0)
    def _():
        place_mlp(ids_ref, pieces, up_ref, down_ref)

    gain = gain_of(up_ref, width)
    for g in range(images):
        normed, _ = norm_rows(mid_ref[g])
        entry_s[g * rows:(g + 1) * rows, :] = (normed * gain).astype(BF)
    step = 256
    for at in range(0, hidden_width, step):
        hidden = dot_nn(entry_s[...], up_ref[:width, at:at + step])
        act, slope = gelu_both(hidden)
        act_s[:, at:at + step] = act.astype(BF)
        for g in range(images):
            slope_ref[g, :, at:at + step] = slope[g * rows:(g + 1) * rows].astype(BF)
    added = dot_nn(act_s[...], down_ref[...])
    for g in range(images):
        act_ref[g] = act_s[g * rows:(g + 1) * rows, :]
        out = mid_ref[g] + added[g * rows:(g + 1) * rows]
        if leaving:
            live = pl.program_id(0) * images + g < ids_ref[2]
            out_ref[g] = jnp.where(live, out[:length], 0.0).astype(BF)
        else:
            out_ref[g] = out.astype(BF)


def mlp_bwd_kernel(length, count, entering, entry_ready, ids_ref, *refs):
    if entering:
        own_ref, came_ref, *refs = refs
        *refs, pad_s = refs
    else:
        cot_ref, *refs = refs
    mid_ref, act_ref, slope_ref, up_ref, down_ref, gmid_ref, keep_ref, send_ref, *refs = refs
    up_acc, down_acc, entry_s, cot_s, gh_s = refs
    images, rows, width = mid_ref.shape
    step_id = pl.program_id(0)

    @pl.when(step_id == 0)
    def _():
        up_acc[...] = jnp.zeros_like(up_acc)
        down_acc[...] = jnp.zeros_like(down_acc)
        if entering:
            pad_s[...] = jnp.zeros_like(pad_s)

    hidden_width = up_ref.shape[1]
    step = 512
    gain = gain_of(up_ref, width)
    for g in range(images):
        if entering:
            live = step_id * images + g < ids_ref[2]
            came = jnp.where(ids_ref[0] == 0, came_ref[g].astype(F32), own_ref[g].astype(F32))
            pad_s[:length, :] = jnp.where(live, came, 0.0)
            cot_s[g * rows:(g + 1) * rows, :] = pad_s[...].astype(BF)
        else:
            cot_s[g * rows:(g + 1) * rows, :] = cot_ref[g]
        if not entry_ready:
            normed, _ = norm_rows(mid_ref[g])
            entry_s[g * rows:(g + 1) * rows, :] = (normed * gain).astype(BF)
    for at in range(0, hidden_width, step):
        tile = slice(at, at + step)
        grad_act = dot_nt(cot_s[...], down_ref[tile, :])
        slope = slope_ref[:, :, tile].reshape(images * rows, step)
        gh_s[:, tile] = (grad_act * slope.astype(F32)).astype(BF)
    down_acc[...] += dot_tn(cot_s[...], act_ref[...].reshape(images * rows, hidden_width))
    up_acc[...] += dot_tn(entry_s[...], gh_s[...])
    grad_entry = dot_nt(gh_s[...], up_ref[:width, :])
    for g in range(images):
        normed, scale = norm_rows(mid_ref[g])
        back = norm_rows_back(grad_entry[g * rows:(g + 1) * rows] * gain, normed, scale)
        gmid_ref[g] = cot_s[g * rows:(g + 1) * rows, :].astype(F32) + back

    @pl.when(step_id == pl.num_programs(0) - 1)
    def _():
        depth = width // count
        tall = hidden_width // count
        for section in range(2):
            @pl.when(ids_ref[0] == section)
            def _():
                for k in range(count):
                    shard = ids_ref[1] ^ k
                    at = pl.ds(pl.multiple_of(shard * depth, depth), depth)
                    up_out, down_out = (keep_ref, send_ref) if section == 0 else (send_ref, keep_ref)
                    for b in range(hidden_width // width):
                        up_out[k, b * depth:(b + 1) * depth, :] = up_acc[at, b * width:(b + 1) * width].astype(BF)
                    for j in range(0, tall, 128):
                        lanes = pl.ds(pl.multiple_of(shard * tall + j, 128), 128)
                        down_out[k, j:j + 128, :] = down_acc[:, lanes].T.astype(BF)


def attn_bwd_kernel(length, count, leaving, carried, final, ids_ref, gmid_ref, x_ref, qkv_ref, probs_ref, mixed_ref,
                    weight_ref, *refs, entry_ready=False):
    if carried:
        begun_ref, *refs = refs
    if final:
        gx_ref, keep_ref, send_ref, acc, *refs = refs
    else:
        gx_ref, acc, *refs = refs
    joint_s, entry_s, low_s, grad_mixed_s, grad_probs_s, grad_scores_s = refs
    images, rows, width = x_ref.shape
    step_id = pl.program_id(0)

    @pl.when(step_id == 0)
    def _():
        acc[...] = begun_ref[...] if carried else jnp.zeros_like(acc)

    lane = lax.broadcasted_iota(jnp.int32, (rows, PAIR), 1)
    gain = gain_of(weight_ref, width)
    for g in range(images):
        low_s[g * rows:(g + 1) * rows, :] = gmid_ref[g].astype(BF)
        if not entry_ready:
            normed, _ = norm_rows(x_ref[g].astype(F32))
            entry_s[g * rows:(g + 1) * rows, :] = (normed * gain).astype(BF)
    acc[:, 3 * width:] += dot_tn(mixed_ref[...].reshape(images * rows, width), low_s[...])
    grad_mixed_s[...] = dot_nt(low_s[...], weight_ref[:width, 3 * width:]).astype(BF)

    def own_half(g, head):
        gm = grad_mixed_s[g * rows:(g + 1) * rows, head // 2 * PAIR:head // 2 * PAIR + PAIR]
        return jnp.where((lane // HEAD_DIM) == head % 2, gm, jnp.zeros_like(gm))

    def fill_grad_probs(g):
        for head in range(HEADS):
            at = 2 * width + head // 2 * PAIR
            grad_probs_s[g % 2 * HEADS + head, :, :rows] = dot_nt(qkv_ref[g, :, at:at + PAIR], own_half(g, head))

    def fill_grad_scores(g):
        for head in range(HEADS):
            for lo in range(0, rows, 128):
                hi = min(lo + 128, rows)
                probs = probs_ref[g, head, :, lo:hi].astype(F32)
                grad_probs = grad_probs_s[g % 2 * HEADS + head, :, lo:hi]
                delta = jnp.sum(probs * grad_probs, axis=0, keepdims=True)
                grad_scores_s[head, :, lo:hi] = (probs * (grad_probs - delta)).astype(BF)

    def fill_joint(g):
        own_rows = slice(g * rows, (g + 1) * rows)
        for pair in range(HEADS // 2):
            at = pair * PAIR
            q = qkv_ref[g, :, at:at + PAIR] * 0.125
            k_t = (qkv_ref[g, :, width + at:width + at + PAIR] * 0.125).T
            grad_k = None
            grad_v = None
            grad_q_t = []
            for side in range(2):
                head = pair * 2 + side
                q_own = jnp.where((lane // HEAD_DIM) == side, q, jnp.zeros_like(q))
                part_v = dot_nn(probs_ref[g, head], own_half(g, head))
                part_k = dot_nn(grad_scores_s[head], q_own)
                grad_v = part_v if grad_v is None else grad_v + part_v
                grad_k = part_k if grad_k is None else grad_k + part_k
                grad_q_t.append(dot_nn(k_t[side * HEAD_DIM:(side + 1) * HEAD_DIM], grad_scores_s[head]))
            joint_s[own_rows, at:at + PAIR] = jnp.concatenate(grad_q_t, axis=0).astype(BF).T
            joint_s[own_rows, width + at:width + at + PAIR] = grad_k.astype(BF)
            joint_s[own_rows, 2 * width + at:2 * width + at + PAIR] = grad_v.astype(BF)

    fill_grad_probs(0)
    for g in range(images):
        if g + 1 < images:
            fill_grad_probs(g + 1)
        fill_grad_scores(g)
        fill_joint(g)
    acc[:, :3 * width] += dot_tn(entry_s[...], joint_s[...])
    grad_entry = dot_nt(joint_s[...], weight_ref[:width, :3 * width])
    for g in range(images):
        normed, scale = norm_rows(x_ref[g].astype(F32))
        grad_x = gmid_ref[g] + norm_rows_back(grad_entry[g * rows:(g + 1) * rows] * gain, normed, scale)
        gx_ref[g] = (grad_x[:length] if leaving else grad_x).astype(BF)

    if not final:
        return

    @pl.when(step_id == pl.num_programs(0) - 1)
    def _():
        depth = width // count
        for section in range(2):
            @pl.when(ids_ref[0] == section)
            def _():
                for k in range(count):
                    at = pl.ds(pl.multiple_of((ids_ref[1] ^ k) * depth, depth), depth)
                    for half, out_ref in ((section, keep_ref), (1 - section, send_ref)):
                        for b in range(2):
                            lanes = (2 * half + b) * width
                            out_ref[k, b * depth:(b + 1) * depth, :] = acc[at, lanes:lanes + width].astype(BF)


def call(body, name, ids, images, entering, streams, fixed, stream_outs, fixed_outs, scratch, flops, start=0, g=PER_STEP):
    g = g if images % g == 0 else 1

    def entering_spec(shape):
        return pl.BlockSpec((g,) + shape[1:], lambda i, ids: (ids[0] * (images // g) + i,) + (0,) * (len(shape) - 1))

    def per_image(shape, at=0):
        return pl.BlockSpec((g,) + shape[1:], lambda i, ids: (i + at // g,) + (0,) * (len(shape) - 1))

    def whole(shape, **more):
        return pl.BlockSpec(shape, lambda i, ids: (0,) * len(shape), **more)

    outs = [jax.ShapeDtypeStruct(s, d) for s, d in stream_outs + fixed_outs]
    moved = sum(a.size * a.dtype.itemsize for a in list(streams) + list(fixed) + outs)
    return pl.pallas_call(
        body,
        name=name,
        grid_spec=pltpu.PrefetchScalarGridSpec(
            num_scalar_prefetch=1,
            grid=(images // g,),
            in_specs=[entering_spec(a.shape) for a in entering] + [per_image(a.shape, start) for a in streams]
            + [whole(a.shape, pipeline_mode=pl.Buffered(1)) for a in fixed],
            out_specs=[per_image(s) for s, _ in stream_outs] + [whole(s) for s, _ in fixed_outs],
            scratch_shapes=scratch(g),
        ),
        out_shape=outs,
        compiler_params=pltpu.CompilerParams(vmem_limit_bytes=VMEM_LIMIT, dimension_semantics=("arbitrary",)),
        cost_estimate=pl.CostEstimate(flops=int(flops), bytes_accessed=int(moved), transcendentals=0),
    )(ids, *entering, *streams, *fixed)


def attn_fwd(ids, x, pieces, dims, entering):
    n, rows, length, width, ff = dims
    count = len(pieces) // 2
    outs = [((n, rows, 3 * width), BF), ((n, HEADS, rows, rows), BF), ((n, rows, width), BF), ((n, rows, width), F32)]
    fixed_outs = [((width + GAIN_ROWS, 4 * width), BF)]
    body = functools.partial(attn_fwd_kernel, length, count, entering)

    def scratch(g):
        refs = [pltpu.VMEM((g * rows, width), BF), pltpu.VMEM((g * rows, 3 * width), BF),
                pltpu.VMEM((min(g, 2) * HEADS, rows, -(-rows // 128) * 128), F32)]
        return refs + ([pltpu.VMEM((g, rows, width), F32)] if entering else [])

    flops = 2 * n * rows * width * 4 * width + 4 * n * rows * rows * width
    if entering:
        def reordered(ids_ref, *refs):
            ins, rest = refs[:2 + 2 * count], refs[2 + 2 * count:]
            qkv, probs, mixed, mid, xp, weight, *scr = rest
            body(ids_ref, *ins, qkv, probs, mixed, mid, weight, xp, *scr)
        return call(reordered, "attention_forward", ids, n, x, [], pieces, outs + [((n, rows, width), BF)], fixed_outs,
                    scratch, flops)
    qkv, probs, mixed, mid, weight = call(body, "attention_forward", ids, n, [], [x], pieces, outs, fixed_outs, scratch, flops)
    return qkv, probs, mixed, mid, x, weight


def mlp_fwd(ids, mid, pieces, dims, leaving):
    n, rows, length, width, ff = dims
    count = len(pieces) // 2
    return call(
        functools.partial(mlp_fwd_kernel, length, count, leaving), "mlp_forward", ids, n, [], [mid], pieces,
        [((n, length if leaving else rows, width), BF), ((n, rows, ff), BF), ((n, rows, ff), BF)],
        [((width + GAIN_ROWS, ff), BF), ((ff, width), BF)],
        lambda g: [pltpu.VMEM((g * rows, width), BF), pltpu.VMEM((g * rows, ff), BF)],
        4 * n * rows * width * ff)


def mlp_bwd(ids, cot, mid, act, slope, up, down, dims, count, entering):
    n, rows, length, width, ff = dims

    def scratch(g):
        refs = [pltpu.VMEM((width, ff), F32), pltpu.VMEM((width, ff), F32), pltpu.VMEM((g * rows, width), BF),
                pltpu.VMEM((g * rows, width), BF), pltpu.VMEM((g * rows, ff), BF)]
        return refs + ([pltpu.VMEM((rows, width), F32)] if entering else [])

    half = (count, ff // count, width)
    return call(
        functools.partial(mlp_bwd_kernel, length, count, entering, False), "mlp_backward", ids, n,
        cot if entering else [], ([] if entering else [cot]) + [mid, act, slope], [up, down],
        [((n, rows, width), F32)], [(half, BF), (half, BF)], scratch, 8 * n * rows * width * ff)


def attn_bwd(ids, streams, weight, dims, count, leaving, span, begun=None, final=True):
    n, rows, length, width, ff = dims
    low, high = span
    half = (count, 2 * width // count, width)
    acc = ((width, 4 * width), F32)
    return call(
        functools.partial(attn_bwd_kernel, length, count, leaving, begun is not None, final), "attention_backward",
        ids, high - low, [], streams, [weight] + ([] if begun is None else [begun]),
        [((high - low, length if leaving else rows, width), BF)], [(half, BF), (half, BF)] if final else [acc],
        lambda g: ([pltpu.VMEM(*acc)] if final else []) + [pltpu.VMEM((g * rows, 3 * width), BF)]
        + [pltpu.VMEM((g * rows, width), BF)] * 3 + [
            pltpu.VMEM((min(g, 2) * HEADS, rows, -(-rows // 128) * 128), F32), pltpu.VMEM((HEADS, rows, rows), BF)],
        (high - low) * (4 * rows * width * 4 * width + 10 * rows * rows * width), start=low)


def middle_kernel(length, count, ids_ref, own_ref, came_ref, x_ref, *refs):
    attn, mlp, refs = refs[:2 * count], refs[2 * count:4 * count], refs[4 * count:]
    out_ref, cot_ref, keep_m_ref, send_m_ref, keep_a_ref, send_a_ref, *refs = refs
    entry_s, qkv_s, scores_s, mid_s, act_s, slope_s, up_s, down_s, up_acc, down_acc, cot_s, gh_s, pad_s, *refs = refs
    qkv3_s, probs_s, mixed_s, weight_s, gmid_s, acc, grad_mixed_s, entry_a_s, grad_scores_s = refs
    skip = down_s.shape[0] // count + GAIN_ROWS
    attn = rows_at(attn, skip, attn[0].shape[0])
    attn_fwd_kernel(length, count, False, ids_ref, x_ref, *attn, qkv3_s, probs_s, mixed_s, mid_s, weight_s,
                    entry_a_s, qkv_s, scores_s)
    mlp_fwd_kernel(length, count, True, ids_ref, mid_s, *mlp, out_ref, act_s, slope_s, up_s, down_s, entry_s, gh_s)
    mlp_bwd_kernel(length, count, True, True, ids_ref, own_ref, came_ref, mid_s, act_s, slope_s, up_s, down_s, gmid_s,
                   keep_m_ref, send_m_ref, up_acc, down_acc, entry_s, cot_s, gh_s, pad_s)
    attn_bwd_kernel(length, count, False, False, True, ids_ref, gmid_s, x_ref, qkv3_s, probs_s, mixed_s, weight_s,
                    cot_ref, keep_a_ref, send_a_ref, acc, qkv_s, entry_a_s, cot_s, grad_mixed_s, scores_s, grad_scores_s, entry_ready=True)


def middle(ids, cots, x, attn, mlp, dims):
    n, rows, length, width, ff = dims
    count = len(attn) // 2
    half_m = (count, ff // count, width)
    half_a = (count, 2 * width // count, width)

    def scratch(g):
        tokens = g * rows
        return [pltpu.VMEM((tokens, width), BF), pltpu.VMEM((tokens, 3 * width), BF),
                pltpu.VMEM((min(g, 2) * HEADS, rows, -(-rows // 128) * 128), F32), pltpu.VMEM((g, rows, width), F32),
                pltpu.VMEM((g, rows, ff), BF), pltpu.VMEM((g, rows, ff), BF), pltpu.VMEM((width + GAIN_ROWS, ff), BF),
                pltpu.VMEM((ff, width), BF), pltpu.VMEM((width, ff), F32), pltpu.VMEM((width, ff), F32),
                pltpu.VMEM((tokens, width), BF), pltpu.VMEM((tokens, ff), BF), pltpu.VMEM((rows, width), F32),
                pltpu.VMEM((g, rows, 3 * width), BF), pltpu.VMEM((g, HEADS, rows, rows), BF),
                pltpu.VMEM((g, rows, width), BF), pltpu.VMEM((width + GAIN_ROWS, 4 * width), BF),
                pltpu.VMEM((g, rows, width), F32), pltpu.VMEM((width, 4 * width), F32),
                pltpu.VMEM((tokens, width), BF), pltpu.VMEM((tokens, width), BF), pltpu.VMEM((HEADS, rows, rows), BF)]

    return call(
        functools.partial(middle_kernel, length, count), "middle", ids, n, cots, [x], attn + mlp,
        [((n, length, width), BF), ((n, rows, width), BF)], [(half_m, BF), (half_m, BF), (half_a, BF), (half_a, BF)], scratch,
        n * rows * width * (24 * width + 12 * ff + 14 * rows), g=MIDDLE_STEP)


def swap_section(value):
    return lax.ppermute(value, "section", [(0, 1), (1, 0)])


def pick(stack, index):
    return lax.dynamic_index_in_dim(stack, index, 0, keepdims=False)


def tie(*values):
    return lax.optimization_barrier(values)


def exchange(values, axis):
    size = lax.axis_size(axis)
    return [lax.ppermute(v, axis, [(i, i ^ (k + 1)) for i in range(size)]) for k, v in enumerate(values)]


def direct(size):
    return size & (size - 1) == 0 and size <= MOST_PIECES


def total(first, others):
    result = first.astype(F32)
    for other in others:
        result = result + other.astype(F32)
    return result.astype(BF)


def local(ends_in, live, gain_attn, w_qkv, w_out, gain_mlp, w_up, w_down):
    me = lax.axis_index("section")
    mine_at = lax.axis_index("fsdp")
    first = me == 0
    shards = lax.axis_size("fsdp")
    replicas = lax.axis_size("replica")
    slots, length, width = ends_in.shape[1:]
    share = slots // 2
    rows = -(-length // 16) * 16
    depth = w_qkv.shape[1]
    ff = w_up.shape[2]
    ratio = ff // width
    dims = (share, rows, length, width, ff)
    packed = direct(shards) and depth % 16 == 0
    count = shards if packed else 1

    live_here = pick(live[:, 0], me)
    ids = jnp.stack([me, mine_at if packed else jnp.zeros_like(mine_at), live_here]).astype(jnp.int32)

    def columns(matrix):
        return matrix.reshape(depth, -1, width).transpose(1, 0, 2).reshape(-1, width)

    def halves(gain, first_half, second_half):
        row = lax.dynamic_update_slice(jnp.zeros((GAIN_ROWS, width), BF), gain, (0, mine_at * depth))
        return jnp.stack([jnp.concatenate([first_half, row]), jnp.concatenate([second_half, row])])

    qkv_own = columns(w_qkv[0])
    attn_own = halves(gain_attn, qkv_own[:2 * depth], jnp.concatenate([qkv_own[2 * depth:], w_out[0]]))
    mlp_own = halves(gain_mlp, columns(w_up[0]), w_down[0])

    def by_layer(own):
        kept, came = pick(own, me), swap_section(pick(own, 1 - me))
        return jnp.where(first, kept, came), jnp.where(first, came, kept)

    def spread(half):
        return [half] + exchange([half] * (shards - 1), "fsdp")

    def whole(half, mlp):
        full = lax.all_gather(half, "fsdp")
        gains = jnp.sum(full[:, -GAIN_ROWS:].astype(F32), axis=0).astype(BF)
        full = full[:, :-GAIN_ROWS]
        blocks = full.reshape(shards, -1, depth, width).transpose(1, 0, 2, 3).reshape(-1, width)
        if mlp:
            blocks = jnp.where(first, blocks, full.reshape(-1, width))
        return jnp.concatenate([blocks, gains])

    attn0, attn1 = by_layer(attn_own)
    mlp0, mlp1 = by_layer(mlp_own)
    came_images = swap_section(ends_in[0])
    images = [ends_in[0], came_images]
    attn0 = spread(attn0) if packed else [whole(attn0, False)]
    attn0 = attn0 + [swap_section(p) for p in attn0]

    *tied, attn1, mlp0 = tie(*attn0, attn1, mlp0)
    attn0 = tied
    if packed:
        both = spread(jnp.concatenate([mlp0, attn1]))
    else:
        both = [jnp.concatenate([whole(mlp0, True), whole(attn1, False)])]
    qkv0, probs0, mixed0, mid0, x0, weight0 = attn_fwd(ids, images, attn0, dims, True)

    mid0, mlp1, *both = tie(mid0, mlp1, *both)
    both = both + [swap_section(p) for p in both]
    mlp1 = spread(mlp1) if packed else [whole(mlp1, True)]
    x1, act0, slope0, up0, down0 = mlp_fwd(ids, mid0, both, dims, False)

    x1, *mlp1 = tie(x1, *mlp1)
    mlp1 = mlp1 + [swap_section(p) for p in mlp1]
    out, cot0, keep_m1, send_m1, keep_a1, send_a1 = middle(ids, images, x1, both, mlp1, dims)

    def scatter(half, came, mlp):
        if packed:
            parts = [total(half[k], [came[k]]) for k in range(count)]
            return [parts[0]] + exchange(parts[1:], "fsdp")
        chip = total(half, [came])
        blocks = chip.reshape(-1, shards, depth, width).transpose(1, 0, 2, 3).reshape(shards, -1, width)
        if mlp:
            blocks = jnp.where(first, blocks, chip.reshape(shards, -1, width))
        return [lax.psum_scatter(blocks, "fsdp", scatter_dimension=0)]

    def added(parts):
        return total(parts[0], parts[1:])

    line = replicas == 4
    at_z = lax.axis_index("replica")

    def inwards(part):
        return [part, lax.ppermute(part, "replica", [(0, 1), (3, 2)])] if line else [lax.psum(part, "replica")]

    def across(part):
        return [part, lax.ppermute(part, "replica", [(1, 2), (2, 1)])] if line else [part]

    def outwards(part):
        return [part, lax.ppermute(part, "replica", [(1, 0), (2, 3)])] if line else [part]

    def settled(parts):
        return jnp.where((at_z == 0) | (at_z == 3), parts[1], parts[0]) if line else parts[0]

    def doubled(part, k):
        return [part, lax.ppermute(part, "replica", [(i, i ^ k) for i in range(replicas)])]

    def tied_lists(lists, *values):
        flat = tie(*values, *[member for group in lists for member in group])
        values, flat = flat[:len(values)], flat[len(values):]
        groups = []
        for group in lists:
            groups.append(list(flat[:len(group)]))
            flat = flat[len(group):]
        return groups, values

    came_m1 = swap_section(send_m1)
    came_out = swap_section(out)
    came_a1 = swap_section(send_a1)
    gmid0, keep_m0, send_m0 = mlp_bwd(ids, cot0, mid0, act0, slope0, up0, down0, dims, count, False)

    gmid0, came_a1, keep_a1, came_m1, keep_m1, came_out = tie(gmid0, came_a1, keep_a1, came_m1, keep_m1, came_out)
    if packed:
        l1 = scatter(jnp.concatenate([keep_m1, keep_a1], 1), jnp.concatenate([came_m1, came_a1], 1), True)
    else:
        l1 = [jnp.concatenate([scatter(keep_m1, came_m1, True)[0], scatter(keep_a1, came_a1, False)[0]])]
    came_m0 = swap_section(send_m0)
    early = (share // 2 + 1) // PER_STEP * PER_STEP
    saved = [gmid0, x0, qkv0, probs0, mixed0]
    gx_early, begun = attn_bwd(ids, saved, weight0, dims, count, True, (0, early), final=False)

    (l1,), (begun, gx_early, came_m0, keep_m0) = tied_lists([l1], begun, gx_early, came_m0, keep_m0)
    m0 = scatter(keep_m0, came_m0, True)
    l1 = inwards(added(l1))
    came_gx_early = swap_section(gx_early)
    gx_late, keep_a0, send_a0 = attn_bwd(ids, saved, weight0, dims, count, True, (early, share), begun)

    (l1, m0), (send_a0, keep_a0, gx_late, came_gx_early) = tied_lists([l1, m0], send_a0, keep_a0, gx_late, came_gx_early)
    came_a0 = swap_section(send_a0)
    came_a0, l1, m0 = tie(came_a0, added(l1), added(m0))
    a0 = scatter(keep_a0, came_a0, False)
    l1 = across(l1)
    m0 = inwards(m0)
    came_gx_late = swap_section(gx_late)
    (a0, l1, m0), (came_gx_late,) = tied_lists([a0, l1, m0], came_gx_late)
    a0 = doubled(added(a0), 1) if line else [lax.psum(added(a0), "replica")]
    l1 = outwards(added(l1))
    m0 = across(added(m0))
    (l1, m0, a0), _ = tied_lists([l1, m0, a0])
    a0 = doubled(added(a0), 3) if line else a0
    m0 = outwards(added(m0))
    (a0, m0, l1), _ = tied_lists([a0, m0, l1])
    l1 = settled(l1)
    m0 = settled(m0)
    m1, a1 = l1[:ff // width * depth], l1[ff // width * depth:]
    gx = jnp.concatenate([gx_early, gx_late])
    came_gx = jnp.concatenate([came_gx_early, came_gx_late])

    def own_layer(sum0, sum1):
        mine = jnp.where(first, sum0, sum1)
        other = swap_section(jnp.where(first, sum1, sum0))
        return jnp.concatenate([jnp.where(first, mine, other), jnp.where(first, other, mine)]).astype(F32)

    mlp_grad = own_layer(m0, m1)
    attn_grad = own_layer(added(a0), a1)

    def rows_of(blocks):
        return blocks.reshape(-1, depth, width).transpose(1, 0, 2).reshape(depth, -1)

    grad_qkv, grad_out = rows_of(attn_grad[:3 * depth])[None], attn_grad[3 * depth:][None]
    grad_up, grad_down = rows_of(mlp_grad[:ratio * depth])[None], mlp_grad[ratio * depth:][None]
    grad_gain_attn = jnp.sum(grad_qkv * w_qkv.astype(F32), axis=-1) / gain_attn.astype(F32)
    grad_gain_mlp = jnp.sum(grad_up * w_up.astype(F32), axis=-1) / gain_mlp.astype(F32)

    own = jnp.where(first, gx, out)
    came = jnp.where(first, came_gx, came_out)
    ends_out = jnp.where(first, jnp.concatenate([own, came]), jnp.concatenate([came, own]))
    return (ends_out[None], grad_gain_attn, grad_qkv, grad_out, grad_gain_mlp, grad_up, grad_down)


def solution(mesh):
    in_specs = (
        P("section", ("fsdp", "replica"), None, None),
        P(None, ("fsdp", "replica")),
        P("section", "fsdp"),
        P("section", "fsdp", None),
        P("section", "fsdp", None),
        P("section", "fsdp"),
        P("section", "fsdp", None),
        P("section", "fsdp", None),
    )
    out_specs = (
        P("section", ("fsdp", "replica"), None, None),
        P("section", "fsdp"),
        P("section", "fsdp", None),
        P("section", "fsdp", None),
        P("section", "fsdp"),
        P("section", "fsdp", None),
        P("section", "fsdp", None),
    )
    return jax.shard_map(local, mesh=mesh, in_specs=in_specs, out_specs=out_specs, check_vma=False)
```

```python
import functools

import jax
import jax.numpy as jnp
from jax import lax
from jax.experimental import pallas as pl
from jax.experimental.pallas import tpu as pltpu
from jax.sharding import PartitionSpec as P

HEADS = 6
HEAD_DIM = 64
PAIR = 2 * HEAD_DIM
EPS = 1e-06
BF = jnp.bfloat16
F32 = jnp.float32
VMEM_LIMIT = 56 * 1024 * 1024
PER_STEP = 2
MIDDLE_STEP = 2
GAIN_ROWS = 16
MOST_PIECES = 8


def dot_nn(a, b):
    return lax.dot_general(a, b, (((1,), (0,)), ((), ())), preferred_element_type=F32)


def dot_nt(a, b):
    return lax.dot_general(a, b, (((1,), (1,)), ((), ())), preferred_element_type=F32)


def dot_tn(a, b):
    return lax.dot_general(a, b, (((0,), (0,)), ((), ())), preferred_element_type=F32)


def norm_rows(values):
    centered = values - jnp.mean(values, axis=-1, keepdims=True)
    scale = lax.rsqrt(jnp.mean(centered * centered, axis=-1, keepdims=True) + EPS)
    return centered * scale, scale


def norm_rows_back(grad_normed, normed, scale):
    first = jnp.mean(grad_normed, axis=-1, keepdims=True)
    second = jnp.mean(grad_normed * normed, axis=-1, keepdims=True)
    return scale * (grad_normed - first - normed * second)


def gelu_both(v):
    cdf = 0.5 * (1.0 + lax.erf(v * 0.7071067811865476))
    density = jnp.exp(-0.5 * v * v) * 0.3989422804014327
    return v * cdf, cdf + v * density


def gain_of(weight_ref, width):
    return weight_ref[width:width + GAIN_ROWS, :width].astype(F32)[:1]


def place_gain(pieces, weight_ref, width):
    last = pieces[0].shape[0] - GAIN_ROWS
    rows = sum(piece[last:last + GAIN_ROWS, :].astype(F32) for piece in pieces)
    weight_ref[width:width + GAIN_ROWS, :width] = rows.astype(BF)


def place_attn(ids_ref, pieces, weight_ref):
    count = len(pieces) // 2
    width = weight_ref.shape[1] // 4
    place_gain(pieces[:count], weight_ref, width)
    depth = width // count
    for section in range(2):
        @pl.when(ids_ref[0] == section)
        def _():
            for k in range(count):
                at = pl.ds(pl.multiple_of((ids_ref[1] ^ k) * depth, depth), depth)
                for half, piece in ((section, pieces[k]), (1 - section, pieces[count + k])):
                    for b in range(2):
                        lanes = (2 * half + b) * width
                        weight_ref[at, lanes:lanes + width] = piece[b * depth:(b + 1) * depth, :]


def place_mlp(ids_ref, pieces, up_ref, down_ref):
    count = len(pieces) // 2
    hidden, width = down_ref.shape
    place_gain(pieces[:count], up_ref, width)
    depth = width // count
    tall = hidden // count
    for section in range(2):
        @pl.when(ids_ref[0] == section)
        def _():
            for k in range(count):
                shard = ids_ref[1] ^ k
                at = pl.ds(pl.multiple_of(shard * depth, depth), depth)
                for half, piece in ((section, pieces[k]), (1 - section, pieces[count + k])):
                    if half == 0:
                        for b in range(hidden // width):
                            up_ref[at, b * width:(b + 1) * width] = piece[b * depth:(b + 1) * depth, :]
                    else:
                        down_ref[pl.ds(pl.multiple_of(shard * tall, tall), tall), :] = piece[:tall, :]


def attn_fwd_kernel(length, count, entering, ids_ref, *refs):
    if entering:
        own_ref, came_ref = refs[:2]
        pieces, refs = refs[2:2 + 2 * count], refs[2 + 2 * count:]
        qkv_ref, probs_ref, mixed_ref, mid_ref, weight_ref, x_ref, entry_s, qkv_s, scores_s, pad_s = refs
    else:
        x_ref = refs[0]
        pieces, refs = refs[1:1 + 2 * count], refs[1 + 2 * count:]
        qkv_ref, probs_ref, mixed_ref, mid_ref, weight_ref, entry_s, qkv_s, scores_s = refs
    images, rows, width = x_ref.shape

    @pl.when(pl.program_id(0) == 0)
    def _():
        place_attn(ids_ref, pieces, weight_ref)
        if entering:
            pad_s[...] = jnp.zeros_like(pad_s)

    gain = gain_of(weight_ref, width)
    for g in range(images):
        if entering:
            pad_s[g, :length, :] = jnp.where(ids_ref[0] == 0, own_ref[g].astype(F32), came_ref[g].astype(F32))
            values = pad_s[g]
            x_ref[g] = values.astype(BF)
        else:
            values = x_ref[g].astype(F32)
        normed, _ = norm_rows(values)
        entry_s[g * rows:(g + 1) * rows, :] = (normed * gain).astype(BF)
    qkv_s[...] = dot_nn(entry_s[...], weight_ref[:width, :3 * width]).astype(BF)
    lane = lax.broadcasted_iota(jnp.int32, (rows, PAIR), 1)
    cut = (length // 8) * 8

    def fill_scores(g):
        own_rows = slice(g * rows, (g + 1) * rows)
        for head in range(HEADS):
            at = head // 2 * PAIR
            q = qkv_s[own_rows, at:at + PAIR] * 0.125
            q = jnp.where((lane // HEAD_DIM) == head % 2, q, jnp.zeros_like(q))
            scores_s[g % 2 * HEADS + head, :, :rows] = dot_nt(qkv_s[own_rows, width + at:width + at + PAIR], q)

    def fill_probs(g):
        for head in range(HEADS):
            for lo in range(0, rows, 128):
                hi = min(lo + 128, rows)
                scores = scores_s[g % 2 * HEADS + head, :, lo:hi]
                tail_row = lax.broadcasted_iota(jnp.int32, (rows - cut, hi - lo), 0) + cut
                scores = jnp.concatenate([scores[:cut], jnp.where(tail_row < length, scores[cut:], -1e30)], axis=0)
                parts = jnp.exp(scores - jnp.max(scores, axis=0, keepdims=True))
                inv = 1.0 / jnp.sum(parts, axis=0, keepdims=True)
                probs_ref[g, head, :, lo:hi] = (parts * inv).astype(BF)

    def fill_mixed(g):
        own_rows = slice(g * rows, (g + 1) * rows)
        for pair in range(HEADS // 2):
            at = pair * PAIR
            v_t = qkv_s[own_rows, 2 * width + at:2 * width + at + PAIR].T
            mixed = [dot_nn(v_t[side * HEAD_DIM:(side + 1) * HEAD_DIM], probs_ref[g, pair * 2 + side]) for side in range(2)]
            mixed_ref[g, :, at:at + PAIR] = jnp.concatenate(mixed, axis=0).astype(BF).T

    fill_scores(0)
    for g in range(images):
        qkv_ref[g] = qkv_s[g * rows:(g + 1) * rows, :]
        if g + 1 < images:
            fill_scores(g + 1)
        fill_probs(g)
        fill_mixed(g)
    added = dot_nn(mixed_ref[...].reshape(images * rows, width), weight_ref[:width, 3 * width:])
    for g in range(images):
        mid_ref[g] = x_ref[g].astype(F32) + added[g * rows:(g + 1) * rows]


def rows_at(pieces, low, high):
    return [piece.at[low:high, :] for piece in pieces]


def mlp_fwd_kernel(length, count, leaving, ids_ref, mid_ref, *refs):
    pieces, refs = refs[:2 * count], refs[2 * count:]
    pieces = rows_at(pieces, 0, refs[4].shape[0] // count + GAIN_ROWS)
    out_ref, act_ref, slope_ref, up_ref, down_ref, entry_s, act_s = refs
    images, rows, width = mid_ref.shape
    hidden_width = up_ref.shape[1]

    @pl.when(pl.program_id(0) == 0)
    def _():
        place_mlp(ids_ref, pieces, up_ref, down_ref)

    gain = gain_of(up_ref, width)
    for g in range(images):
        normed, _ = norm_rows(mid_ref[g])
        entry_s[g * rows:(g + 1) * rows, :] = (normed * gain).astype(BF)
    step = 256
    for at in range(0, hidden_width, step):
        hidden = dot_nn(entry_s[...], up_ref[:width, at:at + step])
        act, slope = gelu_both(hidden)
        act_s[:, at:at + step] = act.astype(BF)
        for g in range(images):
            slope_ref[g, :, at:at + step] = slope[g * rows:(g + 1) * rows].astype(BF)
    added = dot_nn(act_s[...], down_ref[...])
    for g in range(images):
        act_ref[g] = act_s[g * rows:(g + 1) * rows, :]
        out = mid_ref[g] + added[g * rows:(g + 1) * rows]
        if leaving:
            live = pl.program_id(0) * images + g < ids_ref[2]
            out_ref[g] = jnp.where(live, out[:length], 0.0).astype(BF)
        else:
            out_ref[g] = out.astype(BF)


def mlp_bwd_kernel(length, count, entering, entry_ready, ids_ref, *refs):
    if entering:
        own_ref, came_ref, *refs = refs
        *refs, pad_s = refs
    else:
        cot_ref, *refs = refs
    mid_ref, act_ref, slope_ref, up_ref, down_ref, gmid_ref, keep_ref, send_ref, *refs = refs
    up_acc, down_acc, entry_s, cot_s, gh_s = refs
    images, rows, width = mid_ref.shape
    step_id = pl.program_id(0)

    @pl.when(step_id == 0)
    def _():
        up_acc[...] = jnp.zeros_like(up_acc)
        down_acc[...] = jnp.zeros_like(down_acc)
        if entering:
            pad_s[...] = jnp.zeros_like(pad_s)

    hidden_width = up_ref.shape[1]
    step = 512
    gain = gain_of(up_ref, width)
    for g in range(images):
        if entering:
            live = step_id * images + g < ids_ref[2]
            came = jnp.where(ids_ref[0] == 0, came_ref[g].astype(F32), own_ref[g].astype(F32))
            pad_s[:length, :] = jnp.where(live, came, 0.0)
            cot_s[g * rows:(g + 1) * rows, :] = pad_s[...].astype(BF)
        else:
            cot_s[g * rows:(g + 1) * rows, :] = cot_ref[g]
        if not entry_ready:
            normed, _ = norm_rows(mid_ref[g])
            entry_s[g * rows:(g + 1) * rows, :] = (normed * gain).astype(BF)
    for at in range(0, hidden_width, step):
        tile = slice(at, at + step)
        grad_act = dot_nt(cot_s[...], down_ref[tile, :])
        slope = slope_ref[:, :, tile].reshape(images * rows, step)
        gh_s[:, tile] = (grad_act * slope.astype(F32)).astype(BF)
    down_acc[...] += dot_tn(cot_s[...], act_ref[...].reshape(images * rows, hidden_width))
    up_acc[...] += dot_tn(entry_s[...], gh_s[...])
    grad_entry = dot_nt(gh_s[...], up_ref[:width, :])
    for g in range(images):
        normed, scale = norm_rows(mid_ref[g])
        back = norm_rows_back(grad_entry[g * rows:(g + 1) * rows] * gain, normed, scale)
        gmid_ref[g] = cot_s[g * rows:(g + 1) * rows, :].astype(F32) + back

    @pl.when(step_id == pl.num_programs(0) - 1)
    def _():
        depth = width // count
        tall = hidden_width // count
        for section in range(2):
            @pl.when(ids_ref[0] == section)
            def _():
                for k in range(count):
                    shard = ids_ref[1] ^ k
                    at = pl.ds(pl.multiple_of(shard * depth, depth), depth)
                    up_out, down_out = (keep_ref, send_ref) if section == 0 else (send_ref, keep_ref)
                    for b in range(hidden_width // width):
                        up_out[k, b * depth:(b + 1) * depth, :] = up_acc[at, b * width:(b + 1) * width].astype(BF)
                    for j in range(0, tall, 128):
                        lanes = pl.ds(pl.multiple_of(shard * tall + j, 128), 128)
                        down_out[k, j:j + 128, :] = down_acc[:, lanes].T.astype(BF)


def attn_bwd_kernel(length, count, leaving, carried, final, ids_ref, gmid_ref, x_ref, qkv_ref, probs_ref, mixed_ref,
                    weight_ref, *refs, entry_ready=False):
    if carried:
        begun_ref, *refs = refs
    if final:
        gx_ref, keep_ref, send_ref, acc, *refs = refs
    else:
        gx_ref, acc, *refs = refs
    joint_s, entry_s, low_s, grad_mixed_s, grad_probs_s, grad_scores_s = refs
    images, rows, width = x_ref.shape
    step_id = pl.program_id(0)

    @pl.when(step_id == 0)
    def _():
        acc[...] = begun_ref[...] if carried else jnp.zeros_like(acc)

    lane = lax.broadcasted_iota(jnp.int32, (rows, PAIR), 1)
    gain = gain_of(weight_ref, width)
    for g in range(images):
        low_s[g * rows:(g + 1) * rows, :] = gmid_ref[g].astype(BF)
        if not entry_ready:
            normed, _ = norm_rows(x_ref[g].astype(F32))
            entry_s[g * rows:(g + 1) * rows, :] = (normed * gain).astype(BF)
    acc[:, 3 * width:] += dot_tn(mixed_ref[...].reshape(images * rows, width), low_s[...])
    grad_mixed_s[...] = dot_nt(low_s[...], weight_ref[:width, 3 * width:]).astype(BF)

    def own_half(g, head):
        gm = grad_mixed_s[g * rows:(g + 1) * rows, head // 2 * PAIR:head // 2 * PAIR + PAIR]
        return jnp.where((lane // HEAD_DIM) == head % 2, gm, jnp.zeros_like(gm))

    def fill_grad_probs(g):
        for head in range(HEADS):
            at = 2 * width + head // 2 * PAIR
            grad_probs_s[g % 2 * HEADS + head, :, :rows] = dot_nt(qkv_ref[g, :, at:at + PAIR], own_half(g, head))

    def fill_grad_scores(g):
        for head in range(HEADS):
            for lo in range(0, rows, 128):
                hi = min(lo + 128, rows)
                probs = probs_ref[g, head, :, lo:hi].astype(F32)
                grad_probs = grad_probs_s[g % 2 * HEADS + head, :, lo:hi]
                delta = jnp.sum(probs * grad_probs, axis=0, keepdims=True)
                grad_scores_s[head, :, lo:hi] = (probs * (grad_probs - delta)).astype(BF)

    def fill_joint(g):
        own_rows = slice(g * rows, (g + 1) * rows)
        for pair in range(HEADS // 2):
            at = pair * PAIR
            q = qkv_ref[g, :, at:at + PAIR] * 0.125
            k_t = (qkv_ref[g, :, width + at:width + at + PAIR] * 0.125).T
            grad_k = None
            grad_v = None
            grad_q_t = []
            for side in range(2):
                head = pair * 2 + side
                q_own = jnp.where((lane // HEAD_DIM) == side, q, jnp.zeros_like(q))
                part_v = dot_nn(probs_ref[g, head], own_half(g, head))
                part_k = dot_nn(grad_scores_s[head], q_own)
                grad_v = part_v if grad_v is None else grad_v + part_v
                grad_k = part_k if grad_k is None else grad_k + part_k
                grad_q_t.append(dot_nn(k_t[side * HEAD_DIM:(side + 1) * HEAD_DIM], grad_scores_s[head]))
            joint_s[own_rows, at:at + PAIR] = jnp.concatenate(grad_q_t, axis=0).astype(BF).T
            joint_s[own_rows, width + at:width + at + PAIR] = grad_k.astype(BF)
            joint_s[own_rows, 2 * width + at:2 * width + at + PAIR] = grad_v.astype(BF)

    fill_grad_probs(0)
    for g in range(images):
        if g + 1 < images:
            fill_grad_probs(g + 1)
        fill_grad_scores(g)
        fill_joint(g)
    acc[:, :3 * width] += dot_tn(entry_s[...], joint_s[...])
    grad_entry = dot_nt(joint_s[...], weight_ref[:width, :3 * width])
    for g in range(images):
        normed, scale = norm_rows(x_ref[g].astype(F32))
        grad_x = gmid_ref[g] + norm_rows_back(grad_entry[g * rows:(g + 1) * rows] * gain, normed, scale)
        gx_ref[g] = (grad_x[:length] if leaving else grad_x).astype(BF)

    if not final:
        return

    @pl.when(step_id == pl.num_programs(0) - 1)
    def _():
        depth = width // count
        for section in range(2):
            @pl.when(ids_ref[0] == section)
            def _():
                for k in range(count):
                    at = pl.ds(pl.multiple_of((ids_ref[1] ^ k) * depth, depth), depth)
                    for half, out_ref in ((section, keep_ref), (1 - section, send_ref)):
                        for b in range(2):
                            lanes = (2 * half + b) * width
                            out_ref[k, b * depth:(b + 1) * depth, :] = acc[at, lanes:lanes + width].astype(BF)


def call(body, name, ids, images, entering, streams, fixed, stream_outs, fixed_outs, scratch, flops, start=0, g=PER_STEP):
    g = g if images % g == 0 else 1

    def entering_spec(shape):
        return pl.BlockSpec((g,) + shape[1:], lambda i, ids: (ids[0] * (images // g) + i,) + (0,) * (len(shape) - 1))

    def per_image(shape, at=0):
        return pl.BlockSpec((g,) + shape[1:], lambda i, ids: (i + at // g,) + (0,) * (len(shape) - 1))

    def whole(shape, **more):
        return pl.BlockSpec(shape, lambda i, ids: (0,) * len(shape), **more)

    outs = [jax.ShapeDtypeStruct(s, d) for s, d in stream_outs + fixed_outs]
    moved = sum(a.size * a.dtype.itemsize for a in list(streams) + list(fixed) + outs)
    return pl.pallas_call(
        body,
        name=name,
        grid_spec=pltpu.PrefetchScalarGridSpec(
            num_scalar_prefetch=1,
            grid=(images // g,),
            in_specs=[entering_spec(a.shape) for a in entering] + [per_image(a.shape, start) for a in streams]
            + [whole(a.shape, pipeline_mode=pl.Buffered(1)) for a in fixed],
            out_specs=[per_image(s) for s, _ in stream_outs] + [whole(s) for s, _ in fixed_outs],
            scratch_shapes=scratch(g),
        ),
        out_shape=outs,
        compiler_params=pltpu.CompilerParams(vmem_limit_bytes=VMEM_LIMIT, dimension_semantics=("arbitrary",)),
        cost_estimate=pl.CostEstimate(flops=int(flops), bytes_accessed=int(moved), transcendentals=0),
    )(ids, *entering, *streams, *fixed)


def attn_fwd(ids, x, pieces, dims, entering):
    n, rows, length, width, ff = dims
    count = len(pieces) // 2
    outs = [((n, rows, 3 * width), BF), ((n, HEADS, rows, rows), BF), ((n, rows, width), BF), ((n, rows, width), F32)]
    fixed_outs = [((width + GAIN_ROWS, 4 * width), BF)]
    body = functools.partial(attn_fwd_kernel, length, count, entering)

    def scratch(g):
        refs = [pltpu.VMEM((g * rows, width), BF), pltpu.VMEM((g * rows, 3 * width), BF),
                pltpu.VMEM((min(g, 2) * HEADS, rows, -(-rows // 128) * 128), F32)]
        return refs + ([pltpu.VMEM((g, rows, width), F32)] if entering else [])

    flops = 2 * n * rows * width * 4 * width + 4 * n * rows * rows * width
    if entering:
        def reordered(ids_ref, *refs):
            ins, rest = refs[:2 + 2 * count], refs[2 + 2 * count:]
            qkv, probs, mixed, mid, xp, weight, *scr = rest
            body(ids_ref, *ins, qkv, probs, mixed, mid, weight, xp, *scr)
        return call(reordered, "attention_forward", ids, n, x, [], pieces, outs + [((n, rows, width), BF)], fixed_outs,
                    scratch, flops)
    qkv, probs, mixed, mid, weight = call(body, "attention_forward", ids, n, [], [x], pieces, outs, fixed_outs, scratch, flops)
    return qkv, probs, mixed, mid, x, weight


def mlp_fwd(ids, mid, pieces, dims, leaving):
    n, rows, length, width, ff = dims
    count = len(pieces) // 2
    return call(
        functools.partial(mlp_fwd_kernel, length, count, leaving), "mlp_forward", ids, n, [], [mid], pieces,
        [((n, length if leaving else rows, width), BF), ((n, rows, ff), BF), ((n, rows, ff), BF)],
        [((width + GAIN_ROWS, ff), BF), ((ff, width), BF)],
        lambda g: [pltpu.VMEM((g * rows, width), BF), pltpu.VMEM((g * rows, ff), BF)],
        4 * n * rows * width * ff)


def mlp_bwd(ids, cot, mid, act, slope, up, down, dims, count, entering):
    n, rows, length, width, ff = dims

    def scratch(g):
        refs = [pltpu.VMEM((width, ff), F32), pltpu.VMEM((width, ff), F32), pltpu.VMEM((g * rows, width), BF),
                pltpu.VMEM((g * rows, width), BF), pltpu.VMEM((g * rows, ff), BF)]
        return refs + ([pltpu.VMEM((rows, width), F32)] if entering else [])

    half = (count, ff // count, width)
    return call(
        functools.partial(mlp_bwd_kernel, length, count, entering, False), "mlp_backward", ids, n,
        cot if entering else [], ([] if entering else [cot]) + [mid, act, slope], [up, down],
        [((n, rows, width), F32)], [(half, BF), (half, BF)], scratch, 8 * n * rows * width * ff)


def attn_bwd(ids, streams, weight, dims, count, leaving, span, begun=None, final=True):
    n, rows, length, width, ff = dims
    low, high = span
    half = (count, 2 * width // count, width)
    acc = ((width, 4 * width), F32)
    return call(
        functools.partial(attn_bwd_kernel, length, count, leaving, begun is not None, final), "attention_backward",
        ids, high - low, [], streams, [weight] + ([] if begun is None else [begun]),
        [((high - low, length if leaving else rows, width), BF)], [(half, BF), (half, BF)] if final else [acc],
        lambda g: ([pltpu.VMEM(*acc)] if final else []) + [pltpu.VMEM((g * rows, 3 * width), BF)]
        + [pltpu.VMEM((g * rows, width), BF)] * 3 + [
            pltpu.VMEM((min(g, 2) * HEADS, rows, -(-rows // 128) * 128), F32), pltpu.VMEM((HEADS, rows, rows), BF)],
        (high - low) * (4 * rows * width * 4 * width + 10 * rows * rows * width), start=low)


def middle_kernel(length, count, ids_ref, own_ref, came_ref, x_ref, *refs):
    attn, mlp, refs = refs[:2 * count], refs[2 * count:4 * count], refs[4 * count:]
    out_ref, cot_ref, keep_m_ref, send_m_ref, keep_a_ref, send_a_ref, *refs = refs
    entry_s, qkv_s, scores_s, mid_s, act_s, slope_s, up_s, down_s, up_acc, down_acc, cot_s, gh_s, pad_s, *refs = refs
    qkv3_s, probs_s, mixed_s, weight_s, gmid_s, acc, grad_mixed_s, entry_a_s, grad_scores_s = refs
    skip = down_s.shape[0] // count + GAIN_ROWS
    attn = rows_at(attn, skip, attn[0].shape[0])
    attn_fwd_kernel(length, count, False, ids_ref, x_ref, *attn, qkv3_s, probs_s, mixed_s, mid_s, weight_s,
                    entry_a_s, qkv_s, scores_s)
    mlp_fwd_kernel(length, count, True, ids_ref, mid_s, *mlp, out_ref, act_s, slope_s, up_s, down_s, entry_s, gh_s)
    mlp_bwd_kernel(length, count, True, True, ids_ref, own_ref, came_ref, mid_s, act_s, slope_s, up_s, down_s, gmid_s,
                   keep_m_ref, send_m_ref, up_acc, down_acc, entry_s, cot_s, gh_s, pad_s)
    attn_bwd_kernel(length, count, False, False, True, ids_ref, gmid_s, x_ref, qkv3_s, probs_s, mixed_s, weight_s,
                    cot_ref, keep_a_ref, send_a_ref, acc, qkv_s, entry_a_s, cot_s, grad_mixed_s, scores_s, grad_scores_s, entry_ready=True)


def middle(ids, cots, x, attn, mlp, dims):
    n, rows, length, width, ff = dims
    count = len(attn) // 2
    half_m = (count, ff // count, width)
    half_a = (count, 2 * width // count, width)

    def scratch(g):
        tokens = g * rows
        return [pltpu.VMEM((tokens, width), BF), pltpu.VMEM((tokens, 3 * width), BF),
                pltpu.VMEM((min(g, 2) * HEADS, rows, -(-rows // 128) * 128), F32), pltpu.VMEM((g, rows, width), F32),
                pltpu.VMEM((g, rows, ff), BF), pltpu.VMEM((g, rows, ff), BF), pltpu.VMEM((width + GAIN_ROWS, ff), BF),
                pltpu.VMEM((ff, width), BF), pltpu.VMEM((width, ff), F32), pltpu.VMEM((width, ff), F32),
                pltpu.VMEM((tokens, width), BF), pltpu.VMEM((tokens, ff), BF), pltpu.VMEM((rows, width), F32),
                pltpu.VMEM((g, rows, 3 * width), BF), pltpu.VMEM((g, HEADS, rows, rows), BF),
                pltpu.VMEM((g, rows, width), BF), pltpu.VMEM((width + GAIN_ROWS, 4 * width), BF),
                pltpu.VMEM((g, rows, width), F32), pltpu.VMEM((width, 4 * width), F32),
                pltpu.VMEM((tokens, width), BF), pltpu.VMEM((tokens, width), BF), pltpu.VMEM((HEADS, rows, rows), BF)]

    return call(
        functools.partial(middle_kernel, length, count), "middle", ids, n, cots, [x], attn + mlp,
        [((n, length, width), BF), ((n, rows, width), BF)], [(half_m, BF), (half_m, BF), (half_a, BF), (half_a, BF)], scratch,
        n * rows * width * (24 * width + 12 * ff + 14 * rows), g=MIDDLE_STEP)


def swap_section(value):
    return lax.ppermute(value, "section", [(0, 1), (1, 0)])


def pick(stack, index):
    return lax.dynamic_index_in_dim(stack, index, 0, keepdims=False)


def tie(*values):
    return lax.optimization_barrier(values)


def exchange(values, axis):
    size = lax.axis_size(axis)
    return [lax.ppermute(v, axis, [(i, i ^ (k + 1)) for i in range(size)]) for k, v in enumerate(values)]


def direct(size):
    return size & (size - 1) == 0 and size <= MOST_PIECES


def total(first, others):
    result = first.astype(F32)
    for other in others:
        result = result + other.astype(F32)
    return result.astype(BF)


def local(ends_in, live, gain_attn, w_qkv, w_out, gain_mlp, w_up, w_down):
    me = lax.axis_index("section")
    mine_at = lax.axis_index("fsdp")
    first = me == 0
    shards = lax.axis_size("fsdp")
    replicas = lax.axis_size("replica")
    slots, length, width = ends_in.shape[1:]
    share = slots // 2
    rows = -(-length // 16) * 16
    depth = w_qkv.shape[1]
    ff = w_up.shape[2]
    ratio = ff // width
    dims = (share, rows, length, width, ff)
    packed = direct(shards) and depth % 16 == 0
    count = shards if packed else 1

    live_here = pick(live[:, 0], me)
    ids = jnp.stack([me, mine_at if packed else jnp.zeros_like(mine_at), live_here]).astype(jnp.int32)

    def columns(matrix):
        return matrix.reshape(depth, -1, width).transpose(1, 0, 2).reshape(-1, width)

    def halves(gain, first_half, second_half):
        row = lax.dynamic_update_slice(jnp.zeros((GAIN_ROWS, width), BF), gain, (0, mine_at * depth))
        return jnp.stack([jnp.concatenate([first_half, row]), jnp.concatenate([second_half, row])])

    qkv_own = columns(w_qkv[0])
    attn_own = halves(gain_attn, qkv_own[:2 * depth], jnp.concatenate([qkv_own[2 * depth:], w_out[0]]))
    mlp_own = halves(gain_mlp, columns(w_up[0]), w_down[0])

    def by_layer(own):
        kept, came = pick(own, me), swap_section(pick(own, 1 - me))
        return jnp.where(first, kept, came), jnp.where(first, came, kept)

    def spread(half):
        return [half] + exchange([half] * (shards - 1), "fsdp")

    def whole(half, mlp):
        full = lax.all_gather(half, "fsdp")
        gains = jnp.sum(full[:, -GAIN_ROWS:].astype(F32), axis=0).astype(BF)
        full = full[:, :-GAIN_ROWS]
        blocks = full.reshape(shards, -1, depth, width).transpose(1, 0, 2, 3).reshape(-1, width)
        if mlp:
            blocks = jnp.where(first, blocks, full.reshape(-1, width))
        return jnp.concatenate([blocks, gains])

    attn0, attn1 = by_layer(attn_own)
    mlp0, mlp1 = by_layer(mlp_own)
    came_images = swap_section(ends_in[0])
    images = [ends_in[0], came_images]
    attn0 = spread(attn0) if packed else [whole(attn0, False)]
    attn0 = attn0 + [swap_section(p) for p in attn0]

    *tied, attn1, mlp0 = tie(*attn0, attn1, mlp0)
    attn0 = tied
    if packed:
        both = spread(jnp.concatenate([mlp0, attn1]))
    else:
        both = [jnp.concatenate([whole(mlp0, True), whole(attn1, False)])]
    qkv0, probs0, mixed0, mid0, x0, weight0 = attn_fwd(ids, images, attn0, dims, True)

    mid0, mlp1, *both = tie(mid0, mlp1, *both)
    both = both + [swap_section(p) for p in both]
    mlp1 = spread(mlp1) if packed else [whole(mlp1, True)]
    x1, act0, slope0, up0, down0 = mlp_fwd(ids, mid0, both, dims, False)

    x1, *mlp1 = tie(x1, *mlp1)
    mlp1 = mlp1 + [swap_section(p) for p in mlp1]
    out, cot0, keep_m1, send_m1, keep_a1, send_a1 = middle(ids, images, x1, both, mlp1, dims)

    def scatter(half, came, mlp):
        if packed:
            parts = [total(half[k], [came[k]]) for k in range(count)]
            return [parts[0]] + exchange(parts[1:], "fsdp")
        chip = total(half, [came])
        blocks = chip.reshape(-1, shards, depth, width).transpose(1, 0, 2, 3).reshape(shards, -1, width)
        if mlp:
            blocks = jnp.where(first, blocks, chip.reshape(shards, -1, width))
        return [lax.psum_scatter(blocks, "fsdp", scatter_dimension=0)]

    def added(parts):
        return total(parts[0], parts[1:])

    line = replicas == 4
    at_z = lax.axis_index("replica")

    def inwards(part):
        return [part, lax.ppermute(part, "replica", [(0, 1), (3, 2)])] if line else [lax.psum(part, "replica")]

    def across(part):
        return [part, lax.ppermute(part, "replica", [(1, 2), (2, 1)])] if line else [part]

    def outwards(part):
        return [part, lax.ppermute(part, "replica", [(1, 0), (2, 3)])] if line else [part]

    def settled(parts):
        return jnp.where((at_z == 0) | (at_z == 3), parts[1], parts[0]) if line else parts[0]

    def doubled(part, k):
        return [part, lax.ppermute(part, "replica", [(i, i ^ k) for i in range(replicas)])]

    def tied_lists(lists, *values):
        flat = tie(*values, *[member for group in lists for member in group])
        values, flat = flat[:len(values)], flat[len(values):]
        groups = []
        for group in lists:
            groups.append(list(flat[:len(group)]))
            flat = flat[len(group):]
        return groups, values

    came_m1 = swap_section(send_m1)
    came_out = swap_section(out)
    came_a1 = swap_section(send_a1)
    gmid0, keep_m0, send_m0 = mlp_bwd(ids, cot0, mid0, act0, slope0, up0, down0, dims, count, False)

    gmid0, came_a1, keep_a1, came_m1, keep_m1, came_out = tie(gmid0, came_a1, keep_a1, came_m1, keep_m1, came_out)
    if packed:
        l1 = scatter(jnp.concatenate([keep_m1, keep_a1], 1), jnp.concatenate([came_m1, came_a1], 1), True)
    else:
        l1 = [jnp.concatenate([scatter(keep_m1, came_m1, True)[0], scatter(keep_a1, came_a1, False)[0]])]
    came_m0 = swap_section(send_m0)
    early = (share // 2 + 1) // PER_STEP * PER_STEP
    saved = [gmid0, x0, qkv0, probs0, mixed0]
    gx_early, begun = attn_bwd(ids, saved, weight0, dims, count, True, (0, early), final=False)

    (l1,), (begun, gx_early, came_m0, keep_m0) = tied_lists([l1], begun, gx_early, came_m0, keep_m0)
    m0 = scatter(keep_m0, came_m0, True)
    l1 = inwards(added(l1))
    came_gx_early = swap_section(gx_early)
    gx_late, keep_a0, send_a0 = attn_bwd(ids, saved, weight0, dims, count, True, (early, share), begun)

    (l1, m0), (send_a0, keep_a0, gx_late, came_gx_early) = tied_lists([l1, m0], send_a0, keep_a0, gx_late, came_gx_early)
    came_a0 = swap_section(send_a0)
    l1 = across(added(l1))
    m0 = inwards(added(m0))
    came_gx_late = swap_section(gx_late)
    a0 = scatter(keep_a0, came_a0, False)
    m0 = across(added(m0))
    l1 = outwards(added(l1))
    (a0, m0), _ = tied_lists([a0, m0])
    a0 = doubled(added(a0), 1) if line else [lax.psum(added(a0), "replica")]
    m0 = outwards(added(m0))
    a0 = doubled(added(a0), 3) if line else a0
    (a0, m0, l1), _ = tied_lists([a0, m0, l1])
    l1 = settled(l1)
    m0 = settled(m0)
    m1, a1 = l1[:ff // width * depth], l1[ff // width * depth:]
    gx = jnp.concatenate([gx_early, gx_late])
    came_gx = jnp.concatenate([came_gx_early, came_gx_late])

    def own_layer(sum0, sum1):
        mine = jnp.where(first, sum0, sum1)
        other = swap_section(jnp.where(first, sum1, sum0))
        return jnp.concatenate([jnp.where(first, mine, other), jnp.where(first, other, mine)]).astype(F32)

    mlp_grad = own_layer(m0, m1)
    attn_grad = own_layer(added(a0), a1)

    def rows_of(blocks):
        return blocks.reshape(-1, depth, width).transpose(1, 0, 2).reshape(depth, -1)

    grad_qkv, grad_out = rows_of(attn_grad[:3 * depth])[None], attn_grad[3 * depth:][None]
    grad_up, grad_down = rows_of(mlp_grad[:ratio * depth])[None], mlp_grad[ratio * depth:][None]
    grad_gain_attn = jnp.sum(grad_qkv * w_qkv.astype(F32), axis=-1) / gain_attn.astype(F32)
    grad_gain_mlp = jnp.sum(grad_up * w_up.astype(F32), axis=-1) / gain_mlp.astype(F32)

    own = jnp.where(first, gx, out)
    came = jnp.where(first, came_gx, came_out)
    ends_out = jnp.where(first, jnp.concatenate([own, came]), jnp.concatenate([came, own]))
    return (ends_out[None], grad_gain_attn, grad_qkv, grad_out, grad_gain_mlp, grad_up, grad_down)


def solution(mesh):
    in_specs = (
        P("section", ("fsdp", "replica"), None, None),
        P(None, ("fsdp", "replica")),
        P("section", "fsdp"),
        P("section", "fsdp", None),
        P("section", "fsdp", None),
        P("section", "fsdp"),
        P("section", "fsdp", None),
        P("section", "fsdp", None),
    )
    out_specs = (
        P("section", ("fsdp", "replica"), None, None),
        P("section", "fsdp"),
        P("section", "fsdp", None),
        P("section", "fsdp", None),
        P("section", "fsdp"),
        P("section", "fsdp", None),
        P("section", "fsdp", None),
    )
    return jax.shard_map(local, mesh=mesh, in_specs=in_specs, out_specs=out_specs, check_vma=False)
```

```python
import functools

import jax
import jax.numpy as jnp
from jax import lax
from jax.experimental import pallas as pl
from jax.experimental.pallas import tpu as pltpu
from jax.sharding import PartitionSpec as P

HEADS = 6
HEAD_DIM = 64
PAIR = 2 * HEAD_DIM
EPS = 1e-06
BF = jnp.bfloat16
F32 = jnp.float32
VMEM_LIMIT = 56 * 1024 * 1024
PER_STEP = 2
MIDDLE_STEP = 2
GAIN_ROWS = 16
MOST_PIECES = 8


def dot_nn(a, b):
    return lax.dot_general(a, b, (((1,), (0,)), ((), ())), preferred_element_type=F32)


def dot_nt(a, b):
    return lax.dot_general(a, b, (((1,), (1,)), ((), ())), preferred_element_type=F32)


def dot_tn(a, b):
    return lax.dot_general(a, b, (((0,), (0,)), ((), ())), preferred_element_type=F32)


def norm_rows(values):
    centered = values - jnp.mean(values, axis=-1, keepdims=True)
    scale = lax.rsqrt(jnp.mean(centered * centered, axis=-1, keepdims=True) + EPS)
    return centered * scale, scale


def norm_rows_back(grad_normed, normed, scale):
    first = jnp.mean(grad_normed, axis=-1, keepdims=True)
    second = jnp.mean(grad_normed * normed, axis=-1, keepdims=True)
    return scale * (grad_normed - first - normed * second)


def gelu_both(v):
    cdf = 0.5 * (1.0 + lax.erf(v * 0.7071067811865476))
    density = jnp.exp(-0.5 * v * v) * 0.3989422804014327
    return v * cdf, cdf + v * density


def gain_of(weight_ref, width):
    return weight_ref[width:width + GAIN_ROWS, :width].astype(F32)[:1]


def place_gain(pieces, weight_ref, width):
    last = pieces[0].shape[0] - GAIN_ROWS
    rows = sum(piece[last:last + GAIN_ROWS, :].astype(F32) for piece in pieces)
    weight_ref[width:width + GAIN_ROWS, :width] = rows.astype(BF)


def place_attn(ids_ref, pieces, weight_ref):
    count = len(pieces) // 2
    width = weight_ref.shape[1] // 4
    place_gain(pieces[:count], weight_ref, width)
    depth = width // count
    for section in range(2):
        @pl.when(ids_ref[0] == section)
        def _():
            for k in range(count):
                at = pl.ds(pl.multiple_of((ids_ref[1] ^ k) * depth, depth), depth)
                for half, piece in ((section, pieces[k]), (1 - section, pieces[count + k])):
                    for b in range(2):
                        lanes = (2 * half + b) * width
                        weight_ref[at, lanes:lanes + width] = piece[b * depth:(b + 1) * depth, :]


def place_mlp(ids_ref, pieces, up_ref, down_ref):
    count = len(pieces) // 2
    hidden, width = down_ref.shape
    place_gain(pieces[:count], up_ref, width)
    depth = width // count
    tall = hidden // count
    for section in range(2):
        @pl.when(ids_ref[0] == section)
        def _():
            for k in range(count):
                shard = ids_ref[1] ^ k
                at = pl.ds(pl.multiple_of(shard * depth, depth), depth)
                for half, piece in ((section, pieces[k]), (1 - section, pieces[count + k])):
                    if half == 0:
                        for b in range(hidden // width):
                            up_ref[at, b * width:(b + 1) * width] = piece[b * depth:(b + 1) * depth, :]
                    else:
                        down_ref[pl.ds(pl.multiple_of(shard * tall, tall), tall), :] = piece[:tall, :]


def attn_fwd_kernel(length, count, entering, ids_ref, *refs):
    if entering:
        own_ref, came_ref = refs[:2]
        pieces, refs = refs[2:2 + 2 * count], refs[2 + 2 * count:]
        qkv_ref, probs_ref, mixed_ref, mid_ref, weight_ref, x_ref, entry_s, qkv_s, scores_s, pad_s = refs
    else:
        x_ref = refs[0]
        pieces, refs = refs[1:1 + 2 * count], refs[1 + 2 * count:]
        qkv_ref, probs_ref, mixed_ref, mid_ref, weight_ref, entry_s, qkv_s, scores_s = refs
    images, rows, width = x_ref.shape

    @pl.when(pl.program_id(0) == 0)
    def _():
        place_attn(ids_ref, pieces, weight_ref)
        if entering:
            pad_s[...] = jnp.zeros_like(pad_s)

    gain = gain_of(weight_ref, width)
    for g in range(images):
        if entering:
            pad_s[g, :length, :] = jnp.where(ids_ref[0] == 0, own_ref[g].astype(F32), came_ref[g].astype(F32))
            values = pad_s[g]
            x_ref[g] = values.astype(BF)
        else:
            values = x_ref[g].astype(F32)
        normed, _ = norm_rows(values)
        entry_s[g * rows:(g + 1) * rows, :] = (normed * gain).astype(BF)
    qkv_s[...] = dot_nn(entry_s[...], weight_ref[:width, :3 * width]).astype(BF)
    lane = lax.broadcasted_iota(jnp.int32, (rows, PAIR), 1)
    cut = (length // 8) * 8

    def fill_scores(g):
        own_rows = slice(g * rows, (g + 1) * rows)
        for head in range(HEADS):
            at = head // 2 * PAIR
            q = qkv_s[own_rows, at:at + PAIR] * 0.125
            q = jnp.where((lane // HEAD_DIM) == head % 2, q, jnp.zeros_like(q))
            scores_s[g % 2 * HEADS + head, :, :rows] = dot_nt(qkv_s[own_rows, width + at:width + at + PAIR], q)

    def fill_probs(g):
        for head in range(HEADS):
            for lo in range(0, rows, 128):
                hi = min(lo + 128, rows)
                scores = scores_s[g % 2 * HEADS + head, :, lo:hi]
                tail_row = lax.broadcasted_iota(jnp.int32, (rows - cut, hi - lo), 0) + cut
                scores = jnp.concatenate([scores[:cut], jnp.where(tail_row < length, scores[cut:], -1e30)], axis=0)
                parts = jnp.exp(scores - jnp.max(scores, axis=0, keepdims=True))
                inv = 1.0 / jnp.sum(parts, axis=0, keepdims=True)
                probs_ref[g, head, :, lo:hi] = (parts * inv).astype(BF)

    def fill_mixed(g):
        own_rows = slice(g * rows, (g + 1) * rows)
        for pair in range(HEADS // 2):
            at = pair * PAIR
            v_t = qkv_s[own_rows, 2 * width + at:2 * width + at + PAIR].T
            mixed = [dot_nn(v_t[side * HEAD_DIM:(side + 1) * HEAD_DIM], probs_ref[g, pair * 2 + side]) for side in range(2)]
            mixed_ref[g, :, at:at + PAIR] = jnp.concatenate(mixed, axis=0).astype(BF).T

    fill_scores(0)
    for g in range(images):
        qkv_ref[g] = qkv_s[g * rows:(g + 1) * rows, :]
        if g + 1 < images:
            fill_scores(g + 1)
        fill_probs(g)
        fill_mixed(g)
    added = dot_nn(mixed_ref[...].reshape(images * rows, width), weight_ref[:width, 3 * width:])
    for g in range(images):
        mid_ref[g] = x_ref[g].astype(F32) + added[g * rows:(g + 1) * rows]


def rows_at(pieces, low, high):
    return [piece.at[low:high, :] for piece in pieces]


def mlp_fwd_kernel(length, count, leaving, ids_ref, mid_ref, *refs):
    pieces, refs = refs[:2 * count], refs[2 * count:]
    pieces = rows_at(pieces, 0, refs[4].shape[0] // count + GAIN_ROWS)
    out_ref, act_ref, slope_ref, up_ref, down_ref, entry_s, act_s = refs
    images, rows, width = mid_ref.shape
    hidden_width = up_ref.shape[1]

    @pl.when(pl.program_id(0) == 0)
    def _():
        place_mlp(ids_ref, pieces, up_ref, down_ref)

    gain = gain_of(up_ref, width)
    for g in range(images):
        normed, _ = norm_rows(mid_ref[g])
        entry_s[g * rows:(g + 1) * rows, :] = (normed * gain).astype(BF)
    step = 256
    for at in range(0, hidden_width, step):
        hidden = dot_nn(entry_s[...], up_ref[:width, at:at + step])
        act, slope = gelu_both(hidden)
        act_s[:, at:at + step] = act.astype(BF)
        for g in range(images):
            slope_ref[g, :, at:at + step] = slope[g * rows:(g + 1) * rows].astype(BF)
    added = dot_nn(act_s[...], down_ref[...])
    for g in range(images):
        act_ref[g] = act_s[g * rows:(g + 1) * rows, :]
        out = mid_ref[g] + added[g * rows:(g + 1) * rows]
        if leaving:
            live = pl.program_id(0) * images + g < ids_ref[2]
            out_ref[g] = jnp.where(live, out[:length], 0.0).astype(BF)
        else:
            out_ref[g] = out.astype(BF)


def mlp_bwd_kernel(length, count, entering, entry_ready, ids_ref, *refs):
    if entering:
        own_ref, came_ref, *refs = refs
        *refs, pad_s = refs
    else:
        cot_ref, *refs = refs
    mid_ref, act_ref, slope_ref, up_ref, down_ref, gmid_ref, keep_ref, send_ref, *refs = refs
    up_acc, down_acc, entry_s, cot_s, gh_s = refs
    images, rows, width = mid_ref.shape
    step_id = pl.program_id(0)

    @pl.when(step_id == 0)
    def _():
        up_acc[...] = jnp.zeros_like(up_acc)
        down_acc[...] = jnp.zeros_like(down_acc)
        if entering:
            pad_s[...] = jnp.zeros_like(pad_s)

    hidden_width = up_ref.shape[1]
    step = 768
    gain = gain_of(up_ref, width)
    for g in range(images):
        if entering:
            live = step_id * images + g < ids_ref[2]
            came = jnp.where(ids_ref[0] == 0, came_ref[g].astype(F32), own_ref[g].astype(F32))
            pad_s[:length, :] = jnp.where(live, came, 0.0)
            cot_s[g * rows:(g + 1) * rows, :] = pad_s[...].astype(BF)
        else:
            cot_s[g * rows:(g + 1) * rows, :] = cot_ref[g]
        if not entry_ready:
            normed, _ = norm_rows(mid_ref[g])
            entry_s[g * rows:(g + 1) * rows, :] = (normed * gain).astype(BF)
    for at in range(0, hidden_width, step):
        tile = slice(at, at + step)
        grad_act = dot_nt(cot_s[...], down_ref[tile, :])
        slope = slope_ref[:, :, tile].reshape(images * rows, step)
        gh_s[:, tile] = (grad_act * slope.astype(F32)).astype(BF)
    down_acc[...] += dot_tn(cot_s[...], act_ref[...].reshape(images * rows, hidden_width))
    up_acc[...] += dot_tn(entry_s[...], gh_s[...])
    grad_entry = dot_nt(gh_s[...], up_ref[:width, :])
    for g in range(images):
        normed, scale = norm_rows(mid_ref[g])
        back = norm_rows_back(grad_entry[g * rows:(g + 1) * rows] * gain, normed, scale)
        gmid_ref[g] = cot_s[g * rows:(g + 1) * rows, :].astype(F32) + back

    @pl.when(step_id == pl.num_programs(0) - 1)
    def _():
        depth = width // count
        tall = hidden_width // count
        for section in range(2):
            @pl.when(ids_ref[0] == section)
            def _():
                for k in range(count):
                    shard = ids_ref[1] ^ k
                    at = pl.ds(pl.multiple_of(shard * depth, depth), depth)
                    up_out, down_out = (keep_ref, send_ref) if section == 0 else (send_ref, keep_ref)
                    for b in range(hidden_width // width):
                        up_out[k, b * depth:(b + 1) * depth, :] = up_acc[at, b * width:(b + 1) * width].astype(BF)
                    for j in range(0, tall, 128):
                        lanes = pl.ds(pl.multiple_of(shard * tall + j, 128), 128)
                        down_out[k, j:j + 128, :] = down_acc[:, lanes].T.astype(BF)


def attn_bwd_kernel(length, count, leaving, carried, final, ids_ref, gmid_ref, x_ref, qkv_ref, probs_ref, mixed_ref,
                    weight_ref, *refs, entry_ready=False):
    if carried:
        begun_ref, *refs = refs
    if final:
        gx_ref, keep_ref, send_ref, acc, *refs = refs
    else:
        gx_ref, acc, *refs = refs
    joint_s, entry_s, low_s, grad_mixed_s, grad_probs_s, grad_scores_s = refs
    images, rows, width = x_ref.shape
    step_id = pl.program_id(0)

    @pl.when(step_id == 0)
    def _():
        acc[...] = begun_ref[...] if carried else jnp.zeros_like(acc)

    lane = lax.broadcasted_iota(jnp.int32, (rows, PAIR), 1)
    gain = gain_of(weight_ref, width)
    for g in range(images):
        low_s[g * rows:(g + 1) * rows, :] = gmid_ref[g].astype(BF)
        if not entry_ready:
            normed, _ = norm_rows(x_ref[g].astype(F32))
            entry_s[g * rows:(g + 1) * rows, :] = (normed * gain).astype(BF)
    acc[:, 3 * width:] += dot_tn(mixed_ref[...].reshape(images * rows, width), low_s[...])
    grad_mixed_s[...] = dot_nt(low_s[...], weight_ref[:width, 3 * width:]).astype(BF)

    def own_half(g, head):
        gm = grad_mixed_s[g * rows:(g + 1) * rows, head // 2 * PAIR:head // 2 * PAIR + PAIR]
        return jnp.where((lane // HEAD_DIM) == head % 2, gm, jnp.zeros_like(gm))

    def fill_grad_probs(g):
        for head in range(HEADS):
            at = 2 * width + head // 2 * PAIR
            grad_probs_s[g % 2 * HEADS + head, :, :rows] = dot_nt(qkv_ref[g, :, at:at + PAIR], own_half(g, head))

    def fill_grad_scores(g):
        for head in range(HEADS):
            for lo in range(0, rows, 128):
                hi = min(lo + 128, rows)
                probs = probs_ref[g, head, :, lo:hi].astype(F32)
                grad_probs = grad_probs_s[g % 2 * HEADS + head, :, lo:hi]
                delta = jnp.sum(probs * grad_probs, axis=0, keepdims=True)
                grad_scores_s[head, :, lo:hi] = (probs * (grad_probs - delta)).astype(BF)

    def fill_joint(g):
        own_rows = slice(g * rows, (g + 1) * rows)
        for pair in range(HEADS // 2):
            at = pair * PAIR
            q = qkv_ref[g, :, at:at + PAIR] * 0.125
            k_t = (qkv_ref[g, :, width + at:width + at + PAIR] * 0.125).T
            grad_k = None
            grad_v = None
            grad_q_t = []
            for side in range(2):
                head = pair * 2 + side
                q_own = jnp.where((lane // HEAD_DIM) == side, q, jnp.zeros_like(q))
                part_v = dot_nn(probs_ref[g, head], own_half(g, head))
                part_k = dot_nn(grad_scores_s[head], q_own)
                grad_v = part_v if grad_v is None else grad_v + part_v
                grad_k = part_k if grad_k is None else grad_k + part_k
                grad_q_t.append(dot_nn(k_t[side * HEAD_DIM:(side + 1) * HEAD_DIM], grad_scores_s[head]))
            joint_s[own_rows, at:at + PAIR] = jnp.concatenate(grad_q_t, axis=0).astype(BF).T
            joint_s[own_rows, width + at:width + at + PAIR] = grad_k.astype(BF)
            joint_s[own_rows, 2 * width + at:2 * width + at + PAIR] = grad_v.astype(BF)

    fill_grad_probs(0)
    for g in range(images):
        if g + 1 < images:
            fill_grad_probs(g + 1)
        fill_grad_scores(g)
        fill_joint(g)
    acc[:, :3 * width] += dot_tn(entry_s[...], joint_s[...])
    grad_entry = dot_nt(joint_s[...], weight_ref[:width, :3 * width])
    for g in range(images):
        normed, scale = norm_rows(x_ref[g].astype(F32))
        grad_x = gmid_ref[g] + norm_rows_back(grad_entry[g * rows:(g + 1) * rows] * gain, normed, scale)
        gx_ref[g] = (grad_x[:length] if leaving else grad_x).astype(BF)

    if not final:
        return

    @pl.when(step_id == pl.num_programs(0) - 1)
    def _():
        depth = width // count
        for section in range(2):
            @pl.when(ids_ref[0] == section)
            def _():
                for k in range(count):
                    at = pl.ds(pl.multiple_of((ids_ref[1] ^ k) * depth, depth), depth)
                    for half, out_ref in ((section, keep_ref), (1 - section, send_ref)):
                        for b in range(2):
                            lanes = (2 * half + b) * width
                            out_ref[k, b * depth:(b + 1) * depth, :] = acc[at, lanes:lanes + width].astype(BF)


def call(body, name, ids, images, entering, streams, fixed, stream_outs, fixed_outs, scratch, flops, start=0, g=PER_STEP):
    g = g if images % g == 0 else 1

    def entering_spec(shape):
        return pl.BlockSpec((g,) + shape[1:], lambda i, ids: (ids[0] * (images // g) + i,) + (0,) * (len(shape) - 1))

    def per_image(shape, at=0):
        return pl.BlockSpec((g,) + shape[1:], lambda i, ids: (i + at // g,) + (0,) * (len(shape) - 1))

    def whole(shape, **more):
        return pl.BlockSpec(shape, lambda i, ids: (0,) * len(shape), **more)

    outs = [jax.ShapeDtypeStruct(s, d) for s, d in stream_outs + fixed_outs]
    moved = sum(a.size * a.dtype.itemsize for a in list(streams) + list(fixed) + outs)
    return pl.pallas_call(
        body,
        name=name,
        grid_spec=pltpu.PrefetchScalarGridSpec(
            num_scalar_prefetch=1,
            grid=(images // g,),
            in_specs=[entering_spec(a.shape) for a in entering] + [per_image(a.shape, start) for a in streams]
            + [whole(a.shape, pipeline_mode=pl.Buffered(1)) for a in fixed],
            out_specs=[per_image(s) for s, _ in stream_outs] + [whole(s) for s, _ in fixed_outs],
            scratch_shapes=scratch(g),
        ),
        out_shape=outs,
        compiler_params=pltpu.CompilerParams(vmem_limit_bytes=VMEM_LIMIT, dimension_semantics=("arbitrary",)),
        cost_estimate=pl.CostEstimate(flops=int(flops), bytes_accessed=int(moved), transcendentals=0),
    )(ids, *entering, *streams, *fixed)


def attn_fwd(ids, x, pieces, dims, entering):
    n, rows, length, width, ff = dims
    count = len(pieces) // 2
    outs = [((n, rows, 3 * width), BF), ((n, HEADS, rows, rows), BF), ((n, rows, width), BF), ((n, rows, width), F32)]
    fixed_outs = [((width + GAIN_ROWS, 4 * width), BF)]
    body = functools.partial(attn_fwd_kernel, length, count, entering)

    def scratch(g):
        refs = [pltpu.VMEM((g * rows, width), BF), pltpu.VMEM((g * rows, 3 * width), BF),
                pltpu.VMEM((min(g, 2) * HEADS, rows, -(-rows // 128) * 128), F32)]
        return refs + ([pltpu.VMEM((g, rows, width), F32)] if entering else [])

    flops = 2 * n * rows * width * 4 * width + 4 * n * rows * rows * width
    if entering:
        def reordered(ids_ref, *refs):
            ins, rest = refs[:2 + 2 * count], refs[2 + 2 * count:]
            qkv, probs, mixed, mid, xp, weight, *scr = rest
            body(ids_ref, *ins, qkv, probs, mixed, mid, weight, xp, *scr)
        return call(reordered, "attention_forward", ids, n, x, [], pieces, outs + [((n, rows, width), BF)], fixed_outs,
                    scratch, flops)
    qkv, probs, mixed, mid, weight = call(body, "attention_forward", ids, n, [], [x], pieces, outs, fixed_outs, scratch, flops)
    return qkv, probs, mixed, mid, x, weight


def mlp_fwd(ids, mid, pieces, dims, leaving):
    n, rows, length, width, ff = dims
    count = len(pieces) // 2
    return call(
        functools.partial(mlp_fwd_kernel, length, count, leaving), "mlp_forward", ids, n, [], [mid], pieces,
        [((n, length if leaving else rows, width), BF), ((n, rows, ff), BF), ((n, rows, ff), BF)],
        [((width + GAIN_ROWS, ff), BF), ((ff, width), BF)],
        lambda g: [pltpu.VMEM((g * rows, width), BF), pltpu.VMEM((g * rows, ff), BF)],
        4 * n * rows * width * ff)


def mlp_bwd(ids, cot, mid, act, slope, up, down, dims, count, entering):
    n, rows, length, width, ff = dims

    def scratch(g):
        refs = [pltpu.VMEM((width, ff), F32), pltpu.VMEM((width, ff), F32), pltpu.VMEM((g * rows, width), BF),
                pltpu.VMEM((g * rows, width), BF), pltpu.VMEM((g * rows, ff), BF)]
        return refs + ([pltpu.VMEM((rows, width), F32)] if entering else [])

    half = (count, ff // count, width)
    return call(
        functools.partial(mlp_bwd_kernel, length, count, entering, False), "mlp_backward", ids, n,
        cot if entering else [], ([] if entering else [cot]) + [mid, act, slope], [up, down],
        [((n, rows, width), F32)], [(half, BF), (half, BF)], scratch, 8 * n * rows * width * ff)


def attn_bwd(ids, streams, weight, dims, count, leaving, span, begun=None, final=True):
    n, rows, length, width, ff = dims
    low, high = span
    half = (count, 2 * width // count, width)
    acc = ((width, 4 * width), F32)
    return call(
        functools.partial(attn_bwd_kernel, length, count, leaving, begun is not None, final), "attention_backward",
        ids, high - low, [], streams, [weight] + ([] if begun is None else [begun]),
        [((high - low, length if leaving else rows, width), BF)], [(half, BF), (half, BF)] if final else [acc],
        lambda g: ([pltpu.VMEM(*acc)] if final else []) + [pltpu.VMEM((g * rows, 3 * width), BF)]
        + [pltpu.VMEM((g * rows, width), BF)] * 3 + [
            pltpu.VMEM((min(g, 2) * HEADS, rows, -(-rows // 128) * 128), F32), pltpu.VMEM((HEADS, rows, rows), BF)],
        (high - low) * (4 * rows * width * 4 * width + 10 * rows * rows * width), start=low)


def middle_kernel(length, count, ids_ref, own_ref, came_ref, x_ref, *refs):
    attn, mlp, refs = refs[:2 * count], refs[2 * count:4 * count], refs[4 * count:]
    out_ref, cot_ref, keep_m_ref, send_m_ref, keep_a_ref, send_a_ref, *refs = refs
    entry_s, qkv_s, scores_s, mid_s, act_s, slope_s, up_s, down_s, up_acc, down_acc, cot_s, gh_s, pad_s, *refs = refs
    qkv3_s, probs_s, mixed_s, weight_s, gmid_s, acc, grad_mixed_s, entry_a_s, grad_scores_s = refs
    skip = down_s.shape[0] // count + GAIN_ROWS
    attn = rows_at(attn, skip, attn[0].shape[0])
    attn_fwd_kernel(length, count, False, ids_ref, x_ref, *attn, qkv3_s, probs_s, mixed_s, mid_s, weight_s,
                    entry_a_s, qkv_s, scores_s)
    mlp_fwd_kernel(length, count, True, ids_ref, mid_s, *mlp, out_ref, act_s, slope_s, up_s, down_s, entry_s, gh_s)
    mlp_bwd_kernel(length, count, True, True, ids_ref, own_ref, came_ref, mid_s, act_s, slope_s, up_s, down_s, gmid_s,
                   keep_m_ref, send_m_ref, up_acc, down_acc, entry_s, cot_s, gh_s, pad_s)
    attn_bwd_kernel(length, count, False, False, True, ids_ref, gmid_s, x_ref, qkv3_s, probs_s, mixed_s, weight_s,
                    cot_ref, keep_a_ref, send_a_ref, acc, qkv_s, entry_a_s, cot_s, grad_mixed_s, scores_s, grad_scores_s, entry_ready=True)


def middle(ids, cots, x, attn, mlp, dims):
    n, rows, length, width, ff = dims
    count = len(attn) // 2
    half_m = (count, ff // count, width)
    half_a = (count, 2 * width // count, width)

    def scratch(g):
        tokens = g * rows
        return [pltpu.VMEM((tokens, width), BF), pltpu.VMEM((tokens, 3 * width), BF),
                pltpu.VMEM((min(g, 2) * HEADS, rows, -(-rows // 128) * 128), F32), pltpu.VMEM((g, rows, width), F32),
                pltpu.VMEM((g, rows, ff), BF), pltpu.VMEM((g, rows, ff), BF), pltpu.VMEM((width + GAIN_ROWS, ff), BF),
                pltpu.VMEM((ff, width), BF), pltpu.VMEM((width, ff), F32), pltpu.VMEM((width, ff), F32),
                pltpu.VMEM((tokens, width), BF), pltpu.VMEM((tokens, ff), BF), pltpu.VMEM((rows, width), F32),
                pltpu.VMEM((g, rows, 3 * width), BF), pltpu.VMEM((g, HEADS, rows, rows), BF),
                pltpu.VMEM((g, rows, width), BF), pltpu.VMEM((width + GAIN_ROWS, 4 * width), BF),
                pltpu.VMEM((g, rows, width), F32), pltpu.VMEM((width, 4 * width), F32),
                pltpu.VMEM((tokens, width), BF), pltpu.VMEM((tokens, width), BF), pltpu.VMEM((HEADS, rows, rows), BF)]

    return call(
        functools.partial(middle_kernel, length, count), "middle", ids, n, cots, [x], attn + mlp,
        [((n, length, width), BF), ((n, rows, width), BF)], [(half_m, BF), (half_m, BF), (half_a, BF), (half_a, BF)], scratch,
        n * rows * width * (24 * width + 12 * ff + 14 * rows), g=MIDDLE_STEP)


def swap_section(value):
    return lax.ppermute(value, "section", [(0, 1), (1, 0)])


def pick(stack, index):
    return lax.dynamic_index_in_dim(stack, index, 0, keepdims=False)


def tie(*values):
    return lax.optimization_barrier(values)


def exchange(values, axis):
    size = lax.axis_size(axis)
    return [lax.ppermute(v, axis, [(i, i ^ (k + 1)) for i in range(size)]) for k, v in enumerate(values)]


def direct(size):
    return size & (size - 1) == 0 and size <= MOST_PIECES


def total(first, others):
    result = first.astype(F32)
    for other in others:
        result = result + other.astype(F32)
    return result.astype(BF)


def local(ends_in, live, gain_attn, w_qkv, w_out, gain_mlp, w_up, w_down):
    me = lax.axis_index("section")
    mine_at = lax.axis_index("fsdp")
    first = me == 0
    shards = lax.axis_size("fsdp")
    replicas = lax.axis_size("replica")
    slots, length, width = ends_in.shape[1:]
    share = slots // 2
    rows = -(-length // 16) * 16
    depth = w_qkv.shape[1]
    ff = w_up.shape[2]
    ratio = ff // width
    dims = (share, rows, length, width, ff)
    packed = direct(shards) and depth % 16 == 0
    count = shards if packed else 1

    live_here = pick(live[:, 0], me)
    ids = jnp.stack([me, mine_at if packed else jnp.zeros_like(mine_at), live_here]).astype(jnp.int32)

    def columns(matrix):
        return matrix.reshape(depth, -1, width).transpose(1, 0, 2).reshape(-1, width)

    def halves(gain, first_half, second_half):
        row = lax.dynamic_update_slice(jnp.zeros((GAIN_ROWS, width), BF), gain, (0, mine_at * depth))
        return jnp.stack([jnp.concatenate([first_half, row]), jnp.concatenate([second_half, row])])

    qkv_own = columns(w_qkv[0])
    attn_own = halves(gain_attn, qkv_own[:2 * depth], jnp.concatenate([qkv_own[2 * depth:], w_out[0]]))
    mlp_own = halves(gain_mlp, columns(w_up[0]), w_down[0])

    def by_layer(own):
        kept, came = pick(own, me), swap_section(pick(own, 1 - me))
        return jnp.where(first, kept, came), jnp.where(first, came, kept)

    def spread(half):
        return [half] + exchange([half] * (shards - 1), "fsdp")

    def whole(half, mlp):
        full = lax.all_gather(half, "fsdp")
        gains = jnp.sum(full[:, -GAIN_ROWS:].astype(F32), axis=0).astype(BF)
        full = full[:, :-GAIN_ROWS]
        blocks = full.reshape(shards, -1, depth, width).transpose(1, 0, 2, 3).reshape(-1, width)
        if mlp:
            blocks = jnp.where(first, blocks, full.reshape(-1, width))
        return jnp.concatenate([blocks, gains])

    attn0, attn1 = by_layer(attn_own)
    mlp0, mlp1 = by_layer(mlp_own)
    came_images = swap_section(ends_in[0])
    images = [ends_in[0], came_images]
    attn0 = spread(attn0) if packed else [whole(attn0, False)]
    attn0 = attn0 + [swap_section(p) for p in attn0]

    *tied, attn1, mlp0 = tie(*attn0, attn1, mlp0)
    attn0 = tied
    if packed:
        both = spread(jnp.concatenate([mlp0, attn1]))
    else:
        both = [jnp.concatenate([whole(mlp0, True), whole(attn1, False)])]
    qkv0, probs0, mixed0, mid0, x0, weight0 = attn_fwd(ids, images, attn0, dims, True)

    mid0, mlp1, *both = tie(mid0, mlp1, *both)
    both = both + [swap_section(p) for p in both]
    mlp1 = spread(mlp1) if packed else [whole(mlp1, True)]
    x1, act0, slope0, up0, down0 = mlp_fwd(ids, mid0, both, dims, False)

    x1, *mlp1 = tie(x1, *mlp1)
    mlp1 = mlp1 + [swap_section(p) for p in mlp1]
    out, cot0, keep_m1, send_m1, keep_a1, send_a1 = middle(ids, images, x1, both, mlp1, dims)

    def scatter(half, came, mlp):
        if packed:
            parts = [total(half[k], [came[k]]) for k in range(count)]
            return [parts[0]] + exchange(parts[1:], "fsdp")
        chip = total(half, [came])
        blocks = chip.reshape(-1, shards, depth, width).transpose(1, 0, 2, 3).reshape(shards, -1, width)
        if mlp:
            blocks = jnp.where(first, blocks, chip.reshape(shards, -1, width))
        return [lax.psum_scatter(blocks, "fsdp", scatter_dimension=0)]

    def added(parts):
        return total(parts[0], parts[1:])

    line = replicas == 4
    at_z = lax.axis_index("replica")

    def inwards(part):
        return [part, lax.ppermute(part, "replica", [(0, 1), (3, 2)])] if line else [lax.psum(part, "replica")]

    def across(part):
        return [part, lax.ppermute(part, "replica", [(1, 2), (2, 1)])] if line else [part]

    def outwards(part):
        return [part, lax.ppermute(part, "replica", [(1, 0), (2, 3)])] if line else [part]

    def settled(parts):
        return jnp.where((at_z == 0) | (at_z == 3), parts[1], parts[0]) if line else parts[0]

    def doubled(part, k):
        return [part, lax.ppermute(part, "replica", [(i, i ^ k) for i in range(replicas)])]

    def tied_lists(lists, *values):
        flat = tie(*values, *[member for group in lists for member in group])
        values, flat = flat[:len(values)], flat[len(values):]
        groups = []
        for group in lists:
            groups.append(list(flat[:len(group)]))
            flat = flat[len(group):]
        return groups, values

    came_m1 = swap_section(send_m1)
    came_out = swap_section(out)
    came_a1 = swap_section(send_a1)
    gmid0, keep_m0, send_m0 = mlp_bwd(ids, cot0, mid0, act0, slope0, up0, down0, dims, count, False)

    gmid0, came_a1, keep_a1, came_m1, keep_m1, came_out = tie(gmid0, came_a1, keep_a1, came_m1, keep_m1, came_out)
    if packed:
        l1 = scatter(jnp.concatenate([keep_m1, keep_a1], 1), jnp.concatenate([came_m1, came_a1], 1), True)
    else:
        l1 = [jnp.concatenate([scatter(keep_m1, came_m1, True)[0], scatter(keep_a1, came_a1, False)[0]])]
    came_m0 = swap_section(send_m0)
    early = (share // 2 + 1) // PER_STEP * PER_STEP
    saved = [gmid0, x0, qkv0, probs0, mixed0]
    gx_early, begun = attn_bwd(ids, saved, weight0, dims, count, True, (0, early), final=False)

    (l1,), (begun, gx_early, came_m0, keep_m0) = tied_lists([l1], begun, gx_early, came_m0, keep_m0)
    m0 = scatter(keep_m0, came_m0, True)
    l1 = inwards(added(l1))
    came_gx_early = swap_section(gx_early)
    gx_late, keep_a0, send_a0 = attn_bwd(ids, saved, weight0, dims, count, True, (early, share), begun)

    (l1, m0), (send_a0, keep_a0, gx_late, came_gx_early) = tied_lists([l1, m0], send_a0, keep_a0, gx_late, came_gx_early)
    came_a0 = swap_section(send_a0)
    l1 = across(added(l1))
    m0 = inwards(added(m0))
    came_gx_late = swap_section(gx_late)
    a0 = scatter(keep_a0, came_a0, False)
    m0 = across(added(m0))
    l1 = outwards(added(l1))
    (a0, m0), _ = tied_lists([a0, m0])
    a0 = doubled(added(a0), 1) if line else [lax.psum(added(a0), "replica")]
    m0 = outwards(added(m0))
    a0 = doubled(added(a0), 3) if line else a0
    (a0, m0, l1), _ = tied_lists([a0, m0, l1])
    l1 = settled(l1)
    m0 = settled(m0)
    m1, a1 = l1[:ff // width * depth], l1[ff // width * depth:]
    gx = jnp.concatenate([gx_early, gx_late])
    came_gx = jnp.concatenate([came_gx_early, came_gx_late])

    def own_layer(sum0, sum1):
        mine = jnp.where(first, sum0, sum1)
        other = swap_section(jnp.where(first, sum1, sum0))
        return jnp.concatenate([jnp.where(first, mine, other), jnp.where(first, other, mine)]).astype(F32)

    mlp_grad = own_layer(m0, m1)
    attn_grad = own_layer(added(a0), a1)

    def rows_of(blocks):
        return blocks.reshape(-1, depth, width).transpose(1, 0, 2).reshape(depth, -1)

    grad_qkv, grad_out = rows_of(attn_grad[:3 * depth])[None], attn_grad[3 * depth:][None]
    grad_up, grad_down = rows_of(mlp_grad[:ratio * depth])[None], mlp_grad[ratio * depth:][None]
    grad_gain_attn = jnp.sum(grad_qkv * w_qkv.astype(F32), axis=-1) / gain_attn.astype(F32)
    grad_gain_mlp = jnp.sum(grad_up * w_up.astype(F32), axis=-1) / gain_mlp.astype(F32)

    own = jnp.where(first, gx, out)
    came = jnp.where(first, came_gx, came_out)
    ends_out = jnp.where(first, jnp.concatenate([own, came]), jnp.concatenate([came, own]))
    return (ends_out[None], grad_gain_attn, grad_qkv, grad_out, grad_gain_mlp, grad_up, grad_down)


def solution(mesh):
    in_specs = (
        P("section", ("fsdp", "replica"), None, None),
        P(None, ("fsdp", "replica")),
        P("section", "fsdp"),
        P("section", "fsdp", None),
        P("section", "fsdp", None),
        P("section", "fsdp"),
        P("section", "fsdp", None),
        P("section", "fsdp", None),
    )
    out_specs = (
        P("section", ("fsdp", "replica"), None, None),
        P("section", "fsdp"),
        P("section", "fsdp", None),
        P("section", "fsdp", None),
        P("section", "fsdp"),
        P("section", "fsdp", None),
        P("section", "fsdp", None),
    )
    return jax.shard_map(local, mesh=mesh, in_specs=in_specs, out_specs=out_specs, check_vma=False)
```
